32 devices in a mesh: fsdp: 8 (over y, x, core), tensor: 4 (over z).
Axes of the slice: x: 2, y: 2, z: 4, core: 2. Of those that a mesh axis runs over, the one named last changes fastest.
Arguments:
- states: bfloat16 [4608, 2048], P('fsdp'), may hold values from -6 to 6
- segment_ids: int32 [4608], P('fsdp'), may hold values from 0 to 143, as said below
- ln1_gain: bfloat16 [2, 2048], P(None, 'fsdp'), may hold values from 0.5 to 1.5
- ln1_bias: bfloat16 [2, 2048], P(None, 'fsdp'), may hold values from -4 to 4
- qkv_weight: bfloat16 [2, 2048, 3, 2048], P(None, 'fsdp', None, 'tensor'), may hold values from -0.125 to 0.125
- qkv_bias: bfloat16 [2, 3, 32, 64], P(None, None, 'tensor', 'fsdp'), may hold values from -4 to 4
- out_weight: bfloat16 [2, 2048, 2048], P(None, 'tensor', 'fsdp'), may hold values from -0.375 to 0.375
- ln2_gain: bfloat16 [2, 2048], P(None, 'fsdp'), may hold values from 0.5 to 1.5
- ln2_bias: bfloat16 [2, 2048], P(None, 'fsdp'), may hold values from -4 to 4
- gate_up_weight: bfloat16 [2, 2048, 2, 5632], P(None, 'fsdp', None, 'tensor'), may hold values from -0.125 to 0.125
- down_weight: bfloat16 [2, 5632, 2048], P(None, 'tensor', 'fsdp'), may hold values from -0.109375 to 0.109375
- cotangent: bfloat16 [4608, 2048], P('fsdp'), may hold values from -6 to 6
Outputs:
- out_states: bfloat16 [4608, 2048], P('fsdp')
- grad_states: float32 [4608, 2048], P('fsdp')
- grad_ln1_gain: float32 [2, 2048], P(None, 'fsdp')
- grad_ln1_bias: float32 [2, 2048], P(None, 'fsdp')
- grad_qkv_weight: float32 [2, 2048, 3, 2048], P(None, 'fsdp', None, 'tensor')
- grad_qkv_bias: float32 [2, 3, 32, 64], P(None, None, 'tensor', 'fsdp')
- grad_out_weight: float32 [2, 2048, 2048], P(None, 'tensor', 'fsdp')
- grad_ln2_gain: float32 [2, 2048], P(None, 'fsdp')
- grad_ln2_bias: float32 [2, 2048], P(None, 'fsdp')
- grad_gate_up: float32 [2, 2048, 2, 5632], P(None, 'fsdp', None, 'tensor')
- grad_down: float32 [2, 5632, 2048], P(None, 'tensor', 'fsdp')
The draws below stay inside these ranges and needn't reach their ends.
Inputs may be any that keep to these rules, and one draw needn't show every extreme that they name: `segment_ids`: each device's block of 576 tokens holds whole sequences numbered 0, 1, 2, ... in order from the block's start; every sequence starts at a place within its block that is a multiple of 4; some block holds one sequence of all 576 tokens.
All inputs are finite; a program needn't handle non-finite values.
Results may differ from the reference program's by a relative error of at most 0.03.
Values may be sent and summed in bfloat16 or wider, within the bound.
A program may use at most 256 MiB of HBM per device.

```python
import math
import jax
import jax.numpy as jnp
from jax import lax

D = 2048
HEADS = 32
HEAD_DIM = 64
ROT_DIM = 16
FF = 5632
LAYERS = 2
TOK_DEV = 576
TOKENS = 4608
N_FSDP = 8


def draw_segment_ids(key, part):
    key = jax.random.fold_in(key, 7)
    rate_key, cut_key, whole_key = jax.random.split(key, 3)
    blocks = TOKENS // TOK_DEV
    spacing = jax.random.randint(rate_key, (blocks, 1), 1, TOK_DEV // 4 + 1)
    draws_cut = jax.random.randint(cut_key, (blocks, TOK_DEV), 0, 1048576)
    single = jax.random.randint(whole_key, (), 0, blocks)
    dense_block = (single + 1) % blocks
    block_rows = jnp.arange(blocks, dtype=jnp.int32)[:, None]
    places = jnp.arange(TOK_DEV, dtype=jnp.int32)[None, :]
    allowed_cut = (places % 4 == 0) & (places > 0)
    chosen = (draws_cut % spacing == 0) | (block_rows == dense_block)
    cuts = allowed_cut & chosen & (block_rows != single)
    return jnp.cumsum(cuts.astype(jnp.int32), axis=1).reshape(-1).astype(jnp.int32)


def shard_levels(key, extent, shards, least, high):
    def one(axis_at, shards_of):
        steps = jax.random.uniform(jax.random.fold_in(jax.random.fold_in(key, 6), axis_at), (shards_of,), jnp.float32, least / len(shards), high / len(shards))
        return jnp.repeat(jnp.exp(steps), extent[axis_at] // shards_of).reshape((-1,) + (1,) * (len(extent) - axis_at - 1))

    gain = one(*shards[0])
    for cut in shards[1:]:
        gain = gain * one(*cut)
    return gain


def noise(own_key, dims, deviation, most, cuts=(), held_as=jnp.bfloat16):
    entries = deviation * jax.random.normal(own_key, dims, jnp.float32)
    if cuts:
        entries = entries * shard_levels(own_key, dims, cuts, -0.22, 0.18)
    return jnp.clip(entries, -most, most).astype(held_as)


def setup_inputs(seed: int = 0) -> dict:
    seeds = jax.random.split(jax.random.key(seed), 13)
    return {
        "states": noise(seeds[0], (TOKENS, D), 1.0, 6.0, ((0, 8),)),
        "segment_ids": draw_segment_ids(jax.random.fold_in(seeds[12], 71), 0),
        "ln1_gain": jnp.clip(1.0 + 0.1 * jax.random.normal(seeds[2], (LAYERS, D), jnp.float32), 0.5, 1.5).astype(jnp.bfloat16),
        "ln1_bias": noise(seeds[3], (LAYERS, D), 0.3, 4.0, ((1, 8),)),
        "qkv_weight": noise(seeds[4], (LAYERS, D, 3, D), D ** -0.5, 0.125, ((1, 8), (3, 4))),
        "qkv_bias": noise(seeds[5], (LAYERS, 3, HEADS, HEAD_DIM), 0.3, 4.0, ((2, 4), (3, 8))),
        "out_weight": noise(seeds[6], (LAYERS, D, D), (D // 8) ** -0.5, 0.375, ((1, 4), (2, 8))),
        "ln2_gain": jnp.clip(1.0 + 0.1 * jax.random.normal(seeds[7], (LAYERS, D), jnp.float32), 0.5, 1.5).astype(jnp.bfloat16),
        "ln2_bias": noise(seeds[8], (LAYERS, D), 0.3, 4.0, ((1, 8),)),
        "gate_up_weight": noise(seeds[9], (LAYERS, D, 2, FF), D ** -0.5, 0.125, ((1, 8), (3, 4))),
        "down_weight": noise(seeds[10], (LAYERS, FF, D), (FF // 2) ** -0.5, 0.109375, ((1, 4), (2, 8))),
        "cotangent": noise(seeds[11], (TOKENS, D), 1.0, 6.0, ((0, 8),)),
    }


@jax.custom_vjp
def low(v):
    return lax.optimization_barrier(v.astype(jnp.bfloat16)).astype(jnp.float32)

@jax.custom_vjp
def low_back(v):
    return v

def low_keep(v):
    return (low(v), None)

def low_pass(kept, grad):
    return (grad,)

def back_keep(v):
    return (v, None)

def back_low(kept, grad):
    return (low(grad),)
low.defvjp(low_keep, low_pass)
low_back.defvjp(back_keep, back_low)
norm_epsilon = 1e-05
rotary_base = 10000.0

def layer_norm(values, norm_scale, bias):
    average = lax.optimization_barrier(jnp.mean(values, axis=-1, keepdims=True))
    centred = values - average
    spread = lax.optimization_barrier(jnp.mean(centred * centred, axis=-1, keepdims=True))
    return centred * lax.rsqrt(spread + norm_epsilon) * norm_scale + bias

def rotate(values, cosine, sine):
    half = ROT_DIM // 2
    first = values[..., :half]
    second = values[..., half:ROT_DIM]
    return jnp.concatenate([first * cosine - second * sine, second * cosine + first * sine, values[..., ROT_DIM:]], axis=-1)

def attend_pack(packed):
    query_rows, key_rows, value_rows, seg_rows = packed
    scores = jnp.einsum('qhd,khd->hqk', query_rows, key_rows, precision=lax.Precision.HIGHEST) * (1.0 / math.sqrt(HEAD_DIM))
    scores = low_back(scores)
    places = jnp.arange(TOK_DEV, dtype=jnp.int32)
    allowed = (seg_rows[:, None] == seg_rows[None, :]) & (places[None, :] <= places[:, None])
    scores = jnp.where(allowed[None], scores, -1e+30)
    weights = low(jax.nn.softmax(scores, axis=-1))
    return jnp.einsum('hqk,khd->qhd', weights, value_rows, precision=lax.Precision.HIGHEST)

def one_layer(residual_state, params, cosine, sine, segment_ids):
    first_norm_scale, first_norm_bias, qkv_w, qkv_b, out_w, second_norm_scale, second_norm_bias, gate_up_w, down_w = params
    normalized_rows = low(layer_norm(residual_state, first_norm_scale, first_norm_bias))
    mixed = jnp.einsum('td,dce->tce', normalized_rows, qkv_w, precision=lax.Precision.HIGHEST) + qkv_b.reshape(3, D)[None]
    mixed = low_back(mixed)
    heads = mixed.reshape(TOKENS, 3, HEADS, HEAD_DIM)
    query_rows = low(rotate(heads[:, 0], cosine, sine))
    key_rows = low(rotate(heads[:, 1], cosine, sine))
    value_rows = low(heads[:, 2])
    shape_blocks = (N_FSDP, TOK_DEV, HEADS, HEAD_DIM)
    attended = lax.map(jax.checkpoint(attend_pack), (query_rows.reshape(shape_blocks), key_rows.reshape(shape_blocks), value_rows.reshape(shape_blocks), segment_ids.reshape(N_FSDP, TOK_DEV)))
    attended = low(low_back(attended.reshape(TOKENS, D)))
    branch = low_back(jnp.dot(attended, out_w, precision=lax.Precision.HIGHEST))
    residual_between = residual_state + branch
    second_normalized_rows = low(layer_norm(residual_between, second_norm_scale, second_norm_bias))
    gate_up = low_back(jnp.einsum('td,dcf->tcf', second_normalized_rows, gate_up_w, precision=lax.Precision.HIGHEST))
    hidden = low(jax.nn.silu(gate_up[:, 0]) * gate_up[:, 1])
    branch_two = low_back(jnp.dot(hidden, down_w, precision=lax.Precision.HIGHEST))
    return residual_between + branch_two

def rotary_tables(segment_ids):
    seg_blocks = segment_ids.reshape(N_FSDP, TOK_DEV)
    places = jnp.arange(TOK_DEV, dtype=jnp.int32)[None, :]
    previous = jnp.concatenate([seg_blocks[:, :1] - 1, seg_blocks[:, :-1]], axis=1)
    starts = lax.cummax(jnp.where(seg_blocks != previous, places, jnp.zeros_like(places)), axis=1)
    position = (places - starts).reshape(-1)
    half = ROT_DIM // 2
    inverse = rotary_base ** (-(jnp.arange(half, dtype=jnp.float32) * 2.0 / ROT_DIM))
    angle = position.astype(jnp.float32)[:, None] * inverse[None, :]
    return (jnp.cos(angle)[:, None, :], jnp.sin(angle)[:, None, :])

def reference(states, segment_ids, ln1_gain, ln1_bias, qkv_weight, qkv_bias, out_weight, ln2_gain, ln2_bias, gate_up_weight, down_weight, cotangent):
    cosine, sine = rotary_tables(segment_ids)
    params = [p.astype(jnp.float32) for p in (ln1_gain, ln1_bias, qkv_weight, qkv_bias, out_weight, ln2_gain, ln2_bias, gate_up_weight, down_weight)]

    def forward(residual_state, *weights):
        for layer in range(LAYERS):
            residual_state = one_layer(residual_state, tuple((w[layer] for w in weights)), cosine, sine, segment_ids)
        return residual_state
    final_out, pullback = jax.vjp(forward, states.astype(jnp.float32), *params)
    all_grads = pullback(cotangent.astype(jnp.float32))
    return (final_out.astype(jnp.bfloat16), all_grads[0], all_grads[1], all_grads[2], all_grads[3], all_grads[4], all_grads[5], all_grads[6], all_grads[7], all_grads[8], all_grads[9])
```

```python
import functools
import math

import jax
import jax.numpy as jnp
from jax import lax
from jax.experimental import pallas as pl
from jax.experimental.pallas import tpu as pltpu
from jax.sharding import PartitionSpec as P

MESH = pl.DeviceIdType.MESH
HEAD_DIM = 64
ROT_DIM = 16
LAYERS = 2
PAIR = 2 * HEAD_DIM
ANY = pl.BlockSpec(memory_space=pl.ANY)
VMEM = pl.BlockSpec(memory_space=pltpu.VMEM)
BF16 = jnp.bfloat16
F32 = jnp.float32

norm_epsilon = 1e-05
rotary_base = 10000.0


def dot(a, b):
    return lax.dot_general(a, b, (((1,), (0,)), ((), ())), preferred_element_type=F32)


def dot_nt(a, b):
    return lax.dot_general(a, b, (((1,), (1,)), ((), ())), preferred_element_type=F32)


def dot_tn(a, b):
    return lax.dot_general(a, b, (((0,), (0,)), ((), ())), preferred_element_type=F32)


def tiles(extent, most=512):
    return [(at, min(most, extent - at)) for at in range(0, extent, most)]


def standardize(values):
    average = jnp.mean(values, axis=-1, keepdims=True)
    centred = values - average
    spread = jnp.mean(centred * centred, axis=-1, keepdims=True)
    rstd = lax.rsqrt(spread + norm_epsilon)
    return centred * rstd, rstd


def turn(values, rope, sign):
    half = ROT_DIM // 2
    factor, below, above = rope
    return values * factor + sign * (
        pltpu.roll(values, PAIR - half, 1) * below + pltpu.roll(values, half, 1) * above
    )


def when(condition):
    return pl.when(condition)


def to(source, target, send, arrive, place):
    return pltpu.make_async_remote_copy(
        src_ref=source, dst_ref=target, send_sem=send, recv_sem=arrive, device_id=place, device_id_type=MESH
    )


def spread(build, source, target, count=4):
    rows = source.shape[-2] // count
    for r in range(count):
        piece = (slice(None),) * (len(source.shape) - 2) + (pl.ds(r * rows, rows), slice(None))
        build(source.at[piece], target.at[piece]).start()


def start(source, target, build):
    spread(build, source, target)


def whole(source, target, build):
    return build(source, target)


class Line:
    def __init__(self, count):
        place = lax.axis_index("tensor")
        half = count // 2
        left = place < half
        self.inner = jnp.where(left, place + 1, place - 1)
        self.outer = jnp.where(left, place - 1, place + 1)
        self.has_outer = (place != 0) & (place != count - 1)
        self.no_outer = jnp.logical_not(self.has_outer)
        self.distance = jnp.where(left, half - 1 - place, place - half)
        self.centre = self.distance == 0
        self.off_centre = jnp.logical_not(self.centre)


class Group:
    def __init__(self, count):
        self.count = count
        self.chips = count // 2
        self.me = lax.axis_index("fsdp")
        self.chip = self.me // 2
        self.core = self.me % 2
        self.peer = self.me + 1 - 2 * self.core
        self.square = self.chips == 4
        self.everyone = [(self.me + i) % count for i in range(1, count)]
        if self.square:
            self.x = self.at(self.chip + 1 - 2 * (self.chip % 2))
            self.y = self.at(self.chip + 2 - 4 * (self.chip // 2))
            self.far = self.at(3 - self.chip)
            self.others = [self.x, self.y]
        else:
            self.others = [self.at((self.chip + i) % self.chips) for i in range(1, self.chips)]

    def at(self, chip):
        return chip * 2 + self.core


def enter(line, partners):
    barrier = pltpu.get_barrier_semaphore()
    for partner in partners:
        pl.semaphore_signal(barrier, inc=1, device_id={"fsdp": partner}, device_id_type=MESH)
    pl.semaphore_signal(barrier, inc=1, device_id={"tensor": line.inner}, device_id_type=MESH)

    @when(line.has_outer)
    def _():
        pl.semaphore_signal(barrier, inc=1, device_id={"tensor": line.outer}, device_id_type=MESH)
        pl.semaphore_wait(barrier, len(partners) + 2)

    @when(line.no_outer)
    def _():
        pl.semaphore_wait(barrier, len(partners) + 1)


class Flow:
    def __init__(self, line, steps, span, rows, refs):
        self.line, self.steps, self.span, self.rows = line, steps, span, rows
        self.from_outer, self.from_inner, self.running = refs[:3]
        self.send_in, self.got_out, self.send_out, self.got_in, self.credit = refs[3:]
        self.lag = jnp.minimum(3 * line.distance + 2, steps - 1)

    def slot(self, i):
        big = self.rows * self.span
        return pl.ds(pl.multiple_of(i * big, big), big)

    def pieces(self, i):
        for r in range(self.span):
            q = i * self.span + r
            yield q, pl.ds(pl.multiple_of(q * self.rows, self.rows), self.rows)

    def inward(self, q, here, target, arrive):
        return to(
            self.running.at[here], target.at[here], self.send_in.at[q], arrive.at[q], {"tensor": self.line.inner}
        )

    def outward(self, q, here):
        return to(
            self.from_inner.at[here], self.from_inner.at[here], self.send_out.at[q], self.got_in.at[q],
            {"tensor": self.line.outer},
        )

    def clear(self, i):
        for q, here in self.pieces(i):
            self.inward(q, here, self.from_inner, self.got_in).wait_send()

    def push(self, i, again):
        line = self.line

        @when(line.centre & again)
        def _():
            pl.semaphore_wait(self.credit, 1)

        for q, here in self.pieces(i):

            @when(line.has_outer)
            def _(q=q, here=here):
                self.inward(q, here, self.from_outer, self.got_out).wait_recv()
                total = self.running[here, :].astype(F32) + self.from_outer[here, :].astype(F32)
                self.running[here, :] = total.astype(BF16)

            @when(line.centre)
            def _(q=q, here=here):
                self.inward(q, here, self.from_inner, self.got_in).start()

            @when(line.off_centre)
            def _(q=q, here=here):
                self.inward(q, here, self.from_outer, self.got_out).start()

    def pull(self, i):
        line = self.line
        for q, here in self.pieces(i):
            self.inward(q, here, self.from_inner, self.got_in).wait_recv()

            @when(line.centre)
            def _(q=q, here=here):
                total = self.running[here, :].astype(F32) + self.from_inner[here, :].astype(F32)
                self.from_inner[here, :] = total.astype(BF16)

            @when(line.has_outer)
            def _(q=q, here=here):
                self.outward(q, here).start()

    def release(self, i, more):
        line = self.line

        @when(line.has_outer)
        def _():
            for q, here in self.pieces(i):
                self.outward(q, here).wait_send()

        @when(line.centre & more)
        def _():
            pl.semaphore_signal(self.credit, inc=1, device_id={"tensor": line.inner}, device_id_type=MESH)


def flow_scratch(steps, span, tokens, width):
    whole = pltpu.VMEM((tokens, width), BF16)
    sems = pltpu.SemaphoreType.DMA((steps * span,))
    return [whole, whole, whole, sems, sems, sems, sems, pltpu.SemaphoreType.REGULAR]


def gather_kinds(count):
    return 9 if count == 8 else count


class Gather:
    def __init__(self, group, own, whole, send, arrive, load):
        self.group, self.own, self.whole, self.send, self.arrive, self.load_sems = group, own, whole, send, arrive, load
        self.half = own.shape[1] // 2
        self.links = len(group.others)

    def half_at(self, shard, h):
        return self.whole.at[shard, :, pl.ds(h * self.half, self.half), :]

    def way(self, kind):
        g, links = self.group, self.links
        if kind < links:
            return self.own, self.whole.at[g.me], g.others[kind]
        if kind == links:
            return self.own, self.whole.at[g.me], g.peer
        if kind <= 2 * links:
            shard = self.whole.at[g.others[kind - links - 1]]
            return shard, shard, g.peer
        if kind == 2 * links + 1:
            return self.half_at(g.x, 0), self.half_at(g.x, 0), g.y
        if kind == 2 * links + 2:
            return self.half_at(g.y, 1), self.half_at(g.y, 1), g.x
        return self.whole.at[g.far], self.whole.at[g.far], g.peer

    def build(self, kind, source, target):
        return to(source, target, self.send.at[kind], self.arrive.at[kind], {"fsdp": self.way(kind)[2]})

    def copy(self, kind):
        return self.build(kind, *self.way(kind)[:2])

    def start(self, kind):
        spread(functools.partial(self.build, kind), *self.way(kind)[:2])

    def local(self):
        return pltpu.make_async_copy(self.own, self.whole.at[self.group.me], self.send.at[gather_kinds(self.group.count) - 1])

    def begin(self):
        for kind in range(self.links + 1):
            self.start(kind)
        self.local().start()

    def relay(self):
        for kind in range(self.links):
            self.copy(kind).wait_recv()
        if self.group.square:
            self.start(2 * self.links + 1)
            self.start(2 * self.links + 2)
        for kind in range(self.links):
            self.start(self.links + 1 + kind)

    def relay_far(self):
        if self.group.square:
            self.copy(2 * self.links + 1).wait_recv()
            self.copy(2 * self.links + 2).wait_recv()
            self.start(2 * self.links + 3)

    def settle(self):
        self.local().wait()
        for kind in range(self.links, 2 * self.links + 1):
            self.copy(kind).wait_recv()
        if self.group.square:
            self.copy(2 * self.links + 3).wait_recv()

    def loads(self, target):
        depth = self.own.shape[1]
        for k in range(self.group.count):
            yield pltpu.make_async_copy(
                self.whole.at[k], target.at[:, pl.ds(k * depth, depth), :], self.load_sems.at[k]
            )

    def finish(self):
        for kind in range(2 * self.links + 1 + (3 if self.group.square else 0)):
            self.copy(kind).wait_send()


def train_kernel(
    count, shards, steps, span, per_step,
    states, cotangent, own_norms, own_bias, rope, mask, own_q, own_o, own_g, own_d,
    out_states, grad_states, sums_attn, sums_ffn, norm_parts, bias_parts,
    whole_q, whole_o, whole_g, whole_d, s_x, s_n, s_y, s_qkv, s_att, s_gu, s_hid,
    mate_attn, mate_ffn, via_attn, via_ffn,
    res, w_attn, w_ffn, gu, hid, qkv, att, d_key, d_value, x_in, low,
    norms, biases, bias_in, norm_acc, bias_acc, columns, turned, staged,
    x_save, x_sem, low_sem, out_sem, keep_sem, act_sem, misc, load_sem, g_send, g_arrive,
    column_sem, stage_sem, relay_sem, mate_send, mate_got, own_send, own_got, small_send, small_got,
    *flow_refs,
):
    tokens, width = res.shape
    big = tokens // steps
    local, ff = w_attn.shape[2], w_ffn.shape[2]
    depth = width // shards
    line = Line(count)
    group = Group(shards)
    chips = group.chips
    flow = Flow(line, steps, span, big // span, flow_refs)
    scale = 1.0 / math.sqrt(HEAD_DIM)
    half = 2 * LAYERS
    stages = 2 * half
    total = stages * steps
    top = LAYERS - 1
    units = 2 * chips

    def block(c):
        return pl.ds(pl.multiple_of(c * big, big), big)

    kinds = [(own_q, whole_q), (own_o, whole_o), (own_g, whole_g), (own_d, whole_d)]
    targets = [w_attn.at[0:3], w_attn.at[3:4], w_ffn.at[0:2], w_ffn.at[2:3]]

    def gather(layer, kind):
        n = 4 * layer + kind
        own, whole = kinds[kind]
        return Gather(group, own.at[layer], whole.at[layer], g_send.at[n], g_arrive.at[n], load_sem.at[kind])

    def load(layer, kind, wait):
        own, whole = kinds[kind]
        way = Gather(group, own.at[0], whole.at[layer], g_send.at[0], g_arrive.at[0], load_sem.at[kind])
        for copy in way.loads(targets[kind]):
            if wait:
                copy.wait()
            else:
                copy.start()

    events = {}

    def event(t, where, *actions):
        events.setdefault((t, where, None), []).extend(actions)

    def event_by_role(centre, others, *actions):
        events.setdefault(centre + (True,), []).extend(actions)
        events.setdefault(others + (False,), []).extend(actions)

    def loading(layer, kind, wait):
        return functools.partial(load, layer, kind, wait)

    def at(stage, i):
        return stage * steps + min(i, steps - 1)

    q, o, g, d = 0, 1, 2, 3
    event(0, 1, gather(0, o).relay_far, gather(0, o).settle, loading(0, o, False), loading(0, o, True))
    event_by_role((at(0, 3), 0), (at(0, 4), 0), gather(0, g).relay)
    event_by_role((at(0, 5), 0), (at(0, 5), 2), gather(0, g).relay_far, gather(0, d).begin)
    event(at(1, 0), 0, gather(0, g).settle, loading(0, g, False), loading(0, g, True))
    event(at(1, 0), 1, gather(0, d).relay)
    for layer in range(1, LAYERS):
        s = 2 * layer - 1
        event(at(s, 0), 1, gather(layer, q).begin)
        if layer == 1:
            event(at(s, 0), 1, gather(0, d).relay_far, gather(0, d).settle, loading(0, d, False), loading(0, d, True))
        event(at(s, 2), 0, gather(layer, q).relay, gather(layer, o).begin)
        event_by_role((at(s, 3), 0), (at(s, 3), 2), gather(layer, q).relay_far, gather(layer, o).relay, gather(layer, g).begin)
        event(at(s, 4), 2, gather(layer, o).relay_far)
        event(at(s, 5), 2, gather(layer, q).settle, loading(layer, q, False))
        event(at(s, 5), 2, gather(layer, o).settle, loading(layer, o, False))
        s += 1
        event(at(s, 0), 0, loading(layer, q, True), loading(layer, o, True))
        event_by_role((at(s, 0), 0), (at(s, 0), 2), gather(layer, g).relay)
        event_by_role((at(s, 2), 0), (at(s, 2), 2), gather(layer, g).relay_far, gather(layer, d).begin)
        event(at(s, 3), 2, gather(layer, g).settle, loading(layer, g, False))
        event_by_role((at(s, 4), 0), (at(s, 4), 2), gather(layer, d).relay)
        event(at(s, 5), 2, gather(layer, d).relay_far)
        s += 1
        event(at(s, 0), 0, loading(layer, g, True), gather(layer, d).settle, loading(layer, d, False))
        event(at(s, 0), 1, loading(layer, d, True))

    def run_events(t, where):
        ordered = sorted(events.items(), key=lambda item: item[0][:2])
        ordered = [(at, role, actions) for (at, place, role), actions in ordered if place == where]
        for stage in sorted({at // steps for at, _, _ in ordered}):

            @when(t // steps == stage)
            def _(stage=stage):
                for at, role, actions in ordered:
                    if at // steps != stage:
                        continue
                    condition = t == at
                    if role is not None:
                        condition = condition & (line.centre if role else line.off_centre)

                    @when(condition)
                    def _(actions=actions):
                        for action in actions:
                            action()

    enter(line, group.everyone)
    mine = pl.ds(pl.multiple_of(group.me * depth, depth), depth)
    small = []
    for n, other in enumerate(group.everyone):
        sems = (small_send.at[0, n], small_got.at[0, n])
        small.append(to(own_norms, norms.at[:, mine], *sems, {"fsdp": other}))
        sems = (small_send.at[1, n], small_got.at[1, n])
        small.append(to(own_bias, bias_in.at[group.me], *sems, {"fsdp": other}))
    gather(0, q).begin()
    for copy in small:
        copy.start()
    starts = [
        pltpu.make_async_copy(own_norms, norms.at[:, mine], misc.at[0]),
        pltpu.make_async_copy(own_bias, bias_in.at[group.me], misc.at[1]),
        pltpu.make_async_copy(states, flow.running, misc.at[2]),
        pltpu.make_async_copy(cotangent, s_y.at[0], misc.at[3]),
    ]
    for copy in starts:
        copy.start()
    qkv[...] = jnp.zeros_like(qkv)
    norm_acc[...] = jnp.zeros_like(norm_acc)
    bias_acc[...] = jnp.zeros_like(bias_acc)
    for copy in starts:
        copy.wait()
    for c in range(steps):
        res[c * big : (c + 1) * big, :] = flow.running[c * big : (c + 1) * big, :].astype(F32)
    for copy in small:
        copy.wait_recv()
    each = HEAD_DIM // shards
    source = lax.broadcasted_iota(jnp.int32, (PAIR, local), 0)
    column = lax.broadcasted_iota(jnp.int32, (PAIR, local), 1)
    at_head = lax.div(source, each) == lax.div(column, HEAD_DIM)
    whole_bias = jnp.zeros((8, local), F32)
    for k in range(shards):
        match = at_head & (lax.rem(column, HEAD_DIM) == k * each + lax.rem(source, each))
        whole_bias += dot(bias_in[k].astype(BF16), jnp.where(match, 1.0, 0.0).astype(BF16))
    biases[...] = whole_bias
    gather(0, q).relay()
    gather(0, o).begin()
    gather(0, q).relay_far()
    gather(0, o).relay()
    gather(0, g).begin()
    gather(0, q).settle()
    load(0, q, False)
    load(0, q, True)

    lanes = lax.broadcasted_iota(jnp.int32, (big, PAIR), 1)
    first_head = lanes < HEAD_DIM

    def save_x(stage, c):
        return pltpu.make_async_copy(res.at[block(c)], s_x.at[stage, block(c)], x_save.at[c])

    def keeps(layer, kind, c):
        here = block(c)
        if kind == 0:
            pairs = [(gu.at[:, here], s_gu.at[layer, :, here]), (hid.at[here], s_hid.at[layer, here])]
        else:
            pairs = [(qkv.at[:, here], s_qkv.at[layer, :, here]), (att.at[here], s_att.at[layer, here])]
        return [pltpu.make_async_copy(a, b, keep_sem.at[kind, n, c]) for n, (a, b) in enumerate(pairs)]

    def activations(layer, kind):
        if kind == 0:
            pairs = [(s_gu.at[layer], gu), (s_hid.at[layer], hid)]
        else:
            pairs = [(s_qkv.at[layer], qkv), (s_att.at[layer], att)]
        return [pltpu.make_async_copy(a, b, act_sem.at[kind, n]) for n, (a, b) in enumerate(pairs)]

    def project(*pairs):
        def write(i):
            here = flow.slot(i)
            for at, wide in tiles(width, 1024):
                part = sum(dot_nt(right[at : at + wide, :], left()) for left, right in pairs)
                flow.running[here, at : at + wide] = part.T.astype(BF16)

        return write

    def by_extent(c, work):
        early = steps // 2

        @when(c < early)
        def _():
            work(early * big)

        @when(c >= early)
        def _():
            work(tokens)

    def normed_rows(stage, c):
        here = block(c)

        @when(stage > 0)
        def _():
            save_x(stage, c).wait()
            res[here, :] += flow.from_inner[flow.slot(c), :].astype(F32)

        save_x(stage, c).start()
        xhat, _ = standardize(res[here, :])
        low[...] = (xhat * norms[pl.ds(2 * stage, 1), :] + norms[pl.ds(2 * stage + 1, 1), :]).astype(BF16)
        pltpu.make_async_copy(low, s_n.at[stage, here], low_sem.at[0]).start()

    def attention_forward(t, layer, c):
        here = block(c)

        @when(layer > 0)
        def _():
            for copy in keeps(layer - 1, 1, c):
                copy.wait()

        for part in range(3):
            for at, wide in tiles(local):
                mixed = dot(low[...], w_attn[part, :, at : at + wide])
                for pair in range(wide // PAIR):
                    to_lane = at + pair * PAIR
                    span_here = slice(to_lane, to_lane + PAIR)
                    value = mixed[:, pair * PAIR : (pair + 1) * PAIR]
                    value = value + biases[pl.ds(3 * layer + part, 1), :][:, span_here]
                    if part < 2:
                        value = turn(value, [rope[n, here, :] for n in range(3)], 1.0)
                    qkv[part, here, span_here] = value.astype(BF16)
        def attend(keys):
            open_here = mask[c, 0:keys].astype(F32) > 0.0
            for pair in range(local // PAIR):
                lane = slice(pair * PAIR, (pair + 1) * PAIR)
                query, key, value = qkv[0, here, lane], qkv[1, 0:keys, lane], qkv[2, 0:keys, lane]
                outs = []
                for head in range(2):
                    own = first_head if head == 0 else jnp.logical_not(first_head)
                    scores = dot_nt(key, jnp.where(own, query, jnp.zeros_like(query))) * scale
                    scores = jnp.where(open_here, scores, -1e30)
                    exps = jnp.exp(scores - jnp.max(scores, axis=0, keepdims=True))
                    probs = exps * (1.0 / jnp.sum(exps, axis=0, keepdims=True))
                    outs.append(dot_tn(probs.astype(BF16), value))
                att[here, lane] = jnp.where(first_head, outs[0], outs[1]).astype(BF16)

        by_extent(c, attend)

        @when(layer < top)
        def _():
            for copy in keeps(layer, 1, c):
                copy.start()

        run_events(t, 1)
        project((lambda: att[here, :], w_attn.at[3]))(c)

    def ffn_forward(t, layer, c):
        here = block(c)

        @when(layer > 0)
        def _():
            for copy in keeps(layer - 1, 0, c):
                copy.wait()

        for at, wide in tiles(ff):
            gate = dot(low[...], w_ffn[0, :, at : at + wide])
            up = dot(low[...], w_ffn[1, :, at : at + wide])
            gu[0, here, at : at + wide] = gate.astype(BF16)
            gu[1, here, at : at + wide] = up.astype(BF16)
            hid[here, at : at + wide] = (gate * jax.nn.sigmoid(gate) * up).astype(BF16)

        @when(layer < top)
        def _():
            for copy in keeps(layer, 0, c):
                copy.start()

        run_events(t, 1)
        project((lambda: hid[here, :], w_ffn.at[2]))(c)

    def fetch_x(back, c):
        return pltpu.make_async_copy(s_x.at[half - back, block(c)], x_in, x_sem.at[0])

    def fetch_low(c):
        return pltpu.make_async_copy(s_y.at[0, block(c)], low, low_sem.at[1])

    def save_low(back, c):
        return pltpu.make_async_copy(low, s_y.at[back, block(c)], low_sem.at[0])

    def take(back, i, c):
        here = block(c)
        row = 2 * (half - back)
        fetch_x(back, c).wait()

        @when(back == 1)
        def _():
            fetch_low(c).wait()
            res[here, :] = low[...].astype(F32)

        xhat, rstd = standardize(x_in[...])
        e = flow.from_inner[flow.slot(i), :].astype(F32)
        scaled = e * norms[pl.ds(row, 1), :]
        inner = jnp.mean(scaled * xhat, axis=-1, keepdims=True)
        res[here, :] += rstd * (scaled - jnp.mean(scaled, axis=-1, keepdims=True) - xhat * inner)
        norm_acc[pl.ds(row, 1), :] += jnp.sum(e * xhat, axis=0, keepdims=True)
        norm_acc[pl.ds(row + 1, 1), :] += jnp.sum(e, axis=0, keepdims=True)

    def ffn_backward(i, c):
        here = block(c)
        for at, wide in tiles(ff):
            lane = slice(at, at + wide)
            d_hidden = dot(low[...], w_ffn[2, :, lane])
            gate, up = gu[0, here, lane].astype(F32), gu[1, here, lane].astype(F32)
            sigma = jax.nn.sigmoid(gate)
            gu[0, here, lane] = (d_hidden * up * sigma * (1.0 + gate * (1.0 - sigma))).astype(BF16)
            gu[1, here, lane] = (d_hidden * gate * sigma).astype(BF16)
        project((lambda: gu[0, here, :], w_ffn.at[0]), (lambda: gu[1, here, :], w_ffn.at[1]))(i)

    def attention_backward(layer, i, c):
        here = block(c)
        def attend_back(keys):
            open_here = mask[c, 0:keys].astype(F32) > 0.0
            turns = [rope[n, here, :] for n in range(3)]
            for pair in range(local // PAIR):
                lane = slice(pair * PAIR, (pair + 1) * PAIR)
                d_att = dot(low[...], w_attn[3, :, lane]).astype(BF16)
                query, key, value = qkv[0, here, lane], qkv[1, 0:keys, lane], qkv[2, 0:keys, lane]
                d_query = []
                for head in range(2):
                    own = first_head if head == 0 else jnp.logical_not(first_head)
                    own_query = jnp.where(own, query, jnp.zeros_like(query))
                    own_d_att = jnp.where(own, d_att, jnp.zeros_like(d_att))
                    scores = jnp.where(open_here, dot_nt(key, own_query) * scale, -1e30)
                    exps = jnp.exp(scores - jnp.max(scores, axis=0, keepdims=True))
                    probs = exps * (1.0 / jnp.sum(exps, axis=0, keepdims=True))
                    d_probs = dot_nt(value, own_d_att)
                    d_scores = probs * (d_probs - jnp.sum(probs * d_probs, axis=0, keepdims=True))
                    d_scores = d_scores.astype(BF16)
                    d_value[0:keys, lane] += dot(probs.astype(BF16), own_d_att)
                    d_key[0:keys, lane] += dot(d_scores, own_query)
                    d_query.append(dot_tn(d_scores, key))
                parts = [
                    turn(jnp.where(first_head, d_query[0], d_query[1]) * scale, turns, -1.0),
                    turn(d_key[here, lane] * scale, turns, -1.0),
                    d_value[here, lane],
                ]
                for part, values in enumerate(parts):
                    values = values.astype(BF16)
                    qkv[part, here, lane] = values
                    bias_acc[layer, part : part + 1, lane] += jnp.sum(values.astype(F32), axis=0, keepdims=True)

        by_extent(c, attend_back)
        project(
            (lambda: qkv[0, here, :], w_attn.at[0]),
            (lambda: qkv[1, here, :], w_attn.at[1]),
            (lambda: qkv[2, here, :], w_attn.at[2]),
        )(i)

    class Blocks:
        def __init__(self, back, kind):
            self.back_stage, self.kind = back, kind
            layer = top - back // 2
            self.sums = (sums_ffn if kind == 0 else sums_attn).at[layer]
            self.mate = (mate_ffn if kind == 0 else mate_attn).at[layer]
            self.via = (via_ffn if kind == 0 else via_attn).at[layer]
            self.home = 0 if group.square else group.chip
            self.stride = lane_stride(ff if kind == 0 else local)
            self.held = staged.at[:, :, 0 : (4 - (kind == 0)) * self.stride]
            self.x = s_n.at[2 * layer + 1 - kind]
            self.y = s_y.at[back]
            if kind == 0:
                self.right = [(0, gu.at[0]), (0, gu.at[1]), (1, hid)]
            else:
                self.right = [(0, qkv.at[0]), (0, qkv.at[1]), (0, qkv.at[2]), (1, att)]

        def chip(self, u):
            if not group.square:
                return (group.chip + 1 + u) % chips
            x, y, far = group.x // 2, group.y // 2, group.far // 2
            k = u % 4
            return jnp.where(k == 0, far, jnp.where(k == 1, x, jnp.where(k == 2, y, group.chip)))

        def fetch(self, u):
            core = jnp.where(u < chips, 1 - group.core, group.core)
            at = pl.multiple_of((self.chip(u) * 2 + core) * depth, depth)
            return [
                pltpu.make_async_copy(
                    source.at[:, pl.ds(at, depth)], columns.at[u % 2, n], column_sem.at[self.kind, u % 2, n]
                )
                for n, source in enumerate((self.x, self.y))
            ]

        def over(self, u):
            j = self.chip(u)
            sems = (mate_send.at[self.back_stage, j], mate_got.at[self.back_stage, j])
            return self.held.at[u % 2], self.mate.at[j], lambda a, b: to(a, b, *sems, {"fsdp": group.peer})

        def near(self, source, target, u):
            return source, target, lambda a, b: pltpu.make_async_copy(a, b, stage_sem.at[self.kind, u % 2])

        def bring(self, u):
            return self.near(self.mate.at[self.chip(u)], self.held.at[u % 2], u)

        def back(self, u):
            return self.near(self.held.at[u % 2], self.mate.at[self.chip(u)], u)

        def keep(self, u):
            return self.near(self.held.at[u % 2], self.sums.at[self.home], u)

        def push(self, u):
            j = self.chip(u)
            sems = (own_send.at[self.back_stage, j], own_got.at[self.back_stage, group.chip])
            return self.mate.at[j], self.sums.at[group.chip], lambda a, b: to(a, b, *sems, {"fsdp": group.at(j)})

        def hop(self, kind):
            over_x = kind % 2 == 0
            first = over_x if kind < 4 else not over_x
            rows = pl.ds(0 if first else depth // 2, depth // 2)
            target = group.x if over_x else group.y
            sems = (own_send.at[self.back_stage, kind], own_got.at[self.back_stage, kind])
            build = lambda a, b: to(a, b, *sems, {"fsdp": target})
            if kind < 2:
                return self.mate.at[group.far // 2, rows], self.via.at[kind], build
            place = self.sums.at[1 if over_x else 2, rows]
            if kind < 4:
                return self.mate.at[target // 2, rows], place, build
            return self.via.at[1 if over_x else 0], place, build

        def send_on(self, u):
            whole(*self.back(u)).wait()
            if not group.square:
                start(*self.push(u))
                return
            for k, hops in enumerate(((0, 1), (2,), (3,))):

                @when(u % 4 == k)
                def _(hops=hops):
                    for kind in hops:
                        start(*self.hop(kind))

        def relay(self):
            if not group.square:
                return
            rest = depth // 2
            steps_in = []
            for n, (kind, target, rows) in enumerate(
                ((1, group.x, pl.ds(rest, rest)), (0, group.y, pl.ds(0, rest)))
            ):
                whole(*self.hop(kind)).wait_recv()
                pair = [
                    pltpu.make_async_copy(self.mate.at[target // 2, rows], self.held.at[n, pl.ds(0, rest)], relay_sem.at[n, 0]),
                    pltpu.make_async_copy(self.via.at[kind], self.held.at[n, pl.ds(rest, rest)], relay_sem.at[n, 1]),
                ]
                for copy in pair:
                    copy.start()
                steps_in.append((kind, pair))
            returns = []
            lanes_here = (4 - (self.kind == 0)) * self.stride
            for n, (kind, pair) in enumerate(steps_in):
                for copy in pair:
                    copy.wait()
                for at, wide in tiles(lanes_here, 512):
                    lane = slice(at, at + wide)
                    both = staged[n, 0:rest, lane].astype(F32) + staged[n, rest:depth, lane].astype(F32)
                    staged[n, 0:rest, lane] = both.astype(BF16)
                copy = pltpu.make_async_copy(self.held.at[n, pl.ds(0, rest)], self.via.at[kind], relay_sem.at[n, 0])
                copy.start()
                returns.append(copy)
            for copy, kind in zip(returns, (4, 5)):
                copy.wait()
                start(*self.hop(kind))

        def unit(self, u):
            slot = u % 2
            own = u >= chips

            @when(u + 1 < units)
            def _():
                for copy in self.fetch(u + 1):
                    copy.start()

            @when((u >= 2) & (u < chips + 2))
            def _():
                whole(*self.over(u - 2)).wait_send()

            @when(u > chips)
            def _():
                self.send_on(u - 1)

            @when(own)
            def _():
                whole(*self.over(u - chips)).wait_recv()
                start(*self.bring(u))

            for copy in self.fetch(u):
                copy.wait()
            for left in range(2):
                turned[left] = columns[slot, left].T

            @when(own)
            def _():
                whole(*self.bring(u)).wait()

            for m, (left, right) in enumerate(self.right):
                for at, wide in tiles(right.shape[1]):
                    product = dot(turned[left], right[:, at : at + wide])
                    lane = slice(m * self.stride + at, m * self.stride + at + wide)
                    before = staged[slot, :, lane].astype(F32)
                    staged[slot, :, lane] = (product + jnp.where(own, before, 0.0)).astype(BF16)

            @when(jnp.logical_not(own))
            def _():
                start(*self.over(u))

            @when(own & (u < units - 1))
            def _():
                start(*self.back(u))

            @when(u == units - 1)
            def _():
                start(*self.keep(u))

        def begin(self):
            for copy in self.fetch(0):
                copy.start()

        def run(self, i):
            def one(r, carry):
                u = i * per_step + r

                @when(u < units)
                def _():
                    self.unit(u)

                return carry

            lax.fori_loop(0, per_step, one, 0)

        def end(self):
            whole(*self.keep(units - 1)).wait()

        def finish(self):
            if group.square:
                for kind in range(6):
                    whole(*self.hop(kind)).wait_send()
                    if kind >= 2:
                        whole(*self.hop(kind)).wait_recv()
                return
            for j in range(chips):

                @when(j != group.chip)
                def _(j=j):
                    sems = (own_send.at[self.back_stage, j], own_got.at[self.back_stage, j])
                    copy = to(self.mate.at[j], self.sums.at[j], *sems, {"fsdp": group.at(j)})
                    copy.wait_send()
                    copy.wait_recv()

    def save_out(c):
        return pltpu.make_async_copy(flow.running.at[flow.slot(c)], out_states.at[block(c)], out_sem.at[c])

    def save_grad(c):
        return pltpu.make_async_copy(res.at[block(c)], grad_states.at[block(c)], out_sem.at[c])

    def step(t, carry):
        i = t % steps
        stage = t // steps
        back = stage - half
        c = jnp.where(back < 0, i, steps - 1 - i)
        run_events(t, 0)

        @when((t >= steps) & (back < 0))
        def _():
            normed_rows(stage, c)
            flow.release(i, True)

        @when(t < steps)
        def _():
            normed_rows(stage, c)

        @when(back == 0)
        def _():
            save_x(half - 1, i).wait()

        @when((i == 0) & (back >= 1) & (back < half))
        def _():
            for k in range(2):

                @when(back % 2 == k)
                def _(k=k):
                    layer = top - back // 2

                    @when(back >= 2)
                    def _():
                        for kind in (2, 3) if k == 0 else (0, 1):
                            load(layer, kind, True)
                        for copy in activations(layer, k):
                            copy.wait()

                    @when(back + 1 < half)
                    def _():
                        for kind in (0, 1) if k == 0 else (2, 3):
                            load(layer - k, kind, False)

                    if k == 1:
                        d_key[...] = jnp.zeros_like(d_key)
                        d_value[...] = jnp.zeros_like(d_value)

        for k in range(2):

            @when((i == 0) & (back >= 1) & (back % 2 != k))
            def _(k=k):
                Blocks(back - 1, k).begin()

        @when(back >= 1)
        def _():
            take(back, i, c)
            flow.release(i, t < total)

        @when((t >= total - half * steps + steps - 1) & (t < total + steps - 1))
        def _():
            after = t + 1
            fetch_x(after // steps - half, steps - 1 - after % steps).start()

        @when((back >= 1) & (back < half))
        def _():
            low[...] = res[block(c), :].astype(BF16)
            save_low(back, c).start()

        @when(back == half)
        def _():
            save_grad(c).start()

        @when((t >= steps) & (t < total))
        def _():
            flow.clear(i)

        @when(back == 0)
        def _():
            out = res[block(i), :] + flow.from_inner[flow.slot(i), :].astype(F32)
            flow.release(i, True)
            flow.running[flow.slot(i), :] = out.astype(BF16)
            save_out(i).start()
            fetch_low(c).wait()
            save_out(i).wait()

        @when((back < 0) & (stage % 2 == 0))
        def _():
            attention_forward(t, stage // 2, c)

        @when((back < 0) & (stage % 2 == 1))
        def _():
            ffn_forward(t, stage // 2, c)

        @when((back >= 0) & (back < half) & (back % 2 == 0))
        def _():
            ffn_backward(i, c)

        @when((back >= 0) & (back < half) & (back % 2 == 1))
        def _():
            attention_backward(top - back // 2, i, c)

        @when(t < total)
        def _():
            flow.push(i, t >= steps)

        run_events(t, 2)

        @when((t < total) & (back != 0))
        def _():
            save_low(0, c).wait()

        after = t + 1
        @when((after >= half * steps) & (after < (half + 2) * steps))
        def _():
            fetch_low(steps - 1 - after % steps).start()

        for k in range(2):

            @when((back >= 1) & (back % 2 != k))
            def _(k=k):
                blocks = Blocks(back - 1, k)
                blocks.run(i)

                @when(i == steps - 1)
                def _():
                    blocks.end()
                    blocks.relay()

                    @when((back + 1 < half) & (back + 1 >= 2))
                    def _():
                        for copy in activations(top - (back + 1) // 2, k):
                            copy.start()

        k = t - flow.lag

        @when((k >= 0) & (k < total))
        def _():
            flow.pull((k + steps) % steps)

        return carry

    lax.fori_loop(0, total + steps, step, 0)

    for copy in small:
        copy.wait_send()
    parts = []
    for n, other in enumerate(group.everyone):
        at = pl.multiple_of(other * depth, depth)
        sems = (small_send.at[0, n], small_got.at[0, n])
        parts.append(to(norm_acc.at[:, pl.ds(at, depth)], norm_parts.at[shards - 1 - n], *sems, {"fsdp": other}))
        sems = (small_send.at[1, n], small_got.at[1, n])
        parts.append(to(bias_acc, bias_parts.at[shards - 1 - n], *sems, {"fsdp": other}))
    for copy in parts:
        copy.start()
    own = [
        pltpu.make_async_copy(norm_acc.at[:, mine], norm_parts.at[0], misc.at[0]),
        pltpu.make_async_copy(bias_acc, bias_parts.at[0], misc.at[1]),
    ]
    for copy in own:
        copy.start()
    for copy in own:
        copy.wait()
    for i in range(steps):
        save_grad(i).wait()
        flow.clear(i)
    for layer in range(LAYERS):
        for kind in range(4):
            gather(layer, kind).finish()
    for copy in parts:
        copy.wait_send()
        copy.wait_recv()
    for back in range(half):
        Blocks(back, back % 2).finish()


def lane_stride(extent):
    return -(-extent // PAIR) * PAIR


def plan(tokens):
    return next((s, p) for s, p in ((6, 1), (3, 1), (2, 1)) if tokens % (16 * s * p) == 0)


def train(states, cotangent, own_norms, own_bias, rope, mask, own_q, own_o, own_g, own_d):
    count, shards = lax.axis_size("tensor"), lax.axis_size("fsdp")
    tokens, width = states.shape
    steps, span = plan(tokens)
    big = tokens // steps
    chips = shards // 2
    depth = width // shards
    local, ff = own_q.shape[-1], own_g.shape[-1]
    lanes_attn, lanes_ffn = 4 * lane_stride(local), 3 * lane_stride(ff)
    parts = 3 if chips == 4 else chips
    per_step = -(-2 * chips // max(steps - 2, 1))
    shape = jax.ShapeDtypeStruct
    outs = [
        shape((tokens, width), BF16),
        shape((tokens, width), F32),
        shape((LAYERS, parts, depth, lanes_attn), BF16),
        shape((LAYERS, parts, depth, lanes_ffn), BF16),
        shape((shards, 4 * LAYERS, depth), F32),
        shape((shards, LAYERS, 8, local), F32),
        *[shape((LAYERS, shards) + own.shape[1:], BF16) for own in (own_q, own_o, own_g, own_d)],
        shape((2 * LAYERS, tokens, width), F32),
        shape((2 * LAYERS, tokens, width), BF16),
        shape((2 * LAYERS, tokens, width), BF16),
        shape((LAYERS - 1, 3, tokens, local), BF16),
        shape((LAYERS - 1, tokens, local), BF16),
        shape((LAYERS - 1, 2, tokens, ff), BF16),
        shape((LAYERS - 1, tokens, ff), BF16),
        shape((LAYERS, chips, depth, lanes_attn), BF16),
        shape((LAYERS, chips, depth, lanes_ffn), BF16),
        shape((LAYERS, 2, depth // 2, lanes_attn), BF16),
        shape((LAYERS, 2, depth // 2, lanes_ffn), BF16),
    ]
    dma = pltpu.SemaphoreType.DMA
    vmem = pltpu.VMEM
    scratch = [
        vmem((tokens, width), F32),
        vmem((4, width, local), BF16),
        vmem((3, width, ff), BF16),
        vmem((2, tokens, ff), BF16),
        vmem((tokens, ff), BF16),
        vmem((3, tokens, local), BF16),
        vmem((tokens, local), BF16),
        vmem((tokens, local), F32),
        vmem((tokens, local), F32),
        vmem((big, width), F32),
        vmem((big, width), BF16),
        vmem((4 * LAYERS, width), F32),
        vmem((8, local), F32),
        vmem((shards, 8, PAIR), F32),
        vmem((4 * LAYERS, width), F32),
        vmem((LAYERS, 8, local), F32),
        vmem((2, 2, tokens, depth), BF16),
        vmem((2, depth, tokens), BF16),
        vmem((2, depth, max(lanes_attn, lanes_ffn)), BF16),
        dma((steps,)),
        dma((1,)),
        dma((2,)),
        dma((steps,)),
        dma((2, 2, steps)),
        dma((2, 2)),
        dma((4,)),
        dma((4, shards)),
        dma((4 * LAYERS, gather_kinds(shards))),
        dma((4 * LAYERS, gather_kinds(shards))),
        dma((2, 2, 2)),
        dma((2, 2)),
        dma((2, 2)),
        *([dma((2 * LAYERS, max(chips, 6)))] * 4),
        dma((2, shards)),
        dma((2, shards)),
        *flow_scratch(steps, span, tokens, width),
    ]
    flops = 6 * LAYERS * tokens * width * (4 * local + 3 * ff)
    return pl.pallas_call(
        functools.partial(train_kernel, count, shards, steps, span, per_step),
        out_shape=outs,
        in_specs=[ANY, ANY, VMEM, VMEM, VMEM, VMEM, ANY, ANY, ANY, ANY],
        out_specs=[ANY] * len(outs),
        scratch_shapes=scratch,
        compiler_params=pltpu.CompilerParams(
            collective_id=1, has_side_effects=True, vmem_limit_bytes=64 * 1024 * 1024
        ),
        cost_estimate=pl.CostEstimate(flops=flops, bytes_accessed=flops // 256, transcendentals=0),
        name="train",
    )(states, cotangent, own_norms, own_bias, rope, mask, own_q, own_o, own_g, own_d)


def finish_kernel(attn, ffn, states, grads, g_qkv, g_out, g_gate_up, g_down, out_states, out_grads):
    local, ff = g_qkv.shape[3], g_gate_up.shape[3]

    def total(parts, at, wide):
        return sum(parts[0, n, :, at : at + wide].astype(F32) for n in range(parts.shape[1]))

    for m in range(3):
        g_qkv[0, m] = total(attn, m * lane_stride(local), local)
    g_out[0] = total(attn, 3 * lane_stride(local), local).T
    for m in range(2):
        g_gate_up[0, :, m, :] = total(ffn, m * lane_stride(ff), ff)
    g_down[0] = total(ffn, 2 * lane_stride(ff), ff).T
    out_states[...] = states[...]
    out_grads[...] = grads[...]


def finish(sums_attn, sums_ffn, states, grads, local, ff):
    parts, depth = sums_attn.shape[1:3]
    tokens, width = states.shape
    rows = min(PAIR, depth)
    cuts = depth // rows
    pieces = tokens // (LAYERS * cuts)
    shape = jax.ShapeDtypeStruct
    spec = pl.BlockSpec
    token_spec = spec((pieces, width), lambda l, r: (l * cuts + r, 0))
    return pl.pallas_call(
        finish_kernel,
        grid=(LAYERS, cuts),
        in_specs=[
            spec((1, parts, rows, sums_attn.shape[3]), lambda l, r: (l, 0, r, 0)),
            spec((1, parts, rows, sums_ffn.shape[3]), lambda l, r: (l, 0, r, 0)),
            token_spec,
            token_spec,
        ],
        out_specs=[
            spec((1, 3, rows, local), lambda l, r: (l, 0, r, 0)),
            spec((1, local, rows), lambda l, r: (l, 0, r)),
            spec((1, rows, 2, ff), lambda l, r: (l, r, 0, 0)),
            spec((1, ff, rows), lambda l, r: (l, 0, r)),
            token_spec,
            token_spec,
        ],
        out_shape=[
            shape((LAYERS, 3, depth, local), F32),
            shape((LAYERS, local, depth), F32),
            shape((LAYERS, depth, 2, ff), F32),
            shape((LAYERS, ff, depth), F32),
            shape((tokens, width), BF16),
            shape((tokens, width), F32),
        ],
        compiler_params=pltpu.CompilerParams(vmem_limit_bytes=48 * 1024 * 1024),
        name="finish",
    )(sums_attn, sums_ffn, states, grads)


def tables(segment_ids, rows):
    places = jnp.arange(rows, dtype=jnp.int32)
    previous = jnp.concatenate([segment_ids[:1] - 1, segment_ids[:-1]])
    starts = lax.cummax(jnp.where(segment_ids != previous, places, jnp.zeros_like(places)), axis=0)
    position = places - starts
    half = ROT_DIM // 2
    inverse = rotary_base ** (-(jnp.arange(half, dtype=F32) * 2.0 / ROT_DIM))
    angle = position.astype(F32)[:, None] * inverse[None, :]
    cosine, sine = jnp.cos(angle), jnp.sin(angle)
    rest = jnp.zeros((rows, HEAD_DIM - ROT_DIM), F32)
    none = jnp.zeros_like(sine)
    rope = jnp.stack(
        [
            jnp.tile(jnp.concatenate([cosine, cosine, rest + 1.0], axis=1), (1, 2)),
            jnp.tile(jnp.concatenate([-sine, none, rest], axis=1), (1, 2)),
            jnp.tile(jnp.concatenate([none, sine, rest], axis=1), (1, 2)),
        ]
    )
    allowed = (segment_ids[:, None] == segment_ids[None, :]) & (places[None, :] <= places[:, None])
    return rope, allowed.astype(F32)


def on_device(
    states,
    segment_ids,
    ln1_gain,
    ln1_bias,
    qkv_weight,
    qkv_bias,
    out_weight,
    ln2_gain,
    ln2_bias,
    gate_up_weight,
    down_weight,
    cotangent,
):
    tokens = states.shape[0]
    rope, allowed = tables(segment_ids, tokens)
    steps = plan(tokens)[0]
    mask = allowed.reshape(steps, -1, tokens).transpose(0, 2, 1).astype(BF16)
    own_norms = jnp.stack([ln1_gain, ln1_bias, ln2_gain, ln2_bias], axis=1).reshape(4 * LAYERS, -1).astype(F32)
    own_bias = qkv_bias.reshape(LAYERS * 3, -1).astype(F32)
    own_bias = jnp.pad(own_bias, ((0, 8 - own_bias.shape[0]), (0, PAIR - own_bias.shape[1])))
    out_states, grad_states, sums_attn, sums_ffn, norm_parts, bias_parts, *_ = train(
        states,
        cotangent,
        own_norms,
        own_bias,
        rope,
        mask,
        qkv_weight.transpose(0, 2, 1, 3),
        out_weight.transpose(0, 2, 1)[:, None],
        gate_up_weight.transpose(0, 2, 1, 3),
        down_weight.transpose(0, 2, 1)[:, None],
    )
    g_qkv, g_out, g_gate_up, g_down, out_states, grad_states = finish(
        sums_attn, sums_ffn, out_states, grad_states, qkv_weight.shape[3], gate_up_weight.shape[3]
    )
    g_norms = jnp.sum(norm_parts, axis=0).reshape(LAYERS, 4, -1)
    g_bias = jnp.sum(bias_parts, axis=0).reshape(LAYERS, 8, -1, HEAD_DIM)[:, :3]
    share = qkv_bias.shape[3]
    g_bias = lax.dynamic_slice_in_dim(g_bias, lax.axis_index("fsdp") * share, share, axis=3)
    return (
        out_states,
        grad_states,
        g_norms[:, 0],
        g_norms[:, 1],
        g_qkv.transpose(0, 2, 1, 3),
        g_bias,
        g_out,
        g_norms[:, 2],
        g_norms[:, 3],
        g_gate_up,
        g_down,
    )


def solution(mesh):
    in_specs = (
        P("fsdp", None),
        P("fsdp"),
        P(None, "fsdp"),
        P(None, "fsdp"),
        P(None, "fsdp", None, "tensor"),
        P(None, None, "tensor", "fsdp"),
        P(None, "tensor", "fsdp"),
        P(None, "fsdp"),
        P(None, "fsdp"),
        P(None, "fsdp", None, "tensor"),
        P(None, "tensor", "fsdp"),
        P("fsdp", None),
    )
    out_specs = (
        P("fsdp", None),
        P("fsdp", None),
        P(None, "fsdp"),
        P(None, "fsdp"),
        P(None, "fsdp", None, "tensor"),
        P(None, None, "tensor", "fsdp"),
        P(None, "tensor", "fsdp"),
        P(None, "fsdp"),
        P(None, "fsdp"),
        P(None, "fsdp", None, "tensor"),
        P(None, "tensor", "fsdp"),
    )
    return jax.shard_map(
        on_device, mesh=mesh, in_specs=in_specs, out_specs=out_specs, check_vma=False
    )
```

```python
import functools
import math

import jax
import jax.numpy as jnp
from jax import lax
from jax.experimental import pallas as pl
from jax.experimental.pallas import tpu as pltpu
from jax.sharding import PartitionSpec as P

MESH = pl.DeviceIdType.MESH
HEAD_DIM = 64
ROT_DIM = 16
LAYERS = 2
PAIR = 2 * HEAD_DIM
ANY = pl.BlockSpec(memory_space=pl.ANY)
VMEM = pl.BlockSpec(memory_space=pltpu.VMEM)
BF16 = jnp.bfloat16
F32 = jnp.float32

norm_epsilon = 1e-05
rotary_base = 10000.0


def dot(a, b):
    return lax.dot_general(a, b, (((1,), (0,)), ((), ())), preferred_element_type=F32)


def dot_nt(a, b):
    return lax.dot_general(a, b, (((1,), (1,)), ((), ())), preferred_element_type=F32)


def dot_tn(a, b):
    return lax.dot_general(a, b, (((0,), (0,)), ((), ())), preferred_element_type=F32)


def tiles(extent, most=512):
    return [(at, min(most, extent - at)) for at in range(0, extent, most)]


def standardize(values):
    average = jnp.mean(values, axis=-1, keepdims=True)
    centred = values - average
    spread = jnp.mean(centred * centred, axis=-1, keepdims=True)
    rstd = lax.rsqrt(spread + norm_epsilon)
    return centred * rstd, rstd


def turn(values, rope, sign):
    half = ROT_DIM // 2
    factor, below, above = rope
    return values * factor + sign * (
        pltpu.roll(values, PAIR - half, 1) * below + pltpu.roll(values, half, 1) * above
    )


def when(condition):
    return pl.when(condition)


def to(source, target, send, arrive, place):
    return pltpu.make_async_remote_copy(
        src_ref=source, dst_ref=target, send_sem=send, recv_sem=arrive, device_id=place, device_id_type=MESH
    )


def spread(build, source, target, count=4):
    rows = source.shape[-2] // count
    for r in range(count):
        piece = (slice(None),) * (len(source.shape) - 2) + (pl.ds(r * rows, rows), slice(None))
        build(source.at[piece], target.at[piece]).start()


def start(source, target, build):
    spread(build, source, target)


def whole(source, target, build):
    return build(source, target)


class Line:
    def __init__(self, count):
        place = lax.axis_index("tensor")
        half = count // 2
        left = place < half
        self.inner = jnp.where(left, place + 1, place - 1)
        self.outer = jnp.where(left, place - 1, place + 1)
        self.has_outer = (place != 0) & (place != count - 1)
        self.no_outer = jnp.logical_not(self.has_outer)
        self.distance = jnp.where(left, half - 1 - place, place - half)
        self.centre = self.distance == 0
        self.off_centre = jnp.logical_not(self.centre)


class Group:
    def __init__(self, count):
        self.count = count
        self.chips = count // 2
        self.me = lax.axis_index("fsdp")
        self.chip = self.me // 2
        self.core = self.me % 2
        self.peer = self.me + 1 - 2 * self.core
        self.square = self.chips == 4
        self.everyone = [(self.me + i) % count for i in range(1, count)]
        if self.square:
            self.x = self.at(self.chip + 1 - 2 * (self.chip % 2))
            self.y = self.at(self.chip + 2 - 4 * (self.chip // 2))
            self.far = self.at(3 - self.chip)
            self.others = [self.x, self.y]
        else:
            self.others = [self.at((self.chip + i) % self.chips) for i in range(1, self.chips)]

    def at(self, chip):
        return chip * 2 + self.core


def enter(line, partners):
    barrier = pltpu.get_barrier_semaphore()
    for partner in partners:
        pl.semaphore_signal(barrier, inc=1, device_id={"fsdp": partner}, device_id_type=MESH)
    pl.semaphore_signal(barrier, inc=1, device_id={"tensor": line.inner}, device_id_type=MESH)

    @when(line.has_outer)
    def _():
        pl.semaphore_signal(barrier, inc=1, device_id={"tensor": line.outer}, device_id_type=MESH)
        pl.semaphore_wait(barrier, len(partners) + 2)

    @when(line.no_outer)
    def _():
        pl.semaphore_wait(barrier, len(partners) + 1)


class Flow:
    def __init__(self, line, steps, span, rows, refs):
        self.line, self.steps, self.span, self.rows = line, steps, span, rows
        self.from_outer, self.from_inner, self.running = refs[:3]
        self.send_in, self.got_out, self.send_out, self.got_in, self.credit = refs[3:]
        self.lag = jnp.minimum(3 * line.distance + 2, steps - 1)

    def slot(self, i):
        big = self.rows * self.span
        return pl.ds(pl.multiple_of(i * big, big), big)

    def pieces(self, i):
        for r in range(self.span):
            q = i * self.span + r
            yield q, pl.ds(pl.multiple_of(q * self.rows, self.rows), self.rows)

    def inward(self, q, here, target, arrive):
        return to(
            self.running.at[here], target.at[here], self.send_in.at[q], arrive.at[q], {"tensor": self.line.inner}
        )

    def outward(self, q, here):
        return to(
            self.from_inner.at[here], self.from_inner.at[here], self.send_out.at[q], self.got_in.at[q],
            {"tensor": self.line.outer},
        )

    def clear(self, i):
        for q, here in self.pieces(i):
            self.inward(q, here, self.from_inner, self.got_in).wait_send()

    def push(self, i, again):
        line = self.line

        @when(line.centre & again)
        def _():
            pl.semaphore_wait(self.credit, 1)

        for q, here in self.pieces(i):

            @when(line.has_outer)
            def _(q=q, here=here):
                self.inward(q, here, self.from_outer, self.got_out).wait_recv()
                total = self.running[here, :].astype(F32) + self.from_outer[here, :].astype(F32)
                self.running[here, :] = total.astype(BF16)

            @when(line.centre)
            def _(q=q, here=here):
                self.inward(q, here, self.from_inner, self.got_in).start()

            @when(line.off_centre)
            def _(q=q, here=here):
                self.inward(q, here, self.from_outer, self.got_out).start()

    def pull(self, i):
        line = self.line
        for q, here in self.pieces(i):
            self.inward(q, here, self.from_inner, self.got_in).wait_recv()

            @when(line.centre)
            def _(q=q, here=here):
                total = self.running[here, :].astype(F32) + self.from_inner[here, :].astype(F32)
                self.from_inner[here, :] = total.astype(BF16)

            @when(line.has_outer)
            def _(q=q, here=here):
                self.outward(q, here).start()

    def release(self, i, more):
        line = self.line

        @when(line.has_outer)
        def _():
            for q, here in self.pieces(i):
                self.outward(q, here).wait_send()

        @when(line.centre & more)
        def _():
            pl.semaphore_signal(self.credit, inc=1, device_id={"tensor": line.inner}, device_id_type=MESH)


def flow_scratch(steps, span, tokens, width):
    whole = pltpu.VMEM((tokens, width), BF16)
    sems = pltpu.SemaphoreType.DMA((steps * span,))
    return [whole, whole, whole, sems, sems, sems, sems, pltpu.SemaphoreType.REGULAR]


def gather_kinds(count):
    return 9 if count == 8 else count


class Gather:
    def __init__(self, group, own, whole, send, arrive, load):
        self.group, self.own, self.whole, self.send, self.arrive, self.load_sems = group, own, whole, send, arrive, load
        self.half = own.shape[1] // 2
        self.links = len(group.others)

    def half_at(self, shard, h):
        return self.whole.at[shard, :, pl.ds(h * self.half, self.half), :]

    def way(self, kind):
        g, links = self.group, self.links
        if kind < links:
            return self.own, self.whole.at[g.me], g.others[kind]
        if kind == links:
            return self.own, self.whole.at[g.me], g.peer
        if kind <= 2 * links:
            shard = self.whole.at[g.others[kind - links - 1]]
            return shard, shard, g.peer
        if kind == 2 * links + 1:
            return self.half_at(g.x, 0), self.half_at(g.x, 0), g.y
        if kind == 2 * links + 2:
            return self.half_at(g.y, 1), self.half_at(g.y, 1), g.x
        return self.whole.at[g.far], self.whole.at[g.far], g.peer

    def build(self, kind, source, target):
        return to(source, target, self.send.at[kind], self.arrive.at[kind], {"fsdp": self.way(kind)[2]})

    def copy(self, kind):
        return self.build(kind, *self.way(kind)[:2])

    def start(self, kind):
        spread(functools.partial(self.build, kind), *self.way(kind)[:2])

    def local(self):
        return pltpu.make_async_copy(self.own, self.whole.at[self.group.me], self.send.at[gather_kinds(self.group.count) - 1])

    def begin(self):
        for kind in range(self.links + 1):
            self.start(kind)
        self.local().start()

    def relay(self):
        for kind in range(self.links):
            self.copy(kind).wait_recv()
        if self.group.square:
            self.start(2 * self.links + 1)
            self.start(2 * self.links + 2)
        for kind in range(self.links):
            self.start(self.links + 1 + kind)

    def relay_far(self):
        if self.group.square:
            self.copy(2 * self.links + 1).wait_recv()
            self.copy(2 * self.links + 2).wait_recv()
            self.start(2 * self.links + 3)

    def settle(self):
        self.local().wait()
        for kind in range(self.links, 2 * self.links + 1):
            self.copy(kind).wait_recv()
        if self.group.square:
            self.copy(2 * self.links + 3).wait_recv()

    def loads(self, target):
        depth = self.own.shape[1]
        for k in range(self.group.count):
            yield pltpu.make_async_copy(
                self.whole.at[k], target.at[:, pl.ds(k * depth, depth), :], self.load_sems.at[k]
            )

    def finish(self):
        for kind in range(2 * self.links + 1 + (3 if self.group.square else 0)):
            self.copy(kind).wait_send()


def train_kernel(
    count, shards, steps, span, per_step,
    states, cotangent, own_norms, own_bias, rope, mask, own_q, own_o, own_g, own_d,
    out_states, grad_states, sums_attn, sums_ffn, norm_parts, bias_parts,
    whole_q, whole_o, whole_g, whole_d, s_x, s_n, s_y, s_qkv, s_att, s_gu, s_hid,
    mate_attn, mate_ffn, via_attn, via_ffn,
    res, w_attn, w_ffn, gu, hid, qkv, att, d_key, d_value, x_in, low,
    log_total, norms, biases, bias_in, norm_acc, bias_acc, columns, turned, staged,
    x_save, x_sem, low_sem, out_sem, keep_sem, act_sem, misc, load_sem, g_send, g_arrive,
    column_sem, stage_sem, relay_sem, mate_send, mate_got, own_send, own_got, small_send, small_got,
    *flow_refs,
):
    tokens, width = res.shape
    big = tokens // steps
    local, ff = w_attn.shape[2], w_ffn.shape[2]
    depth = width // shards
    line = Line(count)
    group = Group(shards)
    chips = group.chips
    flow = Flow(line, steps, span, big // span, flow_refs)
    scale = jnp.asarray(1.0 / math.sqrt(HEAD_DIM), BF16)
    half = 2 * LAYERS
    stages = 2 * half
    total = stages * steps
    top = LAYERS - 1
    units = 2 * chips

    def block(c):
        return pl.ds(pl.multiple_of(c * big, big), big)

    kinds = [(own_q, whole_q), (own_o, whole_o), (own_g, whole_g), (own_d, whole_d)]
    targets = [w_attn.at[0:3], w_attn.at[3:4], w_ffn.at[0:2], w_ffn.at[2:3]]

    def gather(layer, kind):
        n = 4 * layer + kind
        own, whole = kinds[kind]
        return Gather(group, own.at[layer], whole.at[layer], g_send.at[n], g_arrive.at[n], load_sem.at[kind])

    def load(layer, kind, wait):
        own, whole = kinds[kind]
        way = Gather(group, own.at[0], whole.at[layer], g_send.at[0], g_arrive.at[0], load_sem.at[kind])
        for copy in way.loads(targets[kind]):
            if wait:
                copy.wait()
            else:
                copy.start()

    events = {}

    def event(t, where, *actions):
        events.setdefault((t, where, None), []).extend(actions)

    def event_by_role(centre, others, *actions):
        events.setdefault(centre + (True,), []).extend(actions)
        events.setdefault(others + (False,), []).extend(actions)

    def loading(layer, kind, wait):
        return functools.partial(load, layer, kind, wait)

    def at(stage, i):
        return stage * steps + min(i, steps - 1)

    q, o, g, d = 0, 1, 2, 3
    event(0, 1, gather(0, o).relay_far, gather(0, o).settle, loading(0, o, False), loading(0, o, True))
    event_by_role((at(0, 3), 0), (at(0, 4), 0), gather(0, g).relay)
    event_by_role((at(0, 5), 0), (at(0, 5), 2), gather(0, g).relay_far, gather(0, d).begin)
    event(at(1, 0), 0, gather(0, g).settle, loading(0, g, False), loading(0, g, True))
    event(at(1, 0), 1, gather(0, d).relay)
    for layer in range(1, LAYERS):
        s = 2 * layer - 1
        event(at(s, 0), 1, gather(layer, q).begin)
        if layer == 1:
            event(at(s, 0), 1, gather(0, d).relay_far, gather(0, d).settle, loading(0, d, False), loading(0, d, True))
        event(at(s, 2), 0, gather(layer, q).relay, gather(layer, o).begin)
        event_by_role((at(s, 3), 0), (at(s, 3), 2), gather(layer, q).relay_far, gather(layer, o).relay, gather(layer, g).begin)
        event(at(s, 4), 2, gather(layer, o).relay_far)
        event(at(s, 5), 2, gather(layer, q).settle, loading(layer, q, False))
        event(at(s, 5), 2, gather(layer, o).settle, loading(layer, o, False))
        s += 1
        event(at(s, 0), 0, loading(layer, q, True), loading(layer, o, True))
        event_by_role((at(s, 0), 0), (at(s, 0), 2), gather(layer, g).relay)
        event_by_role((at(s, 2), 0), (at(s, 2), 2), gather(layer, g).relay_far, gather(layer, d).begin)
        event(at(s, 3), 2, gather(layer, g).settle, loading(layer, g, False))
        event_by_role((at(s, 4), 0), (at(s, 4), 2), gather(layer, d).relay)
        event(at(s, 5), 2, gather(layer, d).relay_far)
        s += 1
        event(at(s, 0), 0, loading(layer, g, True), gather(layer, d).settle, loading(layer, d, False))
        event(at(s, 0), 1, loading(layer, d, True))

    def run_events(t, where):
        ordered = sorted(events.items(), key=lambda item: item[0][:2])
        ordered = [(at, role, actions) for (at, place, role), actions in ordered if place == where]
        for stage in sorted({at // steps for at, _, _ in ordered}):

            @when(t // steps == stage)
            def _(stage=stage):
                for at, role, actions in ordered:
                    if at // steps != stage:
                        continue
                    condition = t == at
                    if role is not None:
                        condition = condition & (line.centre if role else line.off_centre)

                    @when(condition)
                    def _(actions=actions):
                        for action in actions:
                            action()

    enter(line, group.everyone)
    mine = pl.ds(pl.multiple_of(group.me * depth, depth), depth)
    small = []
    for n, other in enumerate(group.everyone):
        sems = (small_send.at[0, n], small_got.at[0, n])
        small.append(to(own_norms, norms.at[:, mine], *sems, {"fsdp": other}))
        sems = (small_send.at[1, n], small_got.at[1, n])
        small.append(to(own_bias, bias_in.at[group.me], *sems, {"fsdp": other}))
    gather(0, q).begin()
    for copy in small:
        copy.start()
    starts = [
        pltpu.make_async_copy(own_norms, norms.at[:, mine], misc.at[0]),
        pltpu.make_async_copy(own_bias, bias_in.at[group.me], misc.at[1]),
        pltpu.make_async_copy(states, flow.running, misc.at[2]),
        pltpu.make_async_copy(cotangent, s_y.at[0], misc.at[3]),
    ]
    for copy in starts:
        copy.start()
    qkv[...] = jnp.zeros_like(qkv)
    norm_acc[...] = jnp.zeros_like(norm_acc)
    bias_acc[...] = jnp.zeros_like(bias_acc)
    for copy in starts:
        copy.wait()
    for c in range(steps):
        res[c * big : (c + 1) * big, :] = flow.running[c * big : (c + 1) * big, :].astype(F32)
    for copy in small:
        copy.wait_recv()
    each = HEAD_DIM // shards
    source = lax.broadcasted_iota(jnp.int32, (PAIR, local), 0)
    column = lax.broadcasted_iota(jnp.int32, (PAIR, local), 1)
    at_head = lax.div(source, each) == lax.div(column, HEAD_DIM)
    whole_bias = jnp.zeros((8, local), F32)
    for k in range(shards):
        match = at_head & (lax.rem(column, HEAD_DIM) == k * each + lax.rem(source, each))
        whole_bias += dot(bias_in[k].astype(BF16), jnp.where(match, 1.0, 0.0).astype(BF16))
    biases[...] = whole_bias
    gather(0, q).relay()
    gather(0, o).begin()
    gather(0, q).relay_far()
    gather(0, o).relay()
    gather(0, g).begin()
    gather(0, q).settle()
    load(0, q, False)
    load(0, q, True)

    lanes = lax.broadcasted_iota(jnp.int32, (big, PAIR), 1)
    first_head = lanes < HEAD_DIM

    def save_x(stage, c):
        return pltpu.make_async_copy(res.at[block(c)], s_x.at[stage, block(c)], x_save.at[c])

    def keeps(layer, kind, c):
        here = block(c)
        if kind == 0:
            pairs = [(gu.at[:, here], s_gu.at[layer, :, here]), (hid.at[here], s_hid.at[layer, here])]
        else:
            pairs = [(qkv.at[:, here], s_qkv.at[layer, :, here]), (att.at[here], s_att.at[layer, here])]
        return [pltpu.make_async_copy(a, b, keep_sem.at[kind, n, c]) for n, (a, b) in enumerate(pairs)]

    def activations(layer, kind):
        if kind == 0:
            pairs = [(s_gu.at[layer], gu), (s_hid.at[layer], hid)]
        else:
            pairs = [(s_qkv.at[layer], qkv), (s_att.at[layer], att)]
        return [pltpu.make_async_copy(a, b, act_sem.at[kind, n]) for n, (a, b) in enumerate(pairs)]

    def project(*pairs):
        def write(i):
            here = flow.slot(i)
            for at, wide in tiles(width, 1024):
                part = sum(dot_nt(right[at : at + wide, :], left()) for left, right in pairs)
                flow.running[here, at : at + wide] = part.T.astype(BF16)

        return write

    def by_extent(c, work):
        early = steps // 2

        @when(c < early)
        def _():
            work(early * big)

        @when(c >= early)
        def _():
            work(tokens)

    def normed_rows(stage, c):
        here = block(c)

        @when(stage > 0)
        def _():
            save_x(stage, c).wait()
            res[here, :] += flow.from_inner[flow.slot(c), :].astype(F32)

        save_x(stage, c).start()
        xhat, _ = standardize(res[here, :])
        low[...] = (xhat * norms[pl.ds(2 * stage, 1), :] + norms[pl.ds(2 * stage + 1, 1), :]).astype(BF16)
        pltpu.make_async_copy(low, s_n.at[stage, here], low_sem.at[0]).start()

    def attention_forward(t, layer, c):
        here = block(c)

        @when(layer > 0)
        def _():
            for copy in keeps(layer - 1, 1, c):
                copy.wait()

        for part in range(3):
            for at, wide in tiles(local):
                mixed = dot(low[...], w_attn[part, :, at : at + wide])
                for pair in range(wide // PAIR):
                    to_lane = at + pair * PAIR
                    span_here = slice(to_lane, to_lane + PAIR)
                    value = mixed[:, pair * PAIR : (pair + 1) * PAIR]
                    value = value + biases[pl.ds(3 * layer + part, 1), :][:, span_here]
                    if part < 2:
                        value = turn(value, [rope[n, here, :] for n in range(3)], 1.0)
                    qkv[part, here, span_here] = value.astype(BF16)
        def attend(keys):
            closed = mask[c, 0:keys].astype(F32)
            for pair in range(local // PAIR):
                lane = slice(pair * PAIR, (pair + 1) * PAIR)
                query, key, value = qkv[0, here, lane] * scale, qkv[1, 0:keys, lane], qkv[2, 0:keys, lane]
                outs = []
                for head in range(2):
                    own = first_head if head == 0 else jnp.logical_not(first_head)
                    scores = dot_nt(key, jnp.where(own, query, jnp.zeros_like(query))) + closed
                    most = jnp.max(scores, axis=0, keepdims=True)
                    exps = jnp.exp(scores - most)
                    total_exp = jnp.sum(exps, axis=0, keepdims=True)
                    log_total[layer, c, 2 * pair + head : 2 * pair + head + 1, :] = most + jnp.log(total_exp)
                    probs = exps * (1.0 / total_exp)
                    outs.append(dot_tn(probs.astype(BF16), value))
                att[here, lane] = jnp.where(first_head, outs[0], outs[1]).astype(BF16)

        by_extent(c, attend)

        @when(layer < top)
        def _():
            for copy in keeps(layer, 1, c):
                copy.start()

        run_events(t, 1)
        project((lambda: att[here, :], w_attn.at[3]))(c)

    def ffn_forward(t, layer, c):
        here = block(c)

        @when(layer > 0)
        def _():
            for copy in keeps(layer - 1, 0, c):
                copy.wait()

        for at, wide in tiles(ff):
            gate = dot(low[...], w_ffn[0, :, at : at + wide])
            up = dot(low[...], w_ffn[1, :, at : at + wide])
            gu[0, here, at : at + wide] = gate.astype(BF16)
            gu[1, here, at : at + wide] = up.astype(BF16)
            hid[here, at : at + wide] = (gate * jax.nn.sigmoid(gate) * up).astype(BF16)

        @when(layer < top)
        def _():
            for copy in keeps(layer, 0, c):
                copy.start()

        run_events(t, 1)
        project((lambda: hid[here, :], w_ffn.at[2]))(c)

    def fetch_x(back, c):
        return pltpu.make_async_copy(s_x.at[half - back, block(c)], x_in, x_sem.at[0])

    def fetch_low(c):
        return pltpu.make_async_copy(s_y.at[0, block(c)], low, low_sem.at[1])

    def save_low(back, c):
        return pltpu.make_async_copy(low, s_y.at[back, block(c)], low_sem.at[0])

    def take(back, i, c):
        here = block(c)
        row = 2 * (half - back)
        fetch_x(back, c).wait()

        @when(back == 1)
        def _():
            fetch_low(c).wait()
            res[here, :] = low[...].astype(F32)

        xhat, rstd = standardize(x_in[...])
        e = flow.from_inner[flow.slot(i), :].astype(F32)
        scaled = e * norms[pl.ds(row, 1), :]
        inner = jnp.mean(scaled * xhat, axis=-1, keepdims=True)
        res[here, :] += rstd * (scaled - jnp.mean(scaled, axis=-1, keepdims=True) - xhat * inner)
        norm_acc[pl.ds(row, 1), :] += jnp.sum(e * xhat, axis=0, keepdims=True)
        norm_acc[pl.ds(row + 1, 1), :] += jnp.sum(e, axis=0, keepdims=True)

    def ffn_backward(i, c):
        here = block(c)
        for at, wide in tiles(ff):
            lane = slice(at, at + wide)
            d_hidden = dot(low[...], w_ffn[2, :, lane])
            gate, up = gu[0, here, lane].astype(F32), gu[1, here, lane].astype(F32)
            sigma = jax.nn.sigmoid(gate)
            gu[0, here, lane] = (d_hidden * up * sigma * (1.0 + gate * (1.0 - sigma))).astype(BF16)
            gu[1, here, lane] = (d_hidden * gate * sigma).astype(BF16)
        project((lambda: gu[0, here, :], w_ffn.at[0]), (lambda: gu[1, here, :], w_ffn.at[1]))(i)

    def attention_backward(layer, i, c):
        here = block(c)
        def attend_back(keys):
            closed = mask[c, 0:keys].astype(F32)
            turns = [rope[n, here, :] for n in range(3)]
            for pair in range(local // PAIR):
                lane = slice(pair * PAIR, (pair + 1) * PAIR)
                d_att = dot(low[...], w_attn[3, :, lane]).astype(BF16)
                query, key, value = qkv[0, here, lane], qkv[1, 0:keys, lane], qkv[2, 0:keys, lane]
                d_query = []
                for head in range(2):
                    own = first_head if head == 0 else jnp.logical_not(first_head)
                    own_query = jnp.where(own, query, jnp.zeros_like(query)) * scale
                    own_d_att = jnp.where(own, d_att, jnp.zeros_like(d_att))
                    scores = dot_nt(key, own_query) + closed
                    probs = jnp.exp(scores - log_total[layer, c, 2 * pair + head : 2 * pair + head + 1, :])
                    d_probs = dot_nt(value, own_d_att)
                    d_scores = probs * (d_probs - jnp.sum(probs * d_probs, axis=0, keepdims=True))
                    d_scores = d_scores.astype(BF16)
                    d_value[0:keys, lane] += dot(probs.astype(BF16), own_d_att)
                    d_key[0:keys, lane] += dot(d_scores, own_query)
                    d_query.append(dot_tn(d_scores, key))
                parts = [
                    turn(jnp.where(first_head, d_query[0], d_query[1]) / math.sqrt(HEAD_DIM), turns, -1.0),
                    turn(d_key[here, lane], turns, -1.0),
                    d_value[here, lane],
                ]
                for part, values in enumerate(parts):
                    values = values.astype(BF16)
                    qkv[part, here, lane] = values
                    bias_acc[layer, part : part + 1, lane] += jnp.sum(values.astype(F32), axis=0, keepdims=True)

        by_extent(c, attend_back)
        project(
            (lambda: qkv[0, here, :], w_attn.at[0]),
            (lambda: qkv[1, here, :], w_attn.at[1]),
            (lambda: qkv[2, here, :], w_attn.at[2]),
        )(i)

    class Blocks:
        def __init__(self, back, kind):
            self.back_stage, self.kind = back, kind
            layer = top - back // 2
            self.sums = (sums_ffn if kind == 0 else sums_attn).at[layer]
            self.mate = (mate_ffn if kind == 0 else mate_attn).at[layer]
            self.via = (via_ffn if kind == 0 else via_attn).at[layer]
            self.home = 0 if group.square else group.chip
            self.stride = lane_stride(ff if kind == 0 else local)
            self.held = staged.at[:, :, 0 : (4 - (kind == 0)) * self.stride]
            self.x = s_n.at[2 * layer + 1 - kind]
            self.y = s_y.at[back]
            if kind == 0:
                self.right = [(0, gu.at[0]), (0, gu.at[1]), (1, hid)]
            else:
                self.right = [(0, qkv.at[0]), (0, qkv.at[1]), (0, qkv.at[2]), (1, att)]

        def chip(self, u):
            if not group.square:
                return (group.chip + 1 + u) % chips
            x, y, far = group.x // 2, group.y // 2, group.far // 2
            k = u % 4
            return jnp.where(k == 0, far, jnp.where(k == 1, x, jnp.where(k == 2, y, group.chip)))

        def fetch(self, u):
            core = jnp.where(u < chips, 1 - group.core, group.core)
            at = pl.multiple_of((self.chip(u) * 2 + core) * depth, depth)
            return [
                pltpu.make_async_copy(
                    source.at[:, pl.ds(at, depth)], columns.at[u % 2, n], column_sem.at[self.kind, u % 2, n]
                )
                for n, source in enumerate((self.x, self.y))
            ]

        def over(self, u):
            j = self.chip(u)
            sems = (mate_send.at[self.back_stage, j], mate_got.at[self.back_stage, j])
            return self.held.at[u % 2], self.mate.at[j], lambda a, b: to(a, b, *sems, {"fsdp": group.peer})

        def near(self, source, target, u):
            return source, target, lambda a, b: pltpu.make_async_copy(a, b, stage_sem.at[self.kind, u % 2])

        def bring(self, u):
            return self.near(self.mate.at[self.chip(u)], self.held.at[u % 2], u)

        def back(self, u):
            return self.near(self.held.at[u % 2], self.mate.at[self.chip(u)], u)

        def keep(self, u):
            return self.near(self.held.at[u % 2], self.sums.at[self.home], u)

        def push(self, u):
            j = self.chip(u)
            sems = (own_send.at[self.back_stage, j], own_got.at[self.back_stage, group.chip])
            return self.mate.at[j], self.sums.at[group.chip], lambda a, b: to(a, b, *sems, {"fsdp": group.at(j)})

        def hop(self, kind):
            over_x = kind % 2 == 0
            first = over_x if kind < 4 else not over_x
            rows = pl.ds(0 if first else depth // 2, depth // 2)
            target = group.x if over_x else group.y
            sems = (own_send.at[self.back_stage, kind], own_got.at[self.back_stage, kind])
            build = lambda a, b: to(a, b, *sems, {"fsdp": target})
            if kind < 2:
                return self.mate.at[group.far // 2, rows], self.via.at[kind], build
            place = self.sums.at[1 if over_x else 2, rows]
            if kind < 4:
                return self.mate.at[target // 2, rows], place, build
            return self.via.at[1 if over_x else 0], place, build

        def send_on(self, u):
            whole(*self.back(u)).wait()
            if not group.square:
                start(*self.push(u))
                return
            for k, hops in enumerate(((0, 1), (2,), (3,))):

                @when(u % 4 == k)
                def _(hops=hops):
                    for kind in hops:
                        start(*self.hop(kind))

        def relay(self):
            if not group.square:
                return
            rest = depth // 2
            steps_in = []
            for n, (kind, target, rows) in enumerate(
                ((1, group.x, pl.ds(rest, rest)), (0, group.y, pl.ds(0, rest)))
            ):
                whole(*self.hop(kind)).wait_recv()
                pair = [
                    pltpu.make_async_copy(self.mate.at[target // 2, rows], self.held.at[n, pl.ds(0, rest)], relay_sem.at[n, 0]),
                    pltpu.make_async_copy(self.via.at[kind], self.held.at[n, pl.ds(rest, rest)], relay_sem.at[n, 1]),
                ]
                for copy in pair:
                    copy.start()
                steps_in.append((kind, pair))
            returns = []
            lanes_here = (4 - (self.kind == 0)) * self.stride
            for n, (kind, pair) in enumerate(steps_in):
                for copy in pair:
                    copy.wait()
                for at, wide in tiles(lanes_here, 512):
                    lane = slice(at, at + wide)
                    both = staged[n, 0:rest, lane].astype(F32) + staged[n, rest:depth, lane].astype(F32)
                    staged[n, 0:rest, lane] = both.astype(BF16)
                copy = pltpu.make_async_copy(self.held.at[n, pl.ds(0, rest)], self.via.at[kind], relay_sem.at[n, 0])
                copy.start()
                returns.append(copy)
            for copy, kind in zip(returns, (4, 5)):
                copy.wait()
                start(*self.hop(kind))

        def unit(self, u):
            slot = u % 2
            own = u >= chips

            @when(u + 1 < units)
            def _():
                for copy in self.fetch(u + 1):
                    copy.start()

            @when((u >= 2) & (u < chips + 2))
            def _():
                whole(*self.over(u - 2)).wait_send()

            @when(u > chips)
            def _():
                self.send_on(u - 1)

            @when(own)
            def _():
                whole(*self.over(u - chips)).wait_recv()
                start(*self.bring(u))

            for copy in self.fetch(u):
                copy.wait()
            for left in range(2):
                turned[left] = columns[slot, left].T

            @when(own)
            def _():
                whole(*self.bring(u)).wait()

            for m, (left, right) in enumerate(self.right):
                for at, wide in tiles(right.shape[1]):
                    product = dot(turned[left], right[:, at : at + wide])
                    lane = slice(m * self.stride + at, m * self.stride + at + wide)
                    before = staged[slot, :, lane].astype(F32)
                    staged[slot, :, lane] = (product + jnp.where(own, before, 0.0)).astype(BF16)

            @when(jnp.logical_not(own))
            def _():
                start(*self.over(u))

            @when(own & (u < units - 1))
            def _():
                start(*self.back(u))

            @when(u == units - 1)
            def _():
                start(*self.keep(u))

        def begin(self):
            for copy in self.fetch(0):
                copy.start()

        def run(self, first, last):
            def one(u, carry):
                self.unit(u)
                return carry

            lax.fori_loop(first, last, one, 0)

        def end(self):
            whole(*self.keep(units - 1)).wait()

        def finish(self):
            if group.square:
                for kind in range(6):
                    whole(*self.hop(kind)).wait_send()
                    if kind >= 2:
                        whole(*self.hop(kind)).wait_recv()
                return
            for j in range(chips):

                @when(j != group.chip)
                def _(j=j):
                    sems = (own_send.at[self.back_stage, j], own_got.at[self.back_stage, j])
                    copy = to(self.mate.at[j], self.sums.at[j], *sems, {"fsdp": group.at(j)})
                    copy.wait_send()
                    copy.wait_recv()

    def save_out(c):
        return pltpu.make_async_copy(flow.running.at[flow.slot(c)], out_states.at[block(c)], out_sem.at[c])

    def save_grad(c):
        return pltpu.make_async_copy(res.at[block(c)], grad_states.at[block(c)], out_sem.at[c])

    def step(t, carry):
        i = t % steps
        stage = t // steps
        back = stage - half
        c = jnp.where(back < 0, i, steps - 1 - i)
        run_events(t, 0)

        @when((t >= steps) & (back < 0))
        def _():
            normed_rows(stage, c)
            flow.release(i, True)

        @when(t < steps)
        def _():
            normed_rows(stage, c)

        @when(back == 0)
        def _():
            save_x(half - 1, i).wait()

        @when((i == 0) & (back >= 1) & (back < half))
        def _():
            for k in range(2):

                @when(back % 2 == k)
                def _(k=k):
                    layer = top - back // 2

                    @when(back >= 2)
                    def _():
                        for kind in (2, 3) if k == 0 else (0, 1):
                            load(layer, kind, True)
                        for copy in activations(layer, k):
                            copy.wait()

                    @when(back + 1 < half)
                    def _():
                        for kind in (0, 1) if k == 0 else (2, 3):
                            load(layer - k, kind, False)

                    if k == 1:
                        d_key[...] = jnp.zeros_like(d_key)
                        d_value[...] = jnp.zeros_like(d_value)

        for k in range(2):

            @when((i == 0) & (back >= 1) & (back % 2 != k))
            def _(k=k):
                Blocks(back - 1, k).begin()

        @when(back >= 1)
        def _():
            take(back, i, c)
            flow.release(i, t < total)

        @when((t >= total - half * steps + steps - 1) & (t < total + steps - 1))
        def _():
            after = t + 1
            fetch_x(after // steps - half, steps - 1 - after % steps).start()

        @when((back >= 1) & (back < half))
        def _():
            low[...] = res[block(c), :].astype(BF16)
            save_low(back, c).start()

        @when(back == half)
        def _():
            save_grad(c).start()

        @when((t >= steps) & (t < total))
        def _():
            flow.clear(i)

        @when(back == 0)
        def _():
            out = res[block(i), :] + flow.from_inner[flow.slot(i), :].astype(F32)
            flow.release(i, True)
            flow.running[flow.slot(i), :] = out.astype(BF16)
            save_out(i).start()
            fetch_low(c).wait()
            save_out(i).wait()

        @when((back < 0) & (stage % 2 == 0))
        def _():
            attention_forward(t, stage // 2, c)

        @when((back < 0) & (stage % 2 == 1))
        def _():
            ffn_forward(t, stage // 2, c)

        @when((back >= 0) & (back < half) & (back % 2 == 0))
        def _():
            ffn_backward(i, c)

        @when((back >= 0) & (back < half) & (back % 2 == 1))
        def _():
            attention_backward(top - back // 2, i, c)

        @when(t < total)
        def _():
            flow.push(i, t >= steps)

        run_events(t, 2)

        @when((t < total) & (back != 0))
        def _():
            save_low(0, c).wait()

        after = t + 1
        @when((after >= half * steps) & (after < (half + 2) * steps))
        def _():
            fetch_low(steps - 1 - after % steps).start()

        for k in range(2):

            @when((back >= 1) & (back % 2 != k))
            def _(k=k):
                blocks = Blocks(back - 1, k)
                extra = back == half
                pace = jnp.where(extra, 2 * per_step, per_step)
                blocks.run(jnp.minimum(i * pace, units), jnp.minimum((i + 1) * pace, units))

                @when(i == jnp.where(extra, min(3, steps - 1), steps - 1))
                def _():
                    blocks.end()
                    blocks.relay()

                @when(i == steps - 1)
                def _():

                    @when((back + 1 < half) & (back + 1 >= 2))
                    def _():
                        for copy in activations(top - (back + 1) // 2, k):
                            copy.start()

        k = t - flow.lag

        @when((k >= 0) & (k < total))
        def _():
            flow.pull((k + steps) % steps)

        return carry

    lax.fori_loop(0, total + steps, step, 0)

    for copy in small:
        copy.wait_send()
    parts = []
    for n, other in enumerate(group.everyone):
        at = pl.multiple_of(other * depth, depth)
        sems = (small_send.at[0, n], small_got.at[0, n])
        parts.append(to(norm_acc.at[:, pl.ds(at, depth)], norm_parts.at[shards - 1 - n], *sems, {"fsdp": other}))
        sems = (small_send.at[1, n], small_got.at[1, n])
        parts.append(to(bias_acc, bias_parts.at[shards - 1 - n], *sems, {"fsdp": other}))
    for copy in parts:
        copy.start()
    own = [
        pltpu.make_async_copy(norm_acc.at[:, mine], norm_parts.at[0], misc.at[0]),
        pltpu.make_async_copy(bias_acc, bias_parts.at[0], misc.at[1]),
    ]
    for copy in own:
        copy.start()
    for copy in own:
        copy.wait()
    for i in range(steps):
        save_grad(i).wait()
        flow.clear(i)
    for layer in range(LAYERS):
        for kind in range(4):
            gather(layer, kind).finish()
    for copy in parts:
        copy.wait_send()
        copy.wait_recv()
    for back in range(half):
        Blocks(back, back % 2).finish()


def lane_stride(extent):
    return -(-extent // PAIR) * PAIR


def plan(tokens):
    return next((s, p) for s, p in ((6, 1), (3, 1), (2, 1)) if tokens % (16 * s * p) == 0)


def train(states, cotangent, own_norms, own_bias, rope, mask, own_q, own_o, own_g, own_d):
    count, shards = lax.axis_size("tensor"), lax.axis_size("fsdp")
    tokens, width = states.shape
    steps, span = plan(tokens)
    big = tokens // steps
    chips = shards // 2
    depth = width // shards
    local, ff = own_q.shape[-1], own_g.shape[-1]
    lanes_attn, lanes_ffn = 4 * lane_stride(local), 3 * lane_stride(ff)
    parts = 3 if chips == 4 else chips
    per_step = -(-2 * chips // max(steps - 2, 1))
    shape = jax.ShapeDtypeStruct
    outs = [
        shape((tokens, width), BF16),
        shape((tokens, width), F32),
        shape((LAYERS, parts, depth, lanes_attn), BF16),
        shape((LAYERS, parts, depth, lanes_ffn), BF16),
        shape((shards, 4 * LAYERS, depth), F32),
        shape((shards, LAYERS, 8, local), F32),
        *[shape((LAYERS, shards) + own.shape[1:], BF16) for own in (own_q, own_o, own_g, own_d)],
        shape((2 * LAYERS, tokens, width), F32),
        shape((2 * LAYERS, tokens, width), BF16),
        shape((2 * LAYERS, tokens, width), BF16),
        shape((LAYERS - 1, 3, tokens, local), BF16),
        shape((LAYERS - 1, tokens, local), BF16),
        shape((LAYERS - 1, 2, tokens, ff), BF16),
        shape((LAYERS - 1, tokens, ff), BF16),
        shape((LAYERS, chips, depth, lanes_attn), BF16),
        shape((LAYERS, chips, depth, lanes_ffn), BF16),
        shape((LAYERS, 2, depth // 2, lanes_attn), BF16),
        shape((LAYERS, 2, depth // 2, lanes_ffn), BF16),
    ]
    dma = pltpu.SemaphoreType.DMA
    vmem = pltpu.VMEM
    scratch = [
        vmem((tokens, width), F32),
        vmem((4, width, local), BF16),
        vmem((3, width, ff), BF16),
        vmem((2, tokens, ff), BF16),
        vmem((tokens, ff), BF16),
        vmem((3, tokens, local), BF16),
        vmem((tokens, local), BF16),
        vmem((tokens, local), F32),
        vmem((tokens, local), F32),
        vmem((big, width), F32),
        vmem((big, width), BF16),
        vmem((LAYERS, steps, local // HEAD_DIM, big), F32),
        vmem((4 * LAYERS, width), F32),
        vmem((8, local), F32),
        vmem((shards, 8, PAIR), F32),
        vmem((4 * LAYERS, width), F32),
        vmem((LAYERS, 8, local), F32),
        vmem((2, 2, tokens, depth), BF16),
        vmem((2, depth, tokens), BF16),
        vmem((2, depth, max(lanes_attn, lanes_ffn)), BF16),
        dma((steps,)),
        dma((1,)),
        dma((2,)),
        dma((steps,)),
        dma((2, 2, steps)),
        dma((2, 2)),
        dma((4,)),
        dma((4, shards)),
        dma((4 * LAYERS, gather_kinds(shards))),
        dma((4 * LAYERS, gather_kinds(shards))),
        dma((2, 2, 2)),
        dma((2, 2)),
        dma((2, 2)),
        *([dma((2 * LAYERS, max(chips, 6)))] * 4),
        dma((2, shards)),
        dma((2, shards)),
        *flow_scratch(steps, span, tokens, width),
    ]
    flops = 6 * LAYERS * tokens * width * (4 * local + 3 * ff)
    return pl.pallas_call(
        functools.partial(train_kernel, count, shards, steps, span, per_step),
        out_shape=outs,
        in_specs=[ANY, ANY, VMEM, VMEM, VMEM, VMEM, ANY, ANY, ANY, ANY],
        out_specs=[ANY] * len(outs),
        scratch_shapes=scratch,
        compiler_params=pltpu.CompilerParams(
            collective_id=1, has_side_effects=True, vmem_limit_bytes=64 * 1024 * 1024
        ),
        cost_estimate=pl.CostEstimate(flops=flops, bytes_accessed=flops // 256, transcendentals=0),
        name="train",
    )(states, cotangent, own_norms, own_bias, rope, mask, own_q, own_o, own_g, own_d)


def finish_kernel(attn, ffn, states, grads, g_qkv, g_out, g_gate_up, g_down, out_states, out_grads):
    local, ff = g_qkv.shape[3], g_gate_up.shape[3]

    def total(parts, at, wide):
        return sum(parts[0, n, :, at : at + wide].astype(F32) for n in range(parts.shape[1]))

    for m in range(3):
        g_qkv[0, m] = total(attn, m * lane_stride(local), local)
    g_out[0] = total(attn, 3 * lane_stride(local), local).T
    for m in range(2):
        g_gate_up[0, :, m, :] = total(ffn, m * lane_stride(ff), ff)
    g_down[0] = total(ffn, 2 * lane_stride(ff), ff).T
    out_states[...] = states[...]
    out_grads[...] = grads[...]


def finish(sums_attn, sums_ffn, states, grads, local, ff):
    parts, depth = sums_attn.shape[1:3]
    tokens, width = states.shape
    rows = min(PAIR, depth)
    cuts = depth // rows
    pieces = tokens // (LAYERS * cuts)
    shape = jax.ShapeDtypeStruct
    spec = pl.BlockSpec
    token_spec = spec((pieces, width), lambda l, r: (l * cuts + r, 0))
    return pl.pallas_call(
        finish_kernel,
        grid=(LAYERS, cuts),
        in_specs=[
            spec((1, parts, rows, sums_attn.shape[3]), lambda l, r: (l, 0, r, 0)),
            spec((1, parts, rows, sums_ffn.shape[3]), lambda l, r: (l, 0, r, 0)),
            token_spec,
            token_spec,
        ],
        out_specs=[
            spec((1, 3, rows, local), lambda l, r: (l, 0, r, 0)),
            spec((1, local, rows), lambda l, r: (l, 0, r)),
            spec((1, rows, 2, ff), lambda l, r: (l, r, 0, 0)),
            spec((1, ff, rows), lambda l, r: (l, 0, r)),
            token_spec,
            token_spec,
        ],
        out_shape=[
            shape((LAYERS, 3, depth, local), F32),
            shape((LAYERS, local, depth), F32),
            shape((LAYERS, depth, 2, ff), F32),
            shape((LAYERS, ff, depth), F32),
            shape((tokens, width), BF16),
            shape((tokens, width), F32),
        ],
        compiler_params=pltpu.CompilerParams(vmem_limit_bytes=48 * 1024 * 1024),
        name="finish",
    )(sums_attn, sums_ffn, states, grads)


def tables(segment_ids, rows):
    places = jnp.arange(rows, dtype=jnp.int32)
    previous = jnp.concatenate([segment_ids[:1] - 1, segment_ids[:-1]])
    starts = lax.cummax(jnp.where(segment_ids != previous, places, jnp.zeros_like(places)), axis=0)
    position = places - starts
    half = ROT_DIM // 2
    inverse = rotary_base ** (-(jnp.arange(half, dtype=F32) * 2.0 / ROT_DIM))
    angle = position.astype(F32)[:, None] * inverse[None, :]
    cosine, sine = jnp.cos(angle), jnp.sin(angle)
    rest = jnp.zeros((rows, HEAD_DIM - ROT_DIM), F32)
    none = jnp.zeros_like(sine)
    rope = jnp.stack(
        [
            jnp.tile(jnp.concatenate([cosine, cosine, rest + 1.0], axis=1), (1, 2)),
            jnp.tile(jnp.concatenate([-sine, none, rest], axis=1), (1, 2)),
            jnp.tile(jnp.concatenate([none, sine, rest], axis=1), (1, 2)),
        ]
    )
    allowed = (segment_ids[:, None] == segment_ids[None, :]) & (places[None, :] <= places[:, None])
    return rope, jnp.where(allowed, 0.0, -1e30)


def on_device(
    states,
    segment_ids,
    ln1_gain,
    ln1_bias,
    qkv_weight,
    qkv_bias,
    out_weight,
    ln2_gain,
    ln2_bias,
    gate_up_weight,
    down_weight,
    cotangent,
):
    tokens = states.shape[0]
    rope, allowed = tables(segment_ids, tokens)
    steps = plan(tokens)[0]
    mask = allowed.reshape(steps, -1, tokens).transpose(0, 2, 1).astype(BF16)
    own_norms = jnp.stack([ln1_gain, ln1_bias, ln2_gain, ln2_bias], axis=1).reshape(4 * LAYERS, -1).astype(F32)
    own_bias = qkv_bias.reshape(LAYERS * 3, -1).astype(F32)
    own_bias = jnp.pad(own_bias, ((0, 8 - own_bias.shape[0]), (0, PAIR - own_bias.shape[1])))
    out_states, grad_states, sums_attn, sums_ffn, norm_parts, bias_parts, *_ = train(
        states,
        cotangent,
        own_norms,
        own_bias,
        rope,
        mask,
        qkv_weight.transpose(0, 2, 1, 3),
        out_weight.transpose(0, 2, 1)[:, None],
        gate_up_weight.transpose(0, 2, 1, 3),
        down_weight.transpose(0, 2, 1)[:, None],
    )
    g_qkv, g_out, g_gate_up, g_down, out_states, grad_states = finish(
        sums_attn, sums_ffn, out_states, grad_states, qkv_weight.shape[3], gate_up_weight.shape[3]
    )
    g_norms = jnp.sum(norm_parts, axis=0).reshape(LAYERS, 4, -1)
    g_bias = jnp.sum(bias_parts, axis=0).reshape(LAYERS, 8, -1, HEAD_DIM)[:, :3]
    share = qkv_bias.shape[3]
    g_bias = lax.dynamic_slice_in_dim(g_bias, lax.axis_index("fsdp") * share, share, axis=3)
    return (
        out_states,
        grad_states,
        g_norms[:, 0],
        g_norms[:, 1],
        g_qkv.transpose(0, 2, 1, 3),
        g_bias,
        g_out,
        g_norms[:, 2],
        g_norms[:, 3],
        g_gate_up,
        g_down,
    )


def solution(mesh):
    in_specs = (
        P("fsdp", None),
        P("fsdp"),
        P(None, "fsdp"),
        P(None, "fsdp"),
        P(None, "fsdp", None, "tensor"),
        P(None, None, "tensor", "fsdp"),
        P(None, "tensor", "fsdp"),
        P(None, "fsdp"),
        P(None, "fsdp"),
        P(None, "fsdp", None, "tensor"),
        P(None, "tensor", "fsdp"),
        P("fsdp", None),
    )
    out_specs = (
        P("fsdp", None),
        P("fsdp", None),
        P(None, "fsdp"),
        P(None, "fsdp"),
        P(None, "fsdp", None, "tensor"),
        P(None, None, "tensor", "fsdp"),
        P(None, "tensor", "fsdp"),
        P(None, "fsdp"),
        P(None, "fsdp"),
        P(None, "fsdp", None, "tensor"),
        P(None, "tensor", "fsdp"),
    )
    return jax.shard_map(
        on_device, mesh=mesh, in_specs=in_specs, out_specs=out_specs, check_vma=False
    )
```

```python
import functools
import math

import jax
import jax.numpy as jnp
from jax import lax
from jax.experimental import pallas as pl
from jax.experimental.pallas import tpu as pltpu
from jax.sharding import PartitionSpec as P

MESH = pl.DeviceIdType.MESH
HEAD_DIM = 64
ROT_DIM = 16
LAYERS = 2
PAIR = 2 * HEAD_DIM
ANY = pl.BlockSpec(memory_space=pl.ANY)
VMEM = pl.BlockSpec(memory_space=pltpu.VMEM)
BF16 = jnp.bfloat16
F32 = jnp.float32

norm_epsilon = 1e-05
rotary_base = 10000.0


def dot(a, b):
    return lax.dot_general(a, b, (((1,), (0,)), ((), ())), preferred_element_type=F32)


def dot_nt(a, b):
    return lax.dot_general(a, b, (((1,), (1,)), ((), ())), preferred_element_type=F32)


def dot_tn(a, b):
    return lax.dot_general(a, b, (((0,), (0,)), ((), ())), preferred_element_type=F32)


def tiles(extent, most=512):
    return [(at, min(most, extent - at)) for at in range(0, extent, most)]


def standardize(values):
    average = jnp.mean(values, axis=-1, keepdims=True)
    centred = values - average
    spread = jnp.mean(centred * centred, axis=-1, keepdims=True)
    rstd = lax.rsqrt(spread + norm_epsilon)
    return centred * rstd, rstd


def turn(values, rope, sign):
    half = ROT_DIM // 2
    factor, below, above = rope
    return values * factor + sign * (
        pltpu.roll(values, PAIR - half, 1) * below + pltpu.roll(values, half, 1) * above
    )


def when(condition):
    return pl.when(condition)


def to(source, target, send, arrive, place):
    return pltpu.make_async_remote_copy(
        src_ref=source, dst_ref=target, send_sem=send, recv_sem=arrive, device_id=place, device_id_type=MESH
    )


def spread(build, source, target, count=4):
    rows = source.shape[-2] // count
    for r in range(count):
        piece = (slice(None),) * (len(source.shape) - 2) + (pl.ds(r * rows, rows), slice(None))
        build(source.at[piece], target.at[piece]).start()


def start(source, target, build):
    spread(build, source, target)


def whole(source, target, build):
    return build(source, target)


class Line:
    def __init__(self, count):
        place = lax.axis_index("tensor")
        half = count // 2
        left = place < half
        self.inner = jnp.where(left, place + 1, place - 1)
        self.outer = jnp.where(left, place - 1, place + 1)
        self.has_outer = (place != 0) & (place != count - 1)
        self.no_outer = jnp.logical_not(self.has_outer)
        self.distance = jnp.where(left, half - 1 - place, place - half)
        self.centre = self.distance == 0
        self.off_centre = jnp.logical_not(self.centre)


class Group:
    def __init__(self, count):
        self.count = count
        self.chips = count // 2
        self.me = lax.axis_index("fsdp")
        self.chip = self.me // 2
        self.core = self.me % 2
        self.peer = self.me + 1 - 2 * self.core
        self.square = self.chips == 4
        self.everyone = [(self.me + i) % count for i in range(1, count)]
        if self.square:
            self.x = self.at(self.chip + 1 - 2 * (self.chip % 2))
            self.y = self.at(self.chip + 2 - 4 * (self.chip // 2))
            self.far = self.at(3 - self.chip)
            self.others = [self.x, self.y]
        else:
            self.others = [self.at((self.chip + i) % self.chips) for i in range(1, self.chips)]

    def at(self, chip):
        return chip * 2 + self.core


def enter(line, partners):
    barrier = pltpu.get_barrier_semaphore()
    for partner in partners:
        pl.semaphore_signal(barrier, inc=1, device_id={"fsdp": partner}, device_id_type=MESH)
    pl.semaphore_signal(barrier, inc=1, device_id={"tensor": line.inner}, device_id_type=MESH)

    @when(line.has_outer)
    def _():
        pl.semaphore_signal(barrier, inc=1, device_id={"tensor": line.outer}, device_id_type=MESH)
        pl.semaphore_wait(barrier, len(partners) + 2)

    @when(line.no_outer)
    def _():
        pl.semaphore_wait(barrier, len(partners) + 1)


class Flow:
    def __init__(self, line, steps, span, rows, refs):
        self.line, self.steps, self.span, self.rows = line, steps, span, rows
        self.from_outer, self.from_inner, self.running = refs[:3]
        self.send_in, self.got_out, self.send_out, self.got_in, self.credit = refs[3:]
        self.lag = jnp.minimum(3 * line.distance + 2, steps - 1)

    def slot(self, i):
        big = self.rows * self.span
        return pl.ds(pl.multiple_of(i * big, big), big)

    def pieces(self, i):
        for r in range(self.span):
            q = i * self.span + r
            yield q, pl.ds(pl.multiple_of(q * self.rows, self.rows), self.rows)

    def inward(self, q, here, target, arrive):
        return to(
            self.running.at[here], target.at[here], self.send_in.at[q], arrive.at[q], {"tensor": self.line.inner}
        )

    def outward(self, q, here):
        return to(
            self.from_inner.at[here], self.from_inner.at[here], self.send_out.at[q], self.got_in.at[q],
            {"tensor": self.line.outer},
        )

    def clear(self, i):
        for q, here in self.pieces(i):
            self.inward(q, here, self.from_inner, self.got_in).wait_send()

    def push(self, i, again):
        line = self.line

        @when(line.centre & again)
        def _():
            pl.semaphore_wait(self.credit, 1)

        for q, here in self.pieces(i):

            @when(line.has_outer)
            def _(q=q, here=here):
                self.inward(q, here, self.from_outer, self.got_out).wait_recv()
                total = self.running[here, :].astype(F32) + self.from_outer[here, :].astype(F32)
                self.running[here, :] = total.astype(BF16)

            @when(line.centre)
            def _(q=q, here=here):
                self.inward(q, here, self.from_inner, self.got_in).start()

            @when(line.off_centre)
            def _(q=q, here=here):
                self.inward(q, here, self.from_outer, self.got_out).start()

    def pull(self, i):
        line = self.line
        for q, here in self.pieces(i):
            self.inward(q, here, self.from_inner, self.got_in).wait_recv()

            @when(line.centre)
            def _(q=q, here=here):
                total = self.running[here, :].astype(F32) + self.from_inner[here, :].astype(F32)
                self.from_inner[here, :] = total.astype(BF16)

            @when(line.has_outer)
            def _(q=q, here=here):
                self.outward(q, here).start()

    def release(self, i, more):
        line = self.line

        @when(line.has_outer)
        def _():
            for q, here in self.pieces(i):
                self.outward(q, here).wait_send()

        @when(line.centre & more)
        def _():
            pl.semaphore_signal(self.credit, inc=1, device_id={"tensor": line.inner}, device_id_type=MESH)


def flow_scratch(steps, span, tokens, width):
    whole = pltpu.VMEM((tokens, width), BF16)
    sems = pltpu.SemaphoreType.DMA((steps * span,))
    return [whole, whole, whole, sems, sems, sems, sems, pltpu.SemaphoreType.REGULAR]


def gather_kinds(count):
    return 9 if count == 8 else count


class Gather:
    def __init__(self, group, own, whole, send, arrive, load):
        self.group, self.own, self.whole, self.send, self.arrive, self.load_sems = group, own, whole, send, arrive, load
        self.half = own.shape[1] // 2
        self.links = len(group.others)

    def half_at(self, shard, h):
        return self.whole.at[shard, :, pl.ds(h * self.half, self.half), :]

    def way(self, kind):
        g, links = self.group, self.links
        if kind < links:
            return self.own, self.whole.at[g.me], g.others[kind]
        if kind == links:
            return self.own, self.whole.at[g.me], g.peer
        if kind <= 2 * links:
            shard = self.whole.at[g.others[kind - links - 1]]
            return shard, shard, g.peer
        if kind == 2 * links + 1:
            return self.half_at(g.x, 0), self.half_at(g.x, 0), g.y
        if kind == 2 * links + 2:
            return self.half_at(g.y, 1), self.half_at(g.y, 1), g.x
        return self.whole.at[g.far], self.whole.at[g.far], g.peer

    def build(self, kind, source, target):
        return to(source, target, self.send.at[kind], self.arrive.at[kind], {"fsdp": self.way(kind)[2]})

    def copy(self, kind):
        return self.build(kind, *self.way(kind)[:2])

    def start(self, kind):
        spread(functools.partial(self.build, kind), *self.way(kind)[:2])

    def local(self):
        return pltpu.make_async_copy(self.own, self.whole.at[self.group.me], self.send.at[gather_kinds(self.group.count) - 1])

    def begin(self):
        for kind in range(self.links + 1):
            self.start(kind)
        self.local().start()

    def relay(self):
        for kind in range(self.links):
            self.copy(kind).wait_recv()
        if self.group.square:
            self.start(2 * self.links + 1)
            self.start(2 * self.links + 2)
        for kind in range(self.links):
            self.start(self.links + 1 + kind)

    def relay_far(self):
        if self.group.square:
            self.copy(2 * self.links + 1).wait_recv()
            self.copy(2 * self.links + 2).wait_recv()
            self.start(2 * self.links + 3)

    def settle(self):
        self.local().wait()
        for kind in range(self.links, 2 * self.links + 1):
            self.copy(kind).wait_recv()
        if self.group.square:
            self.copy(2 * self.links + 3).wait_recv()

    def loads(self, target):
        depth = self.own.shape[1]
        for k in range(self.group.count):
            yield pltpu.make_async_copy(
                self.whole.at[k], target.at[:, pl.ds(k * depth, depth), :], self.load_sems.at[k]
            )

    def finish(self):
        for kind in range(2 * self.links + 1 + (3 if self.group.square else 0)):
            self.copy(kind).wait_send()


def train_kernel(
    count, shards, steps, span, per_step,
    states, cotangent, own_norms, own_bias, rope, mask, own_q, own_o, own_g, own_d,
    out_states, grad_states, sums_attn, sums_ffn, norm_parts, bias_parts,
    whole_q, whole_o, whole_g, whole_d, s_x, s_n, s_y, s_qkv, s_att, s_gu, s_hid,
    mate_attn, mate_ffn, via_attn, via_ffn,
    res, w_attn, w_ffn, gu, hid, qkv, att, d_key, d_value, x_in, low,
    log_total, norms, biases, bias_in, norm_acc, bias_acc, columns, turned, staged,
    x_save, x_sem, low_sem, out_sem, keep_sem, act_sem, misc, load_sem, g_send, g_arrive,
    column_sem, stage_sem, relay_sem, mate_send, mate_got, own_send, own_got, small_send, small_got,
    *flow_refs,
):
    tokens, width = res.shape
    big = tokens // steps
    local, ff = w_attn.shape[2], w_ffn.shape[2]
    depth = width // shards
    line = Line(count)
    group = Group(shards)
    chips = group.chips
    flow = Flow(line, steps, span, big // span, flow_refs)
    scale = jnp.asarray(1.0 / math.sqrt(HEAD_DIM), BF16)
    half = 2 * LAYERS
    stages = 2 * half
    total = stages * steps
    top = LAYERS - 1
    units = 2 * chips

    def block(c):
        return pl.ds(pl.multiple_of(c * big, big), big)

    kinds = [(own_q, whole_q), (own_o, whole_o), (own_g, whole_g), (own_d, whole_d)]
    targets = [w_attn.at[0:3], w_attn.at[3:4], w_ffn.at[0:2], w_ffn.at[2:3]]

    def gather(layer, kind):
        n = 4 * layer + kind
        own, whole = kinds[kind]
        return Gather(group, own.at[layer], whole.at[layer], g_send.at[n], g_arrive.at[n], load_sem.at[kind])

    def load(layer, kind, wait):
        own, whole = kinds[kind]
        way = Gather(group, own.at[0], whole.at[layer], g_send.at[0], g_arrive.at[0], load_sem.at[kind])
        for copy in way.loads(targets[kind]):
            if wait:
                copy.wait()
            else:
                copy.start()

    events = {}

    def event(t, where, *actions):
        events.setdefault((t, where, None), []).extend(actions)

    def event_by_role(centre, others, *actions):
        events.setdefault(centre + (True,), []).extend(actions)
        events.setdefault(others + (False,), []).extend(actions)

    def loading(layer, kind, wait):
        return functools.partial(load, layer, kind, wait)

    def at(stage, i):
        return stage * steps + min(i, steps - 1)

    q, o, g, d = 0, 1, 2, 3
    event(0, 1, gather(0, o).relay_far, gather(0, o).settle, loading(0, o, False), loading(0, o, True))
    event_by_role((at(0, 3), 0), (at(0, 4), 0), gather(0, g).relay)
    event_by_role((at(0, 5), 0), (at(0, 5), 2), gather(0, g).relay_far, gather(0, d).begin)
    event(at(1, 0), 0, gather(0, g).settle, loading(0, g, False), loading(0, g, True))
    event(at(1, 0), 1, gather(0, d).relay)
    for layer in range(1, LAYERS):
        s = 2 * layer - 1
        event(at(s, 0), 1, gather(layer, q).begin)
        if layer == 1:
            event(at(s, 0), 1, gather(0, d).relay_far, gather(0, d).settle, loading(0, d, False), loading(0, d, True))
        event(at(s, 2), 0, gather(layer, q).relay, gather(layer, o).begin)
        event_by_role((at(s, 3), 0), (at(s, 3), 2), gather(layer, q).relay_far, gather(layer, o).relay, gather(layer, g).begin)
        event(at(s, 4), 2, gather(layer, o).relay_far)
        event(at(s, 5), 2, gather(layer, q).settle, loading(layer, q, False))
        event(at(s, 5), 2, gather(layer, o).settle, loading(layer, o, False))
        s += 1
        event(at(s, 0), 0, loading(layer, q, True), loading(layer, o, True))
        event_by_role((at(s, 0), 0), (at(s, 0), 2), gather(layer, g).relay)
        event_by_role((at(s, 2), 0), (at(s, 2), 2), gather(layer, g).relay_far, gather(layer, d).begin)
        event(at(s, 3), 2, gather(layer, g).settle, loading(layer, g, False))
        event_by_role((at(s, 4), 0), (at(s, 4), 2), gather(layer, d).relay)
        event(at(s, 5), 2, gather(layer, d).relay_far)
        s += 1
        event(at(s, 0), 0, loading(layer, g, True), gather(layer, d).settle, loading(layer, d, False))
        event(at(s, 0), 1, loading(layer, d, True))

    def run_events(t, where):
        ordered = sorted(events.items(), key=lambda item: item[0][:2])
        ordered = [(at, role, actions) for (at, place, role), actions in ordered if place == where]
        for stage in sorted({at // steps for at, _, _ in ordered}):

            @when(t // steps == stage)
            def _(stage=stage):
                for at, role, actions in ordered:
                    if at // steps != stage:
                        continue
                    condition = t == at
                    if role is not None:
                        condition = condition & (line.centre if role else line.off_centre)

                    @when(condition)
                    def _(actions=actions):
                        for action in actions:
                            action()

    enter(line, group.everyone)
    mine = pl.ds(pl.multiple_of(group.me * depth, depth), depth)
    small = []
    for n, other in enumerate(group.everyone):
        sems = (small_send.at[0, n], small_got.at[0, n])
        small.append(to(own_norms, norms.at[:, mine], *sems, {"fsdp": other}))
        sems = (small_send.at[1, n], small_got.at[1, n])
        small.append(to(own_bias, bias_in.at[group.me], *sems, {"fsdp": other}))
    gather(0, q).begin()
    for copy in small:
        copy.start()
    starts = [
        pltpu.make_async_copy(own_norms, norms.at[:, mine], misc.at[0]),
        pltpu.make_async_copy(own_bias, bias_in.at[group.me], misc.at[1]),
        pltpu.make_async_copy(states, flow.running, misc.at[2]),
        pltpu.make_async_copy(cotangent, s_y.at[0], misc.at[3]),
    ]
    for copy in starts:
        copy.start()
    qkv[...] = jnp.zeros_like(qkv)
    norm_acc[...] = jnp.zeros_like(norm_acc)
    bias_acc[...] = jnp.zeros_like(bias_acc)
    for copy in starts:
        copy.wait()
    for c in range(steps):
        res[c * big : (c + 1) * big, :] = flow.running[c * big : (c + 1) * big, :].astype(F32)
    for copy in small:
        copy.wait_recv()
    each = HEAD_DIM // shards
    source = lax.broadcasted_iota(jnp.int32, (PAIR, local), 0)
    column = lax.broadcasted_iota(jnp.int32, (PAIR, local), 1)
    at_head = lax.div(source, each) == lax.div(column, HEAD_DIM)
    whole_bias = jnp.zeros((8, local), F32)
    for k in range(shards):
        match = at_head & (lax.rem(column, HEAD_DIM) == k * each + lax.rem(source, each))
        whole_bias += dot(bias_in[k].astype(BF16), jnp.where(match, 1.0, 0.0).astype(BF16))
    biases[...] = whole_bias
    gather(0, q).relay()
    gather(0, o).begin()
    gather(0, q).relay_far()
    gather(0, o).relay()
    gather(0, g).begin()
    gather(0, q).settle()
    load(0, q, False)
    load(0, q, True)

    lanes = lax.broadcasted_iota(jnp.int32, (big, PAIR), 1)
    first_head = lanes < HEAD_DIM

    def save_x(stage, c):
        return pltpu.make_async_copy(res.at[block(c)], s_x.at[stage, block(c)], x_save.at[c])

    def keeps(layer, kind, c):
        here = block(c)
        if kind == 0:
            pairs = [(gu.at[:, here], s_gu.at[layer, :, here]), (hid.at[here], s_hid.at[layer, here])]
        else:
            pairs = [(qkv.at[:, here], s_qkv.at[layer, :, here]), (att.at[here], s_att.at[layer, here])]
        return [pltpu.make_async_copy(a, b, keep_sem.at[kind, n, c]) for n, (a, b) in enumerate(pairs)]

    def activations(layer, kind):
        if kind == 0:
            pairs = [(s_gu.at[layer], gu), (s_hid.at[layer], hid)]
        else:
            pairs = [(s_qkv.at[layer], qkv), (s_att.at[layer], att)]
        return [pltpu.make_async_copy(a, b, act_sem.at[kind, n]) for n, (a, b) in enumerate(pairs)]

    def project(*pairs):
        def write(i):
            here = flow.slot(i)
            for at, wide in tiles(width, 1024):
                part = sum(dot_nt(right[at : at + wide, :], left()) for left, right in pairs)
                flow.running[here, at : at + wide] = part.T.astype(BF16)

        return write

    def by_extent(c, work):
        early = steps // 2

        @when(c < early)
        def _():
            work(early * big)

        @when(c >= early)
        def _():
            work(tokens)

    def normed_rows(stage, c):
        here = block(c)

        @when(stage > 0)
        def _():
            save_x(stage, c).wait()
            res[here, :] += flow.from_inner[flow.slot(c), :].astype(F32)

        save_x(stage, c).start()
        xhat, _ = standardize(res[here, :])
        low[...] = (xhat * norms[pl.ds(2 * stage, 1), :] + norms[pl.ds(2 * stage + 1, 1), :]).astype(BF16)
        pltpu.make_async_copy(low, s_n.at[stage, here], low_sem.at[0]).start()

    def attention_forward(t, layer, c):
        here = block(c)

        @when(layer > 0)
        def _():
            for copy in keeps(layer - 1, 1, c):
                copy.wait()

        for part in range(3):
            for at, wide in tiles(local):
                mixed = dot(low[...], w_attn[part, :, at : at + wide])
                for pair in range(wide // PAIR):
                    to_lane = at + pair * PAIR
                    span_here = slice(to_lane, to_lane + PAIR)
                    value = mixed[:, pair * PAIR : (pair + 1) * PAIR]
                    value = value + biases[pl.ds(3 * layer + part, 1), :][:, span_here]
                    if part < 2:
                        value = turn(value, [rope[n, here, :] for n in range(3)], 1.0)
                    qkv[part, here, span_here] = value.astype(BF16)
        def attend(keys):
            closed = mask[c, 0:keys].astype(F32)
            for pair in range(local // PAIR):
                lane = slice(pair * PAIR, (pair + 1) * PAIR)
                query, key, value = qkv[0, here, lane] * scale, qkv[1, 0:keys, lane], qkv[2, 0:keys, lane]
                outs = []
                for head in range(2):
                    own = first_head if head == 0 else jnp.logical_not(first_head)
                    scores = dot_nt(key, jnp.where(own, query, jnp.zeros_like(query))) + closed
                    most = jnp.max(scores, axis=0, keepdims=True)
                    exps = jnp.exp(scores - most)
                    total_exp = jnp.sum(exps, axis=0, keepdims=True)
                    log_total[layer, c, 2 * pair + head : 2 * pair + head + 1, :] = most + jnp.log(total_exp)
                    probs = exps * (1.0 / total_exp)
                    outs.append(dot_tn(probs.astype(BF16), value))
                att[here, lane] = jnp.where(first_head, outs[0], outs[1]).astype(BF16)

        by_extent(c, attend)

        @when(layer < top)
        def _():
            for copy in keeps(layer, 1, c):
                copy.start()

        run_events(t, 1)
        project((lambda: att[here, :], w_attn.at[3]))(c)

    def ffn_forward(t, layer, c):
        here = block(c)

        @when(layer > 0)
        def _():
            for copy in keeps(layer - 1, 0, c):
                copy.wait()

        for at, wide in tiles(ff):
            gate = dot(low[...], w_ffn[0, :, at : at + wide])
            up = dot(low[...], w_ffn[1, :, at : at + wide])
            gu[0, here, at : at + wide] = gate.astype(BF16)
            gu[1, here, at : at + wide] = up.astype(BF16)
            hid[here, at : at + wide] = (gate * jax.nn.sigmoid(gate) * up).astype(BF16)

        @when(layer < top)
        def _():
            for copy in keeps(layer, 0, c):
                copy.start()

        run_events(t, 1)
        project((lambda: hid[here, :], w_ffn.at[2]))(c)

    def fetch_x(back, c):
        return pltpu.make_async_copy(s_x.at[half - back, block(c)], x_in, x_sem.at[0])

    def fetch_low(c):
        return pltpu.make_async_copy(s_y.at[0, block(c)], low, low_sem.at[1])

    def save_low(back, c):
        return pltpu.make_async_copy(low, s_y.at[back, block(c)], low_sem.at[0])

    def take(back, i, c):
        here = block(c)
        row = 2 * (half - back)
        fetch_x(back, c).wait()

        @when(back == 1)
        def _():
            fetch_low(c).wait()
            res[here, :] = low[...].astype(F32)

        xhat, rstd = standardize(x_in[...])
        e = flow.from_inner[flow.slot(i), :].astype(F32)
        scaled = e * norms[pl.ds(row, 1), :]
        inner = jnp.mean(scaled * xhat, axis=-1, keepdims=True)
        res[here, :] += rstd * (scaled - jnp.mean(scaled, axis=-1, keepdims=True) - xhat * inner)
        norm_acc[pl.ds(row, 1), :] += jnp.sum(e * xhat, axis=0, keepdims=True)
        norm_acc[pl.ds(row + 1, 1), :] += jnp.sum(e, axis=0, keepdims=True)

    def ffn_backward(i, c):
        here = block(c)
        for at, wide in tiles(ff):
            lane = slice(at, at + wide)
            d_hidden = dot(low[...], w_ffn[2, :, lane])
            gate, up = gu[0, here, lane].astype(F32), gu[1, here, lane].astype(F32)
            sigma = jax.nn.sigmoid(gate)
            gu[0, here, lane] = (d_hidden * up * sigma * (1.0 + gate * (1.0 - sigma))).astype(BF16)
            gu[1, here, lane] = (d_hidden * gate * sigma).astype(BF16)
        project((lambda: gu[0, here, :], w_ffn.at[0]), (lambda: gu[1, here, :], w_ffn.at[1]))(i)

    def attention_backward(layer, i, c):
        here = block(c)
        def attend_back(keys):
            closed = mask[c, 0:keys].astype(F32)
            turns = [rope[n, here, :] for n in range(3)]
            for pair in range(local // PAIR):
                lane = slice(pair * PAIR, (pair + 1) * PAIR)
                d_att = dot(low[...], w_attn[3, :, lane]).astype(BF16)
                query, key, value = qkv[0, here, lane], qkv[1, 0:keys, lane], qkv[2, 0:keys, lane]
                d_query, key_parts, value_parts = [], [], []
                for head in range(2):
                    own = first_head if head == 0 else jnp.logical_not(first_head)
                    own_query = jnp.where(own, query, jnp.zeros_like(query)) * scale
                    own_d_att = jnp.where(own, d_att, jnp.zeros_like(d_att))
                    scores = dot_nt(key, own_query) + closed
                    probs = jnp.exp(scores - log_total[layer, c, 2 * pair + head : 2 * pair + head + 1, :])
                    d_probs = dot_nt(value, own_d_att)
                    d_scores = probs * (d_probs - jnp.sum(probs * d_probs, axis=0, keepdims=True))
                    d_scores = d_scores.astype(BF16)
                    key_parts.append(dot(d_scores, own_query))
                    value_parts.append(dot(probs.astype(BF16), own_d_att))
                    d_query.append(dot_tn(d_scores, key))
                d_key[0:keys, lane] += key_parts[0] + key_parts[1]
                d_value[0:keys, lane] += value_parts[0] + value_parts[1]
                parts = [
                    turn(jnp.where(first_head, d_query[0], d_query[1]) / math.sqrt(HEAD_DIM), turns, -1.0),
                    turn(d_key[here, lane], turns, -1.0),
                    d_value[here, lane],
                ]
                for part, values in enumerate(parts):
                    values = values.astype(BF16)
                    qkv[part, here, lane] = values
                    bias_acc[layer, part : part + 1, lane] += jnp.sum(values.astype(F32), axis=0, keepdims=True)

        by_extent(c, attend_back)
        project(
            (lambda: qkv[0, here, :], w_attn.at[0]),
            (lambda: qkv[1, here, :], w_attn.at[1]),
            (lambda: qkv[2, here, :], w_attn.at[2]),
        )(i)

    class Blocks:
        def __init__(self, back, kind):
            self.back_stage, self.kind = back, kind
            layer = top - back // 2
            self.sums = (sums_ffn if kind == 0 else sums_attn).at[layer]
            self.mate = (mate_ffn if kind == 0 else mate_attn).at[layer]
            self.via = (via_ffn if kind == 0 else via_attn).at[layer]
            self.home = 0 if group.square else group.chip
            self.stride = lane_stride(ff if kind == 0 else local)
            self.held = staged.at[:, :, 0 : (4 - (kind == 0)) * self.stride]
            self.x = s_n.at[2 * layer + 1 - kind]
            self.y = s_y.at[back]
            if kind == 0:
                self.right = [(0, gu.at[0]), (0, gu.at[1]), (1, hid)]
            else:
                self.right = [(0, qkv.at[0]), (0, qkv.at[1]), (0, qkv.at[2]), (1, att)]

        def chip(self, u):
            if not group.square:
                return (group.chip + 1 + u) % chips
            x, y, far = group.x // 2, group.y // 2, group.far // 2
            k = u % 4
            return jnp.where(k == 0, far, jnp.where(k == 1, x, jnp.where(k == 2, y, group.chip)))

        def fetch(self, u):
            core = jnp.where(u < chips, 1 - group.core, group.core)
            at = pl.multiple_of((self.chip(u) * 2 + core) * depth, depth)
            return [
                pltpu.make_async_copy(
                    source.at[:, pl.ds(at, depth)], columns.at[u % 2, n], column_sem.at[self.kind, u % 2, n]
                )
                for n, source in enumerate((self.x, self.y))
            ]

        def over(self, u):
            j = self.chip(u)
            sems = (mate_send.at[self.back_stage, j], mate_got.at[self.back_stage, j])
            return self.held.at[u % 2], self.mate.at[j], lambda a, b: to(a, b, *sems, {"fsdp": group.peer})

        def near(self, source, target, u):
            return source, target, lambda a, b: pltpu.make_async_copy(a, b, stage_sem.at[self.kind, u % 2])

        def bring(self, u):
            return self.near(self.mate.at[self.chip(u)], self.held.at[u % 2], u)

        def back(self, u):
            return self.near(self.held.at[u % 2], self.mate.at[self.chip(u)], u)

        def keep(self, u):
            return self.near(self.held.at[u % 2], self.sums.at[self.home], u)

        def push(self, u):
            j = self.chip(u)
            sems = (own_send.at[self.back_stage, j], own_got.at[self.back_stage, group.chip])
            return self.mate.at[j], self.sums.at[group.chip], lambda a, b: to(a, b, *sems, {"fsdp": group.at(j)})

        def hop(self, kind):
            over_x = kind % 2 == 0
            first = over_x if kind < 4 else not over_x
            rows = pl.ds(0 if first else depth // 2, depth // 2)
            target = group.x if over_x else group.y
            sems = (own_send.at[self.back_stage, kind], own_got.at[self.back_stage, kind])
            build = lambda a, b: to(a, b, *sems, {"fsdp": target})
            if kind < 2:
                return self.mate.at[group.far // 2, rows], self.via.at[kind], build
            place = self.sums.at[1 if over_x else 2, rows]
            if kind < 4:
                return self.mate.at[target // 2, rows], place, build
            return self.via.at[1 if over_x else 0], place, build

        def send_on(self, u):
            whole(*self.back(u)).wait()
            if not group.square:
                start(*self.push(u))
                return
            for k, hops in enumerate(((0, 1), (2,), (3,))):

                @when(u % 4 == k)
                def _(hops=hops):
                    for kind in hops:
                        start(*self.hop(kind))

        def relay(self):
            if not group.square:
                return
            rest = depth // 2
            steps_in = []
            for n, (kind, target, rows) in enumerate(
                ((1, group.x, pl.ds(rest, rest)), (0, group.y, pl.ds(0, rest)))
            ):
                whole(*self.hop(kind)).wait_recv()
                pair = [
                    pltpu.make_async_copy(self.mate.at[target // 2, rows], self.held.at[n, pl.ds(0, rest)], relay_sem.at[n, 0]),
                    pltpu.make_async_copy(self.via.at[kind], self.held.at[n, pl.ds(rest, rest)], relay_sem.at[n, 1]),
                ]
                for copy in pair:
                    copy.start()
                steps_in.append((kind, pair))
            returns = []
            lanes_here = (4 - (self.kind == 0)) * self.stride
            for n, (kind, pair) in enumerate(steps_in):
                for copy in pair:
                    copy.wait()
                for at, wide in tiles(lanes_here, 512):
                    lane = slice(at, at + wide)
                    both = staged[n, 0:rest, lane].astype(F32) + staged[n, rest:depth, lane].astype(F32)
                    staged[n, 0:rest, lane] = both.astype(BF16)
                copy = pltpu.make_async_copy(self.held.at[n, pl.ds(0, rest)], self.via.at[kind], relay_sem.at[n, 0])
                copy.start()
                returns.append(copy)
            for copy, kind in zip(returns, (4, 5)):
                copy.wait()
                start(*self.hop(kind))

        def unit(self, u):
            slot = u % 2
            own = u >= chips

            @when(u + 1 < units)
            def _():
                for copy in self.fetch(u + 1):
                    copy.start()

            @when((u >= 2) & (u < chips + 2))
            def _():
                whole(*self.over(u - 2)).wait_send()

            @when(u > chips)
            def _():
                self.send_on(u - 1)

            @when(own)
            def _():
                whole(*self.over(u - chips)).wait_recv()
                start(*self.bring(u))

            for copy in self.fetch(u):
                copy.wait()
            for left in range(2):
                turned[left] = columns[slot, left].T

            @when(own)
            def _():
                whole(*self.bring(u)).wait()

            def form(add):
                for m, (left, right) in enumerate(self.right):
                    for at, wide in tiles(right.shape[1]):
                        product = dot(turned[left], right[:, at : at + wide])
                        lane = slice(m * self.stride + at, m * self.stride + at + wide)
                        if add:
                            product = product + staged[slot, :, lane].astype(F32)
                        staged[slot, :, lane] = product.astype(BF16)

            @when(own)
            def _():
                form(True)

            @when(jnp.logical_not(own))
            def _():
                form(False)

            @when(jnp.logical_not(own))
            def _():
                start(*self.over(u))

            @when(own & (u < units - 1))
            def _():
                start(*self.back(u))

            @when(u == units - 1)
            def _():
                start(*self.keep(u))

        def begin(self):
            for copy in self.fetch(0):
                copy.start()

        def run(self, first, last):
            def one(u, carry):
                self.unit(u)
                return carry

            lax.fori_loop(first, last, one, 0)

        def end(self):
            whole(*self.keep(units - 1)).wait()

        def finish(self):
            if group.square:
                for kind in range(6):
                    whole(*self.hop(kind)).wait_send()
                    if kind >= 2:
                        whole(*self.hop(kind)).wait_recv()
                return
            for j in range(chips):

                @when(j != group.chip)
                def _(j=j):
                    sems = (own_send.at[self.back_stage, j], own_got.at[self.back_stage, j])
                    copy = to(self.mate.at[j], self.sums.at[j], *sems, {"fsdp": group.at(j)})
                    copy.wait_send()
                    copy.wait_recv()

    def save_out(c):
        return pltpu.make_async_copy(flow.running.at[flow.slot(c)], out_states.at[block(c)], out_sem.at[c])

    def save_grad(c):
        return pltpu.make_async_copy(res.at[block(c)], grad_states.at[block(c)], out_sem.at[c])

    def step(t, carry):
        i = t % steps
        stage = t // steps
        back = stage - half
        c = jnp.where(back < 0, i, steps - 1 - i)
        run_events(t, 0)

        @when((t >= steps) & (back < 0))
        def _():
            normed_rows(stage, c)
            flow.release(i, True)

        @when(t < steps)
        def _():
            normed_rows(stage, c)

        @when(back == 0)
        def _():
            save_x(half - 1, i).wait()

        @when((i == 0) & (back >= 1) & (back < half))
        def _():
            for k in range(2):

                @when(back % 2 == k)
                def _(k=k):
                    layer = top - back // 2

                    @when(back >= 2)
                    def _():
                        for kind in (2, 3) if k == 0 else (0, 1):
                            load(layer, kind, True)
                        for copy in activations(layer, k):
                            copy.wait()

                    @when(back + 1 < half)
                    def _():
                        for kind in (0, 1) if k == 0 else (2, 3):
                            load(layer - k, kind, False)

                    if k == 1:
                        d_key[...] = jnp.zeros_like(d_key)
                        d_value[...] = jnp.zeros_like(d_value)

        for k in range(2):

            @when((i == 0) & (back >= 1) & (back % 2 != k))
            def _(k=k):
                Blocks(back - 1, k).begin()

        @when(back >= 1)
        def _():
            take(back, i, c)
            flow.release(i, t < total)

        @when((t >= total - half * steps + steps - 1) & (t < total + steps - 1))
        def _():
            after = t + 1
            fetch_x(after // steps - half, steps - 1 - after % steps).start()

        @when((back >= 1) & (back < half))
        def _():
            low[...] = res[block(c), :].astype(BF16)
            save_low(back, c).start()

        @when(back == half)
        def _():
            save_grad(c).start()

        @when((t >= steps) & (t < total))
        def _():
            flow.clear(i)

        @when(back == 0)
        def _():
            out = res[block(i), :] + flow.from_inner[flow.slot(i), :].astype(F32)
            flow.release(i, True)
            flow.running[flow.slot(i), :] = out.astype(BF16)
            save_out(i).start()
            fetch_low(c).wait()
            save_out(i).wait()

        @when((back < 0) & (stage % 2 == 0))
        def _():
            attention_forward(t, stage // 2, c)

        @when((back < 0) & (stage % 2 == 1))
        def _():
            ffn_forward(t, stage // 2, c)

        @when((back >= 0) & (back < half) & (back % 2 == 0))
        def _():
            ffn_backward(i, c)

        @when((back >= 0) & (back < half) & (back % 2 == 1))
        def _():
            attention_backward(top - back // 2, i, c)

        @when(t < total)
        def _():
            flow.push(i, t >= steps)

        run_events(t, 2)

        @when((t < total) & (back != 0))
        def _():
            save_low(0, c).wait()

        after = t + 1
        @when((after >= half * steps) & (after < (half + 2) * steps))
        def _():
            fetch_low(steps - 1 - after % steps).start()

        for k in range(2):

            @when((back >= 1) & (back % 2 != k))
            def _(k=k):
                blocks = Blocks(back - 1, k)
                extra = back == half
                pace = jnp.where(extra, 2 * per_step, per_step)
                blocks.run(jnp.minimum(i * pace, units), jnp.minimum((i + 1) * pace, units))

                @when(i == jnp.where(extra, min(3, steps - 1), steps - 1))
                def _():
                    blocks.end()
                    blocks.relay()

                @when(i == steps - 1)
                def _():

                    @when((back + 1 < half) & (back + 1 >= 2))
                    def _():
                        for copy in activations(top - (back + 1) // 2, k):
                            copy.start()

        k = t - flow.lag

        @when((k >= 0) & (k < total))
        def _():
            flow.pull((k + steps) % steps)

        return carry

    lax.fori_loop(0, total + steps, step, 0)

    for copy in small:
        copy.wait_send()
    parts = []
    for n, other in enumerate(group.everyone):
        at = pl.multiple_of(other * depth, depth)
        sems = (small_send.at[0, n], small_got.at[0, n])
        parts.append(to(norm_acc.at[:, pl.ds(at, depth)], norm_parts.at[shards - 1 - n], *sems, {"fsdp": other}))
        sems = (small_send.at[1, n], small_got.at[1, n])
        parts.append(to(bias_acc, bias_parts.at[shards - 1 - n], *sems, {"fsdp": other}))
    for copy in parts:
        copy.start()
    own = [
        pltpu.make_async_copy(norm_acc.at[:, mine], norm_parts.at[0], misc.at[0]),
        pltpu.make_async_copy(bias_acc, bias_parts.at[0], misc.at[1]),
    ]
    for copy in own:
        copy.start()
    for copy in own:
        copy.wait()
    for i in range(steps):
        save_grad(i).wait()
        flow.clear(i)
    for layer in range(LAYERS):
        for kind in range(4):
            gather(layer, kind).finish()
    for copy in parts:
        copy.wait_send()
        copy.wait_recv()
    for back in range(half):
        Blocks(back, back % 2).finish()


def lane_stride(extent):
    return -(-extent // PAIR) * PAIR


def plan(tokens):
    return next((s, p) for s, p in ((6, 1), (3, 1), (2, 1)) if tokens % (16 * s * p) == 0)


def train(states, cotangent, own_norms, own_bias, rope, mask, own_q, own_o, own_g, own_d):
    count, shards = lax.axis_size("tensor"), lax.axis_size("fsdp")
    tokens, width = states.shape
    steps, span = plan(tokens)
    big = tokens // steps
    chips = shards // 2
    depth = width // shards
    local, ff = own_q.shape[-1], own_g.shape[-1]
    lanes_attn, lanes_ffn = 4 * lane_stride(local), 3 * lane_stride(ff)
    parts = 3 if chips == 4 else chips
    per_step = -(-2 * chips // max(steps - 2, 1))
    shape = jax.ShapeDtypeStruct
    outs = [
        shape((tokens, width), BF16),
        shape((tokens, width), F32),
        shape((LAYERS, parts, depth, lanes_attn), BF16),
        shape((LAYERS, parts, depth, lanes_ffn), BF16),
        shape((shards, 4 * LAYERS, depth), F32),
        shape((shards, LAYERS, 8, local), F32),
        *[shape((LAYERS, shards) + own.shape[1:], BF16) for own in (own_q, own_o, own_g, own_d)],
        shape((2 * LAYERS, tokens, width), F32),
        shape((2 * LAYERS, tokens, width), BF16),
        shape((2 * LAYERS, tokens, width), BF16),
        shape((LAYERS - 1, 3, tokens, local), BF16),
        shape((LAYERS - 1, tokens, local), BF16),
        shape((LAYERS - 1, 2, tokens, ff), BF16),
        shape((LAYERS - 1, tokens, ff), BF16),
        shape((LAYERS, chips, depth, lanes_attn), BF16),
        shape((LAYERS, chips, depth, lanes_ffn), BF16),
        shape((LAYERS, 2, depth // 2, lanes_attn), BF16),
        shape((LAYERS, 2, depth // 2, lanes_ffn), BF16),
    ]
    dma = pltpu.SemaphoreType.DMA
    vmem = pltpu.VMEM
    scratch = [
        vmem((tokens, width), F32),
        vmem((4, width, local), BF16),
        vmem((3, width, ff), BF16),
        vmem((2, tokens, ff), BF16),
        vmem((tokens, ff), BF16),
        vmem((3, tokens, local), BF16),
        vmem((tokens, local), BF16),
        vmem((tokens, local), F32),
        vmem((tokens, local), F32),
        vmem((big, width), F32),
        vmem((big, width), BF16),
        vmem((LAYERS, steps, local // HEAD_DIM, big), F32),
        vmem((4 * LAYERS, width), F32),
        vmem((8, local), F32),
        vmem((shards, 8, PAIR), F32),
        vmem((4 * LAYERS, width), F32),
        vmem((LAYERS, 8, local), F32),
        vmem((2, 2, tokens, depth), BF16),
        vmem((2, depth, tokens), BF16),
        vmem((2, depth, max(lanes_attn, lanes_ffn)), BF16),
        dma((steps,)),
        dma((1,)),
        dma((2,)),
        dma((steps,)),
        dma((2, 2, steps)),
        dma((2, 2)),
        dma((4,)),
        dma((4, shards)),
        dma((4 * LAYERS, gather_kinds(shards))),
        dma((4 * LAYERS, gather_kinds(shards))),
        dma((2, 2, 2)),
        dma((2, 2)),
        dma((2, 2)),
        *([dma((2 * LAYERS, max(chips, 6)))] * 4),
        dma((2, shards)),
        dma((2, shards)),
        *flow_scratch(steps, span, tokens, width),
    ]
    flops = 6 * LAYERS * tokens * width * (4 * local + 3 * ff)
    return pl.pallas_call(
        functools.partial(train_kernel, count, shards, steps, span, per_step),
        out_shape=outs,
        in_specs=[ANY, ANY, VMEM, VMEM, VMEM, VMEM, ANY, ANY, ANY, ANY],
        out_specs=[ANY] * len(outs),
        scratch_shapes=scratch,
        compiler_params=pltpu.CompilerParams(
            collective_id=1, has_side_effects=True, vmem_limit_bytes=64 * 1024 * 1024
        ),
        cost_estimate=pl.CostEstimate(flops=flops, bytes_accessed=flops // 256, transcendentals=0),
        name="train",
    )(states, cotangent, own_norms, own_bias, rope, mask, own_q, own_o, own_g, own_d)


def finish_kernel(attn, ffn, states, grads, g_qkv, g_out, g_gate_up, g_down, out_states, out_grads):
    local, ff = g_qkv.shape[3], g_gate_up.shape[3]

    def total(parts, at, wide):
        return sum(parts[0, n, :, at : at + wide].astype(F32) for n in range(parts.shape[1]))

    for m in range(3):
        g_qkv[0, m] = total(attn, m * lane_stride(local), local)
    g_out[0] = total(attn, 3 * lane_stride(local), local).T
    for m in range(2):
        g_gate_up[0, :, m, :] = total(ffn, m * lane_stride(ff), ff)
    g_down[0] = total(ffn, 2 * lane_stride(ff), ff).T
    out_states[...] = states[...]
    out_grads[...] = grads[...]


def finish(sums_attn, sums_ffn, states, grads, local, ff):
    parts, depth = sums_attn.shape[1:3]
    tokens, width = states.shape
    rows = min(PAIR, depth)
    cuts = depth // rows
    pieces = tokens // (LAYERS * cuts)
    shape = jax.ShapeDtypeStruct
    spec = pl.BlockSpec
    token_spec = spec((pieces, width), lambda l, r: (l * cuts + r, 0))
    return pl.pallas_call(
        finish_kernel,
        grid=(LAYERS, cuts),
        in_specs=[
            spec((1, parts, rows, sums_attn.shape[3]), lambda l, r: (l, 0, r, 0)),
            spec((1, parts, rows, sums_ffn.shape[3]), lambda l, r: (l, 0, r, 0)),
            token_spec,
            token_spec,
        ],
        out_specs=[
            spec((1, 3, rows, local), lambda l, r: (l, 0, r, 0)),
            spec((1, local, rows), lambda l, r: (l, 0, r)),
            spec((1, rows, 2, ff), lambda l, r: (l, r, 0, 0)),
            spec((1, ff, rows), lambda l, r: (l, 0, r)),
            token_spec,
            token_spec,
        ],
        out_shape=[
            shape((LAYERS, 3, depth, local), F32),
            shape((LAYERS, local, depth), F32),
            shape((LAYERS, depth, 2, ff), F32),
            shape((LAYERS, ff, depth), F32),
            shape((tokens, width), BF16),
            shape((tokens, width), F32),
        ],
        compiler_params=pltpu.CompilerParams(vmem_limit_bytes=48 * 1024 * 1024),
        name="finish",
    )(sums_attn, sums_ffn, states, grads)


def tables(segment_ids, rows):
    places = jnp.arange(rows, dtype=jnp.int32)
    same = segment_ids[:, None] == segment_ids[None, :]
    earlier = places[None, :] < places[:, None]
    position = jnp.sum(jnp.where(same & earlier, 1.0, 0.0), axis=1)
    half = ROT_DIM // 2
    lane = jnp.arange(PAIR, dtype=jnp.int32) % HEAD_DIM
    inverse = rotary_base ** (-((lane % half).astype(F32) * 2.0 / ROT_DIM))
    angle = position[:, None] * jnp.where(lane < ROT_DIM, inverse, 0.0)[None, :]
    sine = jnp.sin(angle)
    rope = jnp.stack(
        [jnp.cos(angle), jnp.where(lane < half, -sine, 0.0), jnp.where((lane >= half) & (lane < ROT_DIM), sine, 0.0)]
    )
    return rope, jnp.where(same & (places[None, :] <= places[:, None]), 0.0, -1e30)


def on_device(
    states,
    segment_ids,
    ln1_gain,
    ln1_bias,
    qkv_weight,
    qkv_bias,
    out_weight,
    ln2_gain,
    ln2_bias,
    gate_up_weight,
    down_weight,
    cotangent,
):
    tokens = states.shape[0]
    rope, allowed = tables(segment_ids, tokens)
    steps = plan(tokens)[0]
    mask = allowed.reshape(steps, -1, tokens).transpose(0, 2, 1).astype(BF16)
    own_norms = jnp.stack([ln1_gain, ln1_bias, ln2_gain, ln2_bias], axis=1).reshape(4 * LAYERS, -1).astype(F32)
    own_bias = qkv_bias.reshape(LAYERS * 3, -1).astype(F32)
    own_bias = jnp.pad(own_bias, ((0, 8 - own_bias.shape[0]), (0, PAIR - own_bias.shape[1])))
    out_states, grad_states, sums_attn, sums_ffn, norm_parts, bias_parts, *_ = train(
        states,
        cotangent,
        own_norms,
        own_bias,
        rope,
        mask,
        qkv_weight.transpose(0, 2, 1, 3),
        out_weight.transpose(0, 2, 1)[:, None],
        gate_up_weight.transpose(0, 2, 1, 3),
        down_weight.transpose(0, 2, 1)[:, None],
    )
    g_qkv, g_out, g_gate_up, g_down, out_states, grad_states = finish(
        sums_attn, sums_ffn, out_states, grad_states, qkv_weight.shape[3], gate_up_weight.shape[3]
    )
    g_norms = jnp.sum(norm_parts, axis=0).reshape(LAYERS, 4, -1)
    g_bias = jnp.sum(bias_parts, axis=0).reshape(LAYERS, 8, -1, HEAD_DIM)[:, :3]
    share = qkv_bias.shape[3]
    g_bias = lax.dynamic_slice_in_dim(g_bias, lax.axis_index("fsdp") * share, share, axis=3)
    return (
        out_states,
        grad_states,
        g_norms[:, 0],
        g_norms[:, 1],
        g_qkv.transpose(0, 2, 1, 3),
        g_bias,
        g_out,
        g_norms[:, 2],
        g_norms[:, 3],
        g_gate_up,
        g_down,
    )


def solution(mesh):
    in_specs = (
        P("fsdp", None),
        P("fsdp"),
        P(None, "fsdp"),
        P(None, "fsdp"),
        P(None, "fsdp", None, "tensor"),
        P(None, None, "tensor", "fsdp"),
        P(None, "tensor", "fsdp"),
        P(None, "fsdp"),
        P(None, "fsdp"),
        P(None, "fsdp", None, "tensor"),
        P(None, "tensor", "fsdp"),
        P("fsdp", None),
    )
    out_specs = (
        P("fsdp", None),
        P("fsdp", None),
        P(None, "fsdp"),
        P(None, "fsdp"),
        P(None, "fsdp", None, "tensor"),
        P(None, None, "tensor", "fsdp"),
        P(None, "tensor", "fsdp"),
        P(None, "fsdp"),
        P(None, "fsdp"),
        P(None, "fsdp", None, "tensor"),
        P(None, "tensor", "fsdp"),
    )
    return jax.shard_map(
        on_device, mesh=mesh, in_specs=in_specs, out_specs=out_specs, check_vma=False
    )
```

```python
import functools
import math

import jax
import jax.numpy as jnp
from jax import lax
from jax.experimental import pallas as pl
from jax.experimental.pallas import tpu as pltpu
from jax.sharding import PartitionSpec as P

MESH = pl.DeviceIdType.MESH
HEAD_DIM = 64
ROT_DIM = 16
LAYERS = 2
PAIR = 2 * HEAD_DIM
ANY = pl.BlockSpec(memory_space=pl.ANY)
VMEM = pl.BlockSpec(memory_space=pltpu.VMEM)
BF16 = jnp.bfloat16
F32 = jnp.float32

norm_epsilon = 1e-05
rotary_base = 10000.0


def dot(a, b):
    return lax.dot_general(a, b, (((1,), (0,)), ((), ())), preferred_element_type=F32)


def dot_nt(a, b):
    return lax.dot_general(a, b, (((1,), (1,)), ((), ())), preferred_element_type=F32)


def dot_tn(a, b):
    return lax.dot_general(a, b, (((0,), (0,)), ((), ())), preferred_element_type=F32)


def tiles(extent, most=512):
    return [(at, min(most, extent - at)) for at in range(0, extent, most)]


def standardize(values):
    average = jnp.mean(values, axis=-1, keepdims=True)
    centred = values - average
    spread = jnp.mean(centred * centred, axis=-1, keepdims=True)
    rstd = lax.rsqrt(spread + norm_epsilon)
    return centred * rstd, rstd


def turn(values, rope, sign):
    half = ROT_DIM // 2
    factor, below, above = rope
    return values * factor + sign * (
        pltpu.roll(values, PAIR - half, 1) * below + pltpu.roll(values, half, 1) * above
    )


def when(condition):
    return pl.when(condition)


def to(source, target, send, arrive, place):
    return pltpu.make_async_remote_copy(
        src_ref=source, dst_ref=target, send_sem=send, recv_sem=arrive, device_id=place, device_id_type=MESH
    )


def spread(build, source, target, count=4):
    rows = source.shape[-2] // count
    for r in range(count):
        piece = (slice(None),) * (len(source.shape) - 2) + (pl.ds(r * rows, rows), slice(None))
        build(source.at[piece], target.at[piece]).start()


def start(source, target, build):
    spread(build, source, target)


def whole(source, target, build):
    return build(source, target)


class Line:
    def __init__(self, count):
        place = lax.axis_index("tensor")
        half = count // 2
        left = place < half
        self.inner = jnp.where(left, place + 1, place - 1)
        self.outer = jnp.where(left, place - 1, place + 1)
        self.has_outer = (place != 0) & (place != count - 1)
        self.no_outer = jnp.logical_not(self.has_outer)
        self.distance = jnp.where(left, half - 1 - place, place - half)
        self.centre = self.distance == 0
        self.off_centre = jnp.logical_not(self.centre)


class Group:
    def __init__(self, count):
        self.count = count
        self.chips = count // 2
        self.me = lax.axis_index("fsdp")
        self.chip = self.me // 2
        self.core = self.me % 2
        self.peer = self.me + 1 - 2 * self.core
        self.square = self.chips == 4
        self.everyone = [(self.me + i) % count for i in range(1, count)]
        if self.square:
            self.x = self.at(self.chip + 1 - 2 * (self.chip % 2))
            self.y = self.at(self.chip + 2 - 4 * (self.chip // 2))
            self.far = self.at(3 - self.chip)
            self.others = [self.x, self.y]
        else:
            self.others = [self.at((self.chip + i) % self.chips) for i in range(1, self.chips)]

    def at(self, chip):
        return chip * 2 + self.core


def enter(line, partners):
    barrier = pltpu.get_barrier_semaphore()
    for partner in partners:
        pl.semaphore_signal(barrier, inc=1, device_id={"fsdp": partner}, device_id_type=MESH)
    pl.semaphore_signal(barrier, inc=1, device_id={"tensor": line.inner}, device_id_type=MESH)

    @when(line.has_outer)
    def _():
        pl.semaphore_signal(barrier, inc=1, device_id={"tensor": line.outer}, device_id_type=MESH)
        pl.semaphore_wait(barrier, len(partners) + 2)

    @when(line.no_outer)
    def _():
        pl.semaphore_wait(barrier, len(partners) + 1)


class Flow:
    def __init__(self, line, steps, span, rows, refs):
        self.line, self.steps, self.span, self.rows = line, steps, span, rows
        self.from_outer, self.from_inner, self.running = refs[:3]
        self.send_in, self.got_out, self.send_out, self.got_in, self.credit = refs[3:]
        self.lag = jnp.minimum(3 * line.distance + 2, steps - 1)

    def slot(self, i):
        big = self.rows * self.span
        return pl.ds(pl.multiple_of(i * big, big), big)

    def pieces(self, i):
        for r in range(self.span):
            q = i * self.span + r
            yield q, pl.ds(pl.multiple_of(q * self.rows, self.rows), self.rows)

    def inward(self, q, here, target, arrive):
        return to(
            self.running.at[here], target.at[here], self.send_in.at[q], arrive.at[q], {"tensor": self.line.inner}
        )

    def outward(self, q, here):
        return to(
            self.from_inner.at[here], self.from_inner.at[here], self.send_out.at[q], self.got_in.at[q],
            {"tensor": self.line.outer},
        )

    def clear(self, i):
        for q, here in self.pieces(i):
            self.inward(q, here, self.from_inner, self.got_in).wait_send()

    def push(self, i, again):
        line = self.line

        @when(line.centre & again)
        def _():
            pl.semaphore_wait(self.credit, 1)

        for q, here in self.pieces(i):

            @when(line.has_outer)
            def _(q=q, here=here):
                self.inward(q, here, self.from_outer, self.got_out).wait_recv()
                total = self.running[here, :].astype(F32) + self.from_outer[here, :].astype(F32)
                self.running[here, :] = total.astype(BF16)

            @when(line.centre)
            def _(q=q, here=here):
                self.inward(q, here, self.from_inner, self.got_in).start()

            @when(line.off_centre)
            def _(q=q, here=here):
                self.inward(q, here, self.from_outer, self.got_out).start()

    def pull(self, i):
        line = self.line
        for q, here in self.pieces(i):
            self.inward(q, here, self.from_inner, self.got_in).wait_recv()

            @when(line.centre)
            def _(q=q, here=here):
                total = self.running[here, :].astype(F32) + self.from_inner[here, :].astype(F32)
                self.from_inner[here, :] = total.astype(BF16)

            @when(line.has_outer)
            def _(q=q, here=here):
                self.outward(q, here).start()

    def release(self, i, more):
        line = self.line

        @when(line.has_outer)
        def _():
            for q, here in self.pieces(i):
                self.outward(q, here).wait_send()

        @when(line.centre & more)
        def _():
            pl.semaphore_signal(self.credit, inc=1, device_id={"tensor": line.inner}, device_id_type=MESH)


def flow_scratch(steps, span, tokens, width):
    whole = pltpu.VMEM((tokens, width), BF16)
    sems = pltpu.SemaphoreType.DMA((steps * span,))
    return [whole, whole, whole, sems, sems, sems, sems, pltpu.SemaphoreType.REGULAR]


def gather_kinds(count):
    return 9 if count == 8 else count


class Gather:
    def __init__(self, group, own, whole, send, arrive, load):
        self.group, self.own, self.whole, self.send, self.arrive, self.load_sems = group, own, whole, send, arrive, load
        self.half = own.shape[1] // 2
        self.links = len(group.others)

    def half_at(self, shard, h):
        return self.whole.at[shard, :, pl.ds(h * self.half, self.half), :]

    def way(self, kind):
        g, links = self.group, self.links
        if kind < links:
            return self.own, self.whole.at[g.me], g.others[kind]
        if kind == links:
            return self.own, self.whole.at[g.me], g.peer
        if kind <= 2 * links:
            shard = self.whole.at[g.others[kind - links - 1]]
            return shard, shard, g.peer
        if kind == 2 * links + 1:
            return self.half_at(g.x, 0), self.half_at(g.x, 0), g.y
        if kind == 2 * links + 2:
            return self.half_at(g.y, 1), self.half_at(g.y, 1), g.x
        return self.whole.at[g.far], self.whole.at[g.far], g.peer

    def build(self, kind, source, target):
        return to(source, target, self.send.at[kind], self.arrive.at[kind], {"fsdp": self.way(kind)[2]})

    def copy(self, kind):
        return self.build(kind, *self.way(kind)[:2])

    def start(self, kind):
        spread(functools.partial(self.build, kind), *self.way(kind)[:2])

    def local(self):
        return pltpu.make_async_copy(self.own, self.whole.at[self.group.me], self.send.at[gather_kinds(self.group.count) - 1])

    def begin(self):
        for kind in range(self.links + 1):
            self.start(kind)
        self.local().start()

    def relay(self):
        for kind in range(self.links):
            self.copy(kind).wait_recv()
        if self.group.square:
            self.start(2 * self.links + 1)
            self.start(2 * self.links + 2)
        for kind in range(self.links):
            self.start(self.links + 1 + kind)

    def relay_far(self):
        if self.group.square:
            self.copy(2 * self.links + 1).wait_recv()
            self.copy(2 * self.links + 2).wait_recv()
            self.start(2 * self.links + 3)

    def settle(self):
        self.local().wait()
        for kind in range(self.links, 2 * self.links + 1):
            self.copy(kind).wait_recv()
        if self.group.square:
            self.copy(2 * self.links + 3).wait_recv()

    def loads(self, target):
        depth = self.own.shape[1]
        for k in range(self.group.count):
            yield pltpu.make_async_copy(
                self.whole.at[k], target.at[:, pl.ds(k * depth, depth), :], self.load_sems.at[k]
            )

    def finish(self):
        for kind in range(2 * self.links + 1 + (3 if self.group.square else 0)):
            self.copy(kind).wait_send()


def train_kernel(
    count, shards, steps, span, per_step,
    states, cotangent, own_norms, own_bias, rope, mask, own_q, own_o, own_g, own_d,
    out_states, grad_states, sums_attn, sums_ffn, norm_parts, bias_parts,
    whole_q, whole_o, whole_g, whole_d, s_x, s_n, s_y, s_qkv, s_att, s_gu, s_hid,
    mate_attn, mate_ffn, via_attn, via_ffn,
    res, w_attn, w_ffn, gu, hid, qkv, att, d_key, d_value, x_in, low,
    log_total, norms, biases, bias_in, norm_acc, bias_acc, columns, turned, staged,
    x_save, x_sem, low_sem, out_sem, keep_sem, act_sem, misc, load_sem, g_send, g_arrive,
    column_sem, stage_sem, relay_sem, mate_send, mate_got, own_send, own_got, small_send, small_got,
    *flow_refs,
):
    tokens, width = res.shape
    big = tokens // steps
    local, ff = w_attn.shape[2], w_ffn.shape[2]
    depth = width // shards
    line = Line(count)
    group = Group(shards)
    chips = group.chips
    flow = Flow(line, steps, span, big // span, flow_refs)
    scale = jnp.asarray(1.0 / math.sqrt(HEAD_DIM), BF16)
    half = 2 * LAYERS
    stages = 2 * half
    total = stages * steps
    top = LAYERS - 1
    units = 2 * chips

    def block(c):
        return pl.ds(pl.multiple_of(c * big, big), big)

    kinds = [(own_q, whole_q), (own_o, whole_o), (own_g, whole_g), (own_d, whole_d)]
    targets = [w_attn.at[0:3], w_attn.at[3:4], w_ffn.at[0:2], w_ffn.at[2:3]]

    def gather(layer, kind):
        n = 4 * layer + kind
        own, whole = kinds[kind]
        return Gather(group, own.at[layer], whole.at[layer], g_send.at[n], g_arrive.at[n], load_sem.at[kind])

    def load(layer, kind, wait):
        own, whole = kinds[kind]
        way = Gather(group, own.at[0], whole.at[layer], g_send.at[0], g_arrive.at[0], load_sem.at[kind])
        for copy in way.loads(targets[kind]):
            if wait:
                copy.wait()
            else:
                copy.start()

    events = {}

    def event(t, where, *actions):
        events.setdefault((t, where, None), []).extend(actions)

    def event_by_role(centre, others, *actions):
        events.setdefault(centre + (True,), []).extend(actions)
        events.setdefault(others + (False,), []).extend(actions)

    def loading(layer, kind, wait):
        return functools.partial(load, layer, kind, wait)

    def at(stage, i):
        return stage * steps + min(i, steps - 1)

    q, o, g, d = 0, 1, 2, 3
    event(0, 1, gather(0, o).relay_far, gather(0, o).settle, loading(0, o, False), loading(0, o, True))
    event_by_role((at(0, 3), 0), (at(0, 4), 0), gather(0, g).relay)
    event_by_role((at(0, 5), 0), (at(0, 5), 2), gather(0, g).relay_far, gather(0, d).begin)
    event(at(1, 0), 0, gather(0, g).settle, loading(0, g, False), loading(0, g, True))
    event(at(1, 0), 1, gather(0, d).relay)
    for layer in range(1, LAYERS):
        s = 2 * layer - 1
        event(at(s, 0), 1, gather(layer, q).begin)
        if layer == 1:
            event(at(s, 0), 1, gather(0, d).relay_far, gather(0, d).settle, loading(0, d, False), loading(0, d, True))
        event(at(s, 2), 0, gather(layer, q).relay, gather(layer, o).begin)
        event_by_role((at(s, 3), 0), (at(s, 3), 2), gather(layer, q).relay_far, gather(layer, o).relay, gather(layer, g).begin)
        event(at(s, 4), 2, gather(layer, o).relay_far)
        event(at(s, 5), 2, gather(layer, q).settle, loading(layer, q, False))
        event(at(s, 5), 2, gather(layer, o).settle, loading(layer, o, False))
        s += 1
        event(at(s, 0), 0, loading(layer, q, True), loading(layer, o, True))
        event_by_role((at(s, 0), 0), (at(s, 0), 2), gather(layer, g).relay)
        event_by_role((at(s, 2), 0), (at(s, 2), 2), gather(layer, g).relay_far, gather(layer, d).begin)
        event(at(s, 3), 2, gather(layer, g).settle, loading(layer, g, False))
        event_by_role((at(s, 4), 0), (at(s, 4), 2), gather(layer, d).relay)
        event(at(s, 5), 2, gather(layer, d).relay_far)
        s += 1
        event(at(s, 0), 0, loading(layer, g, True), gather(layer, d).settle, loading(layer, d, False))
        event(at(s, 0), 1, loading(layer, d, True))

    def run_events(t, where):
        ordered = sorted(events.items(), key=lambda item: item[0][:2])
        ordered = [(at, role, actions) for (at, place, role), actions in ordered if place == where]
        for stage in sorted({at // steps for at, _, _ in ordered}):

            @when(t // steps == stage)
            def _(stage=stage):
                for at, role, actions in ordered:
                    if at // steps != stage:
                        continue
                    condition = t == at
                    if role is not None:
                        condition = condition & (line.centre if role else line.off_centre)

                    @when(condition)
                    def _(actions=actions):
                        for action in actions:
                            action()

    enter(line, group.everyone)
    mine = pl.ds(pl.multiple_of(group.me * depth, depth), depth)
    small = []
    for n, other in enumerate(group.everyone):
        sems = (small_send.at[0, n], small_got.at[0, n])
        small.append(to(own_norms, norms.at[:, mine], *sems, {"fsdp": other}))
        sems = (small_send.at[1, n], small_got.at[1, n])
        small.append(to(own_bias, bias_in.at[group.me], *sems, {"fsdp": other}))
    gather(0, q).begin()
    for copy in small:
        copy.start()
    starts = [
        pltpu.make_async_copy(own_norms, norms.at[:, mine], misc.at[0]),
        pltpu.make_async_copy(own_bias, bias_in.at[group.me], misc.at[1]),
        pltpu.make_async_copy(states, flow.running, misc.at[2]),
        pltpu.make_async_copy(cotangent, s_y.at[0], misc.at[3]),
    ]
    for copy in starts:
        copy.start()
    qkv[...] = jnp.zeros_like(qkv)
    norm_acc[...] = jnp.zeros_like(norm_acc)
    bias_acc[...] = jnp.zeros_like(bias_acc)
    for copy in starts:
        copy.wait()
    for c in range(steps):
        res[c * big : (c + 1) * big, :] = flow.running[c * big : (c + 1) * big, :].astype(F32)
    for copy in small:
        copy.wait_recv()
    each = HEAD_DIM // shards
    source = lax.broadcasted_iota(jnp.int32, (PAIR, local), 0)
    column = lax.broadcasted_iota(jnp.int32, (PAIR, local), 1)
    at_head = lax.div(source, each) == lax.div(column, HEAD_DIM)
    whole_bias = jnp.zeros((8, local), F32)
    for k in range(shards):
        match = at_head & (lax.rem(column, HEAD_DIM) == k * each + lax.rem(source, each))
        whole_bias += dot(bias_in[k].astype(BF16), jnp.where(match, 1.0, 0.0).astype(BF16))
    biases[...] = whole_bias
    gather(0, q).relay()
    gather(0, o).begin()
    gather(0, q).relay_far()
    gather(0, o).relay()
    gather(0, g).begin()
    gather(0, q).settle()
    load(0, q, False)
    load(0, q, True)

    lanes = lax.broadcasted_iota(jnp.int32, (big, PAIR), 1)
    first_head = lanes < HEAD_DIM

    def save_x(stage, c):
        return pltpu.make_async_copy(res.at[block(c)], s_x.at[stage, block(c)], x_save.at[c])

    def keeps(layer, kind, c):
        here = block(c)
        if kind == 0:
            pairs = [(gu.at[:, here], s_gu.at[layer, :, here]), (hid.at[here], s_hid.at[layer, here])]
        else:
            pairs = [(qkv.at[:, here], s_qkv.at[layer, :, here]), (att.at[here], s_att.at[layer, here])]
        return [pltpu.make_async_copy(a, b, keep_sem.at[kind, n, c]) for n, (a, b) in enumerate(pairs)]

    def activations(layer, kind):
        if kind == 0:
            pairs = [(s_gu.at[layer], gu), (s_hid.at[layer], hid)]
        else:
            pairs = [(s_qkv.at[layer], qkv), (s_att.at[layer], att)]
        return [pltpu.make_async_copy(a, b, act_sem.at[kind, n]) for n, (a, b) in enumerate(pairs)]

    def project(*pairs):
        def write(i):
            here = flow.slot(i)
            for at, wide in tiles(width, 1024):
                part = sum(dot_nt(right[at : at + wide, :], left()) for left, right in pairs)
                flow.running[here, at : at + wide] = part.T.astype(BF16)

        return write

    def by_extent(c, work):
        early = steps // 2

        @when(c < early)
        def _():
            work(early * big)

        @when(c >= early)
        def _():
            work(tokens)

    def normed_rows(stage, c):
        here = block(c)

        @when(stage > 0)
        def _():
            save_x(stage, c).wait()
            res[here, :] += flow.from_inner[flow.slot(c), :].astype(F32)

        save_x(stage, c).start()
        xhat, _ = standardize(res[here, :])
        low[...] = (xhat * norms[pl.ds(2 * stage, 1), :] + norms[pl.ds(2 * stage + 1, 1), :]).astype(BF16)
        pltpu.make_async_copy(low, s_n.at[stage, here], low_sem.at[0]).start()

    def attention_forward(t, layer, c):
        here = block(c)

        @when(layer > 0)
        def _():
            for copy in keeps(layer - 1, 1, c):
                copy.wait()

        for part in range(3):
            for at, wide in tiles(local):
                mixed = dot(low[...], w_attn[part, :, at : at + wide])
                for pair in range(wide // PAIR):
                    to_lane = at + pair * PAIR
                    span_here = slice(to_lane, to_lane + PAIR)
                    value = mixed[:, pair * PAIR : (pair + 1) * PAIR]
                    value = value + biases[pl.ds(3 * layer + part, 1), :][:, span_here]
                    if part < 2:
                        value = turn(value, [rope[n, here, :] for n in range(3)], 1.0)
                    qkv[part, here, span_here] = value.astype(BF16)
        def attend(keys):
            closed = mask[c, 0:keys].astype(F32)
            for pair in range(local // PAIR):
                lane = slice(pair * PAIR, (pair + 1) * PAIR)
                query, key, value = qkv[0, here, lane] * scale, qkv[1, 0:keys, lane], qkv[2, 0:keys, lane]
                outs = []
                for head in range(2):
                    own = first_head if head == 0 else jnp.logical_not(first_head)
                    scores = dot_nt(key, jnp.where(own, query, jnp.zeros_like(query))) + closed
                    most = jnp.max(scores, axis=0, keepdims=True)
                    exps = jnp.exp(scores - most)
                    total_exp = jnp.sum(exps, axis=0, keepdims=True)
                    log_total[layer, c, 2 * pair + head : 2 * pair + head + 1, :] = most + jnp.log(total_exp)
                    probs = exps * (1.0 / total_exp)
                    outs.append(dot_tn(probs.astype(BF16), value))
                att[here, lane] = jnp.where(first_head, outs[0], outs[1]).astype(BF16)

        by_extent(c, attend)

        @when(layer < top)
        def _():
            for copy in keeps(layer, 1, c):
                copy.start()

        run_events(t, 1)
        project((lambda: att[here, :], w_attn.at[3]))(c)

    def ffn_forward(t, layer, c):
        here = block(c)

        @when(layer > 0)
        def _():
            for copy in keeps(layer - 1, 0, c):
                copy.wait()

        for at, wide in tiles(ff):
            gate = dot(low[...], w_ffn[0, :, at : at + wide])
            up = dot(low[...], w_ffn[1, :, at : at + wide])
            gu[0, here, at : at + wide] = gate.astype(BF16)
            gu[1, here, at : at + wide] = up.astype(BF16)
            hid[here, at : at + wide] = (gate * jax.nn.sigmoid(gate) * up).astype(BF16)

        @when(layer < top)
        def _():
            for copy in keeps(layer, 0, c):
                copy.start()

        run_events(t, 1)
        project((lambda: hid[here, :], w_ffn.at[2]))(c)

    def fetch_x(back, c):
        return pltpu.make_async_copy(s_x.at[half - back, block(c)], x_in, x_sem.at[0])

    def fetch_low(c):
        return pltpu.make_async_copy(s_y.at[0, block(c)], low, low_sem.at[1])

    def save_low(back, c):
        return pltpu.make_async_copy(low, s_y.at[back, block(c)], low_sem.at[0])

    def take(back, i, c):
        here = block(c)
        row = 2 * (half - back)
        fetch_x(back, c).wait()

        @when(back == 1)
        def _():
            fetch_low(c).wait()
            res[here, :] = low[...].astype(F32)

        xhat, rstd = standardize(x_in[...])
        e = flow.from_inner[flow.slot(i), :].astype(F32)
        scaled = e * norms[pl.ds(row, 1), :]
        inner = jnp.mean(scaled * xhat, axis=-1, keepdims=True)
        res[here, :] += rstd * (scaled - jnp.mean(scaled, axis=-1, keepdims=True) - xhat * inner)
        norm_acc[pl.ds(row, 1), :] += jnp.sum(e * xhat, axis=0, keepdims=True)
        norm_acc[pl.ds(row + 1, 1), :] += jnp.sum(e, axis=0, keepdims=True)

    def ffn_backward(i, c):
        here = block(c)
        for at, wide in tiles(ff):
            lane = slice(at, at + wide)
            d_hidden = dot(low[...], w_ffn[2, :, lane])
            gate, up = gu[0, here, lane].astype(F32), gu[1, here, lane].astype(F32)
            sigma = jax.nn.sigmoid(gate)
            gu[0, here, lane] = (d_hidden * up * sigma * (1.0 + gate * (1.0 - sigma))).astype(BF16)
            gu[1, here, lane] = (d_hidden * gate * sigma).astype(BF16)
        project((lambda: gu[0, here, :], w_ffn.at[0]), (lambda: gu[1, here, :], w_ffn.at[1]))(i)

    def attention_backward(layer, i, c):
        here = block(c)
        def attend_back(keys):
            closed = mask[c, 0:keys].astype(F32)
            turns = [rope[n, here, :] for n in range(3)]
            for pair in range(local // PAIR):
                lane = slice(pair * PAIR, (pair + 1) * PAIR)
                d_att = dot(low[...], w_attn[3, :, lane]).astype(BF16)
                query, key, value = qkv[0, here, lane], qkv[1, 0:keys, lane], qkv[2, 0:keys, lane]
                d_query, key_parts, value_parts = [], [], []
                for head in range(2):
                    own = first_head if head == 0 else jnp.logical_not(first_head)
                    own_query = jnp.where(own, query, jnp.zeros_like(query)) * scale
                    own_d_att = jnp.where(own, d_att, jnp.zeros_like(d_att))
                    scores = dot_nt(key, own_query) + closed
                    probs = jnp.exp(scores - log_total[layer, c, 2 * pair + head : 2 * pair + head + 1, :])
                    d_probs = dot_nt(value, own_d_att)
                    d_scores = probs * (d_probs - jnp.sum(probs * d_probs, axis=0, keepdims=True))
                    d_scores = d_scores.astype(BF16)
                    key_parts.append(dot(d_scores, own_query))
                    value_parts.append(dot(probs.astype(BF16), own_d_att))
                    d_query.append(dot_tn(d_scores, key))
                d_key[0:keys, lane] += key_parts[0] + key_parts[1]
                d_value[0:keys, lane] += value_parts[0] + value_parts[1]
                parts = [
                    turn(jnp.where(first_head, d_query[0], d_query[1]) / math.sqrt(HEAD_DIM), turns, -1.0),
                    turn(d_key[here, lane], turns, -1.0),
                    d_value[here, lane],
                ]
                for part, values in enumerate(parts):
                    values = values.astype(BF16)
                    qkv[part, here, lane] = values
                    bias_acc[layer, part : part + 1, lane] += jnp.sum(values.astype(F32), axis=0, keepdims=True)

        by_extent(c, attend_back)
        project(
            (lambda: qkv[0, here, :], w_attn.at[0]),
            (lambda: qkv[1, here, :], w_attn.at[1]),
            (lambda: qkv[2, here, :], w_attn.at[2]),
        )(i)

    class Blocks:
        def __init__(self, back, kind):
            self.back_stage, self.kind = back, kind
            layer = top - back // 2
            self.sums = (sums_ffn if kind == 0 else sums_attn).at[layer]
            self.mate = (mate_ffn if kind == 0 else mate_attn).at[layer]
            self.via = (via_ffn if kind == 0 else via_attn).at[layer]
            self.home = 0 if group.square else group.chip
            self.stride = lane_stride(ff if kind == 0 else local)
            self.held = staged.at[:, :, 0 : (4 - (kind == 0)) * self.stride]
            self.x = s_n.at[2 * layer + 1 - kind]
            self.y = s_y.at[back]
            if kind == 0:
                self.right = [(0, gu.at[0]), (0, gu.at[1]), (1, hid)]
            else:
                self.right = [(0, qkv.at[0]), (0, qkv.at[1]), (0, qkv.at[2]), (1, att)]

        def own(self, u):
            return (u == 3) | (u >= 5) if group.square else u >= chips

        def place(self, u):
            if not group.square:
                return u % chips
            return jnp.where(u < 3, u, jnp.where(u == 3, 0, jnp.where(u == 4, 3, u - 4)))

        def chip(self, u):
            if not group.square:
                return (group.chip + 1 + u) % chips
            x, y, far = group.x // 2, group.y // 2, group.far // 2
            k = self.place(u)
            return jnp.where(k == 0, far, jnp.where(k == 1, x, jnp.where(k == 2, y, group.chip)))

        def fetch(self, u):
            core = jnp.where(self.own(u), group.core, 1 - group.core)
            at = pl.multiple_of((self.chip(u) * 2 + core) * depth, depth)
            return [
                pltpu.make_async_copy(
                    source.at[:, pl.ds(at, depth)], columns.at[u % 2, n], column_sem.at[self.kind, u % 2, n]
                )
                for n, source in enumerate((self.x, self.y))
            ]

        def over(self, u):
            j = self.chip(u)
            sems = (mate_send.at[self.back_stage, j], mate_got.at[self.back_stage, j])
            return self.held.at[u % 2], self.mate.at[j], lambda a, b: to(a, b, *sems, {"fsdp": group.peer})

        def near(self, source, target, u):
            return source, target, lambda a, b: pltpu.make_async_copy(a, b, stage_sem.at[self.kind, u % 2])

        def bring(self, u):
            return self.near(self.mate.at[self.chip(u)], self.held.at[u % 2], u)

        def back(self, u):
            return self.near(self.held.at[u % 2], self.mate.at[self.chip(u)], u)

        def keep(self, u):
            return self.near(self.held.at[u % 2], self.sums.at[self.home], u)

        def push(self, u):
            j = self.chip(u)
            sems = (own_send.at[self.back_stage, j], own_got.at[self.back_stage, group.chip])
            return self.mate.at[j], self.sums.at[group.chip], lambda a, b: to(a, b, *sems, {"fsdp": group.at(j)})

        def hop(self, kind):
            over_x = kind % 2 == 0
            first = over_x if kind < 4 else not over_x
            rows = pl.ds(0 if first else depth // 2, depth // 2)
            target = group.x if over_x else group.y
            sems = (own_send.at[self.back_stage, kind], own_got.at[self.back_stage, kind])
            build = lambda a, b: to(a, b, *sems, {"fsdp": target})
            if kind < 2:
                return self.mate.at[group.far // 2, rows], self.via.at[kind], build
            place = self.sums.at[1 if over_x else 2, rows]
            if kind < 4:
                return self.mate.at[target // 2, rows], place, build
            return self.via.at[1 if over_x else 0], place, build

        def send_on(self, u):
            whole(*self.back(u)).wait()
            if not group.square:
                start(*self.push(u))
                return
            for k, hops in enumerate(((0, 1), (2,), (3,))):

                @when(self.place(u) == k)
                def _(hops=hops):
                    for kind in hops:
                        start(*self.hop(kind))

        def relay(self):
            if not group.square:
                return
            rest = depth // 2
            steps_in = []
            for n, (kind, target, rows) in enumerate(
                ((1, group.x, pl.ds(rest, rest)), (0, group.y, pl.ds(0, rest)))
            ):
                whole(*self.hop(kind)).wait_recv()
                pair = [
                    pltpu.make_async_copy(self.mate.at[target // 2, rows], self.held.at[n, pl.ds(0, rest)], relay_sem.at[n, 0]),
                    pltpu.make_async_copy(self.via.at[kind], self.held.at[n, pl.ds(rest, rest)], relay_sem.at[n, 1]),
                ]
                for copy in pair:
                    copy.start()
                steps_in.append((kind, pair))
            returns = []
            lanes_here = (4 - (self.kind == 0)) * self.stride
            for n, (kind, pair) in enumerate(steps_in):
                for copy in pair:
                    copy.wait()
                for at, wide in tiles(lanes_here, 512):
                    lane = slice(at, at + wide)
                    both = staged[n, 0:rest, lane].astype(F32) + staged[n, rest:depth, lane].astype(F32)
                    staged[n, 0:rest, lane] = both.astype(BF16)
                copy = pltpu.make_async_copy(self.held.at[n, pl.ds(0, rest)], self.via.at[kind], relay_sem.at[n, 0])
                copy.start()
                returns.append(copy)
            for copy, kind in zip(returns, (4, 5)):
                copy.wait()
                start(*self.hop(kind))

        def unit(self, u):
            slot = u % 2
            own = self.own(u)

            @when(u + 1 < units)
            def _():
                for copy in self.fetch(u + 1):
                    copy.start()

            @when((u >= 2) & jnp.logical_not(self.own(u - 2)))
            def _():
                whole(*self.over(u - 2)).wait_send()

            @when((u >= 1) & self.own(u - 1))
            def _():
                self.send_on(u - 1)

            @when(own)
            def _():
                whole(*self.over(u)).wait_recv()
                start(*self.bring(u))

            for copy in self.fetch(u):
                copy.wait()
            for left in range(2):
                turned[left] = columns[slot, left].T

            @when(own)
            def _():
                whole(*self.bring(u)).wait()

            def form(add):
                for m, (left, right) in enumerate(self.right):
                    for at, wide in tiles(right.shape[1]):
                        product = dot(turned[left], right[:, at : at + wide])
                        lane = slice(m * self.stride + at, m * self.stride + at + wide)
                        if add:
                            product = product + staged[slot, :, lane].astype(F32)
                        staged[slot, :, lane] = product.astype(BF16)

            @when(own)
            def _():
                form(True)

            @when(jnp.logical_not(own))
            def _():
                form(False)

            @when(jnp.logical_not(own))
            def _():
                start(*self.over(u))

            @when(own & (u < units - 1))
            def _():
                start(*self.back(u))

            @when(u == units - 1)
            def _():
                start(*self.keep(u))

        def begin(self):
            for copy in self.fetch(0):
                copy.start()

        def run(self, first, last):
            def one(u, carry):
                self.unit(u)
                return carry

            lax.fori_loop(first, last, one, 0)

        def end(self):
            whole(*self.keep(units - 1)).wait()

        def finish(self):
            if group.square:
                for kind in range(6):
                    whole(*self.hop(kind)).wait_send()
                    if kind >= 2:
                        whole(*self.hop(kind)).wait_recv()
                return
            for j in range(chips):

                @when(j != group.chip)
                def _(j=j):
                    sems = (own_send.at[self.back_stage, j], own_got.at[self.back_stage, j])
                    copy = to(self.mate.at[j], self.sums.at[j], *sems, {"fsdp": group.at(j)})
                    copy.wait_send()
                    copy.wait_recv()

    def save_out(c):
        return pltpu.make_async_copy(flow.running.at[flow.slot(c)], out_states.at[block(c)], out_sem.at[c])

    def save_grad(c):
        return pltpu.make_async_copy(res.at[block(c)], grad_states.at[block(c)], out_sem.at[c])

    def step(t, carry):
        i = t % steps
        stage = t // steps
        back = stage - half
        c = jnp.where(back < 0, i, steps - 1 - i)
        run_events(t, 0)

        @when((t >= steps) & (back < 0))
        def _():
            normed_rows(stage, c)
            flow.release(i, True)

        @when(t < steps)
        def _():
            normed_rows(stage, c)

        @when(back == 0)
        def _():
            save_x(half - 1, i).wait()

        @when((i == 0) & (back >= 1) & (back < half))
        def _():
            for k in range(2):

                @when(back % 2 == k)
                def _(k=k):
                    layer = top - back // 2

                    @when(back >= 2)
                    def _():
                        for kind in (2, 3) if k == 0 else (0, 1):
                            load(layer, kind, True)
                        for copy in activations(layer, k):
                            copy.wait()

                    @when(back + 1 < half)
                    def _():
                        for kind in (0, 1) if k == 0 else (2, 3):
                            load(layer - k, kind, False)

                    if k == 1:
                        d_key[...] = jnp.zeros_like(d_key)
                        d_value[...] = jnp.zeros_like(d_value)

        for k in range(2):

            @when((i == 0) & (back >= 1) & (back % 2 != k))
            def _(k=k):
                Blocks(back - 1, k).begin()

        @when(back >= 1)
        def _():
            take(back, i, c)
            flow.release(i, t < total)

        @when((t >= total - half * steps + steps - 1) & (t < total + steps - 1))
        def _():
            after = t + 1
            fetch_x(after // steps - half, steps - 1 - after % steps).start()

        @when((back >= 1) & (back < half))
        def _():
            low[...] = res[block(c), :].astype(BF16)
            save_low(back, c).start()

        @when(back == half)
        def _():
            save_grad(c).start()

        @when((t >= steps) & (t < total))
        def _():
            flow.clear(i)

        @when(back == 0)
        def _():
            out = res[block(i), :] + flow.from_inner[flow.slot(i), :].astype(F32)
            flow.release(i, True)
            flow.running[flow.slot(i), :] = out.astype(BF16)
            save_out(i).start()
            fetch_low(c).wait()
            save_out(i).wait()

        @when((back < 0) & (stage % 2 == 0))
        def _():
            attention_forward(t, stage // 2, c)

        @when((back < 0) & (stage % 2 == 1))
        def _():
            ffn_forward(t, stage // 2, c)

        @when((back >= 0) & (back < half) & (back % 2 == 0))
        def _():
            ffn_backward(i, c)

        @when((back >= 0) & (back < half) & (back % 2 == 1))
        def _():
            attention_backward(top - back // 2, i, c)

        @when(t < total)
        def _():
            flow.push(i, t >= steps)

        run_events(t, 2)

        @when((t < total) & (back != 0))
        def _():
            save_low(0, c).wait()

        after = t + 1
        @when((after >= half * steps) & (after < (half + 2) * steps))
        def _():
            fetch_low(steps - 1 - after % steps).start()

        for k in range(2):

            @when((back >= 1) & (back % 2 != k))
            def _(k=k):
                blocks = Blocks(back - 1, k)
                extra = back == half
                pace = 2 * per_step
                first = jnp.where(extra, jnp.minimum(i * pace, units), i * units // steps)
                last = jnp.where(extra, jnp.minimum((i + 1) * pace, units), (i + 1) * units // steps)
                blocks.run(first, last)

                @when(i == jnp.where(extra, min(3, steps - 1), steps - 1))
                def _():
                    blocks.end()
                    blocks.relay()

                @when(i == steps - 1)
                def _():

                    @when((back + 1 < half) & (back + 1 >= 2))
                    def _():
                        for copy in activations(top - (back + 1) // 2, k):
                            copy.start()

        k = t - flow.lag

        @when((k >= 0) & (k < total))
        def _():
            flow.pull((k + steps) % steps)

        return carry

    lax.fori_loop(0, total + steps, step, 0)

    for copy in small:
        copy.wait_send()
    parts = []
    for n, other in enumerate(group.everyone):
        at = pl.multiple_of(other * depth, depth)
        sems = (small_send.at[0, n], small_got.at[0, n])
        parts.append(to(norm_acc.at[:, pl.ds(at, depth)], norm_parts.at[shards - 1 - n], *sems, {"fsdp": other}))
        sems = (small_send.at[1, n], small_got.at[1, n])
        parts.append(to(bias_acc, bias_parts.at[shards - 1 - n], *sems, {"fsdp": other}))
    for copy in parts:
        copy.start()
    own = [
        pltpu.make_async_copy(norm_acc.at[:, mine], norm_parts.at[0], misc.at[0]),
        pltpu.make_async_copy(bias_acc, bias_parts.at[0], misc.at[1]),
    ]
    for copy in own:
        copy.start()
    for copy in own:
        copy.wait()
    for i in range(steps):
        save_grad(i).wait()
        flow.clear(i)
    for layer in range(LAYERS):
        for kind in range(4):
            gather(layer, kind).finish()
    for copy in parts:
        copy.wait_send()
        copy.wait_recv()
    for back in range(half):
        Blocks(back, back % 2).finish()


def lane_stride(extent):
    return -(-extent // PAIR) * PAIR


def plan(tokens):
    return next((s, p) for s, p in ((6, 1), (3, 1), (2, 1)) if tokens % (16 * s * p) == 0)


def train(states, cotangent, own_norms, own_bias, rope, mask, own_q, own_o, own_g, own_d):
    count, shards = lax.axis_size("tensor"), lax.axis_size("fsdp")
    tokens, width = states.shape
    steps, span = plan(tokens)
    big = tokens // steps
    chips = shards // 2
    depth = width // shards
    local, ff = own_q.shape[-1], own_g.shape[-1]
    lanes_attn, lanes_ffn = 4 * lane_stride(local), 3 * lane_stride(ff)
    parts = 3 if chips == 4 else chips
    per_step = -(-2 * chips // max(steps - 2, 1))
    shape = jax.ShapeDtypeStruct
    outs = [
        shape((tokens, width), BF16),
        shape((tokens, width), F32),
        shape((LAYERS, parts, depth, lanes_attn), BF16),
        shape((LAYERS, parts, depth, lanes_ffn), BF16),
        shape((shards, 4 * LAYERS, depth), F32),
        shape((shards, LAYERS, 8, local), F32),
        *[shape((LAYERS, shards) + own.shape[1:], BF16) for own in (own_q, own_o, own_g, own_d)],
        shape((2 * LAYERS, tokens, width), F32),
        shape((2 * LAYERS, tokens, width), BF16),
        shape((2 * LAYERS, tokens, width), BF16),
        shape((LAYERS - 1, 3, tokens, local), BF16),
        shape((LAYERS - 1, tokens, local), BF16),
        shape((LAYERS - 1, 2, tokens, ff), BF16),
        shape((LAYERS - 1, tokens, ff), BF16),
        shape((LAYERS, chips, depth, lanes_attn), BF16),
        shape((LAYERS, chips, depth, lanes_ffn), BF16),
        shape((LAYERS, 2, depth // 2, lanes_attn), BF16),
        shape((LAYERS, 2, depth // 2, lanes_ffn), BF16),
    ]
    dma = pltpu.SemaphoreType.DMA
    vmem = pltpu.VMEM
    scratch = [
        vmem((tokens, width), F32),
        vmem((4, width, local), BF16),
        vmem((3, width, ff), BF16),
        vmem((2, tokens, ff), BF16),
        vmem((tokens, ff), BF16),
        vmem((3, tokens, local), BF16),
        vmem((tokens, local), BF16),
        vmem((tokens, local), F32),
        vmem((tokens, local), F32),
        vmem((big, width), F32),
        vmem((big, width), BF16),
        vmem((LAYERS, steps, local // HEAD_DIM, big), F32),
        vmem((4 * LAYERS, width), F32),
        vmem((8, local), F32),
        vmem((shards, 8, PAIR), F32),
        vmem((4 * LAYERS, width), F32),
        vmem((LAYERS, 8, local), F32),
        vmem((2, 2, tokens, depth), BF16),
        vmem((2, depth, tokens), BF16),
        vmem((2, depth, max(lanes_attn, lanes_ffn)), BF16),
        dma((steps,)),
        dma((1,)),
        dma((2,)),
        dma((steps,)),
        dma((2, 2, steps)),
        dma((2, 2)),
        dma((4,)),
        dma((4, shards)),
        dma((4 * LAYERS, gather_kinds(shards))),
        dma((4 * LAYERS, gather_kinds(shards))),
        dma((2, 2, 2)),
        dma((2, 2)),
        dma((2, 2)),
        *([dma((2 * LAYERS, max(chips, 6)))] * 4),
        dma((2, shards)),
        dma((2, shards)),
        *flow_scratch(steps, span, tokens, width),
    ]
    flops = 6 * LAYERS * tokens * width * (4 * local + 3 * ff)
    return pl.pallas_call(
        functools.partial(train_kernel, count, shards, steps, span, per_step),
        out_shape=outs,
        in_specs=[ANY, ANY, VMEM, VMEM, VMEM, VMEM, ANY, ANY, ANY, ANY],
        out_specs=[ANY] * len(outs),
        scratch_shapes=scratch,
        compiler_params=pltpu.CompilerParams(
            collective_id=1, has_side_effects=True, vmem_limit_bytes=64 * 1024 * 1024
        ),
        cost_estimate=pl.CostEstimate(flops=flops, bytes_accessed=flops // 256, transcendentals=0),
        name="train",
    )(states, cotangent, own_norms, own_bias, rope, mask, own_q, own_o, own_g, own_d)


def finish_kernel(attn, ffn, states, grads, g_qkv, g_out, g_gate_up, g_down, out_states, out_grads):
    local, ff = g_qkv.shape[3], g_gate_up.shape[3]

    def total(parts, at, wide):
        return sum(parts[0, n, :, at : at + wide].astype(F32) for n in range(parts.shape[1]))

    for m in range(3):
        g_qkv[0, m] = total(attn, m * lane_stride(local), local)
    g_out[0] = total(attn, 3 * lane_stride(local), local).T
    for m in range(2):
        g_gate_up[0, :, m, :] = total(ffn, m * lane_stride(ff), ff)
    g_down[0] = total(ffn, 2 * lane_stride(ff), ff).T
    out_states[...] = states[...]
    out_grads[...] = grads[...]


def finish(sums_attn, sums_ffn, states, grads, local, ff):
    parts, depth = sums_attn.shape[1:3]
    tokens, width = states.shape
    rows = min(PAIR, depth)
    cuts = depth // rows
    pieces = tokens // (LAYERS * cuts)
    shape = jax.ShapeDtypeStruct
    spec = pl.BlockSpec
    token_spec = spec((pieces, width), lambda l, r: (l * cuts + r, 0))
    return pl.pallas_call(
        finish_kernel,
        grid=(LAYERS, cuts),
        in_specs=[
            spec((1, parts, rows, sums_attn.shape[3]), lambda l, r: (l, 0, r, 0)),
            spec((1, parts, rows, sums_ffn.shape[3]), lambda l, r: (l, 0, r, 0)),
            token_spec,
            token_spec,
        ],
        out_specs=[
            spec((1, 3, rows, local), lambda l, r: (l, 0, r, 0)),
            spec((1, local, rows), lambda l, r: (l, 0, r)),
            spec((1, rows, 2, ff), lambda l, r: (l, r, 0, 0)),
            spec((1, ff, rows), lambda l, r: (l, 0, r)),
            token_spec,
            token_spec,
        ],
        out_shape=[
            shape((LAYERS, 3, depth, local), F32),
            shape((LAYERS, local, depth), F32),
            shape((LAYERS, depth, 2, ff), F32),
            shape((LAYERS, ff, depth), F32),
            shape((tokens, width), BF16),
            shape((tokens, width), F32),
        ],
        compiler_params=pltpu.CompilerParams(vmem_limit_bytes=48 * 1024 * 1024),
        name="finish",
    )(sums_attn, sums_ffn, states, grads)


def tables(segment_ids, rows):
    places = jnp.arange(rows, dtype=jnp.int32)
    same = segment_ids[:, None] == segment_ids[None, :]
    earlier = places[None, :] < places[:, None]
    position = jnp.sum(jnp.where(same & earlier, 1.0, 0.0), axis=1)
    half = ROT_DIM // 2
    lane = jnp.arange(PAIR, dtype=jnp.int32) % HEAD_DIM
    inverse = rotary_base ** (-((lane % half).astype(F32) * 2.0 / ROT_DIM))
    angle = position[:, None] * jnp.where(lane < ROT_DIM, inverse, 0.0)[None, :]
    sine = jnp.sin(angle)
    rope = jnp.stack(
        [jnp.cos(angle), jnp.where(lane < half, -sine, 0.0), jnp.where((lane >= half) & (lane < ROT_DIM), sine, 0.0)]
    )
    return rope, jnp.where(same & (places[None, :] <= places[:, None]), 0.0, -1e30)


def on_device(
    states,
    segment_ids,
    ln1_gain,
    ln1_bias,
    qkv_weight,
    qkv_bias,
    out_weight,
    ln2_gain,
    ln2_bias,
    gate_up_weight,
    down_weight,
    cotangent,
):
    tokens = states.shape[0]
    rope, allowed = tables(segment_ids, tokens)
    steps = plan(tokens)[0]
    mask = allowed.reshape(steps, -1, tokens).transpose(0, 2, 1).astype(BF16)
    own_norms = jnp.stack([ln1_gain, ln1_bias, ln2_gain, ln2_bias], axis=1).reshape(4 * LAYERS, -1).astype(F32)
    own_bias = qkv_bias.reshape(LAYERS * 3, -1).astype(F32)
    own_bias = jnp.pad(own_bias, ((0, 8 - own_bias.shape[0]), (0, PAIR - own_bias.shape[1])))
    out_states, grad_states, sums_attn, sums_ffn, norm_parts, bias_parts, *_ = train(
        states,
        cotangent,
        own_norms,
        own_bias,
        rope,
        mask,
        qkv_weight.transpose(0, 2, 1, 3),
        out_weight.transpose(0, 2, 1)[:, None],
        gate_up_weight.transpose(0, 2, 1, 3),
        down_weight.transpose(0, 2, 1)[:, None],
    )
    g_qkv, g_out, g_gate_up, g_down, out_states, grad_states = finish(
        sums_attn, sums_ffn, out_states, grad_states, qkv_weight.shape[3], gate_up_weight.shape[3]
    )
    g_norms = jnp.sum(norm_parts, axis=0).reshape(LAYERS, 4, -1)
    g_bias = jnp.sum(bias_parts, axis=0).reshape(LAYERS, 8, -1, HEAD_DIM)[:, :3]
    share = qkv_bias.shape[3]
    g_bias = lax.dynamic_slice_in_dim(g_bias, lax.axis_index("fsdp") * share, share, axis=3)
    return (
        out_states,
        grad_states,
        g_norms[:, 0],
        g_norms[:, 1],
        g_qkv.transpose(0, 2, 1, 3),
        g_bias,
        g_out,
        g_norms[:, 2],
        g_norms[:, 3],
        g_gate_up,
        g_down,
    )


def solution(mesh):
    in_specs = (
        P("fsdp", None),
        P("fsdp"),
        P(None, "fsdp"),
        P(None, "fsdp"),
        P(None, "fsdp", None, "tensor"),
        P(None, None, "tensor", "fsdp"),
        P(None, "tensor", "fsdp"),
        P(None, "fsdp"),
        P(None, "fsdp"),
        P(None, "fsdp", None, "tensor"),
        P(None, "tensor", "fsdp"),
        P("fsdp", None),
    )
    out_specs = (
        P("fsdp", None),
        P("fsdp", None),
        P(None, "fsdp"),
        P(None, "fsdp"),
        P(None, "fsdp", None, "tensor"),
        P(None, None, "tensor", "fsdp"),
        P(None, "tensor", "fsdp"),
        P(None, "fsdp"),
        P(None, "fsdp"),
        P(None, "fsdp", None, "tensor"),
        P(None, "tensor", "fsdp"),
    )
    return jax.shard_map(
        on_device, mesh=mesh, in_specs=in_specs, out_specs=out_specs, check_vma=False
    )
```
